128 devices in a mesh: hash: 8 (over y, core), dp: 16 (over x, z).
Axes of the slice: x: 4, y: 4, z: 4, core: 2. Of those that a mesh axis runs over, the one named last changes fastest.
Arguments:
- histories: bfloat16 [512, 256, 512], P(('hash', 'dp')), may hold values from -6 to 6
- weight_in: bfloat16 [512, 2048], replicated, may hold values from -0.25 to 0.25
- weight_out: bfloat16 [512, 512], replicated, may hold values from -0.25 to 0.25
- candidates: bfloat16 [32768, 512], P(('hash', 'dp')), may hold values from -6 to 6
- cotangent: bfloat16 [32768, 512], P(('hash', 'dp')), may hold values from -6 to 6
- owner_ids: int32 [32768, 1], P(('hash', 'dp')), may hold values from 0 to 127; in each aligned block of 256 rows (0 to 255, 256 to 511, ...) at most 4 rows name the same one
- hist_slot: int32 [32768], P(('hash', 'dp')), may hold values from 0 to 3
- lengths: int32 [32768], P(('hash', 'dp')), may hold values from 1 to 256
Outputs:
- history_grad: bfloat16 [512, 256, 512], P(('hash', 'dp'))
- candidate_grad: bfloat16 [32768, 512], P(('hash', 'dp'))
- weight_in_grad: float32 [512, 2048], P(('hash', 'dp'))
- weight_out_grad: float32 [512, 512], P(('hash', 'dp'))
The draws below stay inside these ranges and needn't reach their ends.
Inputs may be any that keep to these rules, and one draw needn't show every extreme that they name: `owner_ids`: in the rows of one device, at most 4 impressions name the same owner; the bound is reached.
All inputs are finite; a program needn't handle non-finite values.
Results may differ from the reference program's by a relative error of at most 0.012.
Values may be sent and summed in bfloat16 or wider, within the bound.
A program may use at most 128 MiB of HBM per device.

```python
import math
import jax
import jax.numpy as jnp
import numpy as np
from jax import lax

D = 512
HEADS = 8
HEAD_DIM = 64
L = 256
HIST_DEV = 4
IMP_DEV = 256
CAP = 4
HIST = 512
IMP = 32768
DEVICES = 128


def touch_ends(result, own_key, least, top_value):
    place = [jax.random.randint(jax.random.fold_in(own_key, axis), (), 0, length) for axis, length in enumerate(result.shape)]
    longest = result.shape.index(max(result.shape))
    beside = place[:longest] + [(place[longest] + 1) % result.shape[longest]] + place[longest + 1:]
    return result.at[tuple(place)].set(least).at[tuple(beside)].set(top_value)


def level_of(own_key, extent, cuts, low, largest):
    factor_of = 1.0
    for axis_at, parts in cuts:
        heights = jax.random.uniform(jax.random.fold_in(jax.random.fold_in(own_key, 6), axis_at), (parts,), jnp.float32, low / len(cuts), largest / len(cuts))
        factor_of = factor_of * jnp.repeat(jnp.exp(heights), extent[axis_at] // parts).reshape((-1,) + (1,) * (len(extent) - 1 - axis_at))
    return factor_of


def shared_out(stream_key, own, number, rows, amount, top, most, slope):
    sequence = jax.random.permutation(stream_key, amount)
    heavy_load, usual = load_shares(amount, rows * top, most, slope, True), load_shares(amount, rows * top, most, slope, False)
    places = jnp.arange(amount)

    def named(sizes, turn):
        used = int((sizes > 0).sum())
        fixed = max(1, used // 4)
        passed = fixed + (places - fixed + turn * (used - fixed)) % max(1, amount - fixed)
        return jnp.zeros((amount,), jnp.int32).at[sequence[jnp.where(places < fixed, places, passed)]].set(jnp.asarray(sizes, jnp.int32))

    sizes = jnp.where(number % 4 == 0, named(heavy_load, number // 4), named(usual, number - number // 4 - 1))
    mixed = jax.random.permutation(jax.random.fold_in(own, 3), amount)
    donor, sink = mixed[0:amount // 2 * 2:2], mixed[1:amount // 2 * 2:2]
    margin = jnp.minimum(sizes[donor] - 1, most - sizes[sink]) // 2
    margin = jnp.where((donor == sequence[0]) | (sink == sequence[0]) | (sizes[sink] == 0), 0, jnp.maximum(margin, 0))
    passed = jax.random.randint(jax.random.fold_in(own, 4), (amount // 2,), 0, 1 << 20) % (margin + 1)
    sizes = sizes.at[donor].add(-passed).at[sink].add(passed)
    items = jnp.searchsorted(jnp.cumsum(sizes), jnp.arange(rows * top), side="right").astype(jnp.int32)
    grid = items.reshape(top, rows).T
    grid = grid[jax.random.permutation(jax.random.fold_in(own, 1), rows)]
    turn = jax.random.randint(jax.random.fold_in(own, 2), (rows, 1), 0, top)
    return jnp.take_along_axis(grid, (jnp.arange(top)[None, :] + turn) % top, axis=1)


def load_shares(count, total, reach, skew, full):
    portions = [(1 << 20) // math.isqrt(grade ** skew) + 1 for grade in range(1, count + 1)]
    largest = reach if full else min(reach, max(-(-total // count), total * portions[0] // sum(portions)))
    least = 1 if total - largest >= count - 1 else 0
    given, rest = [largest] + [least] * (count - 1), total - largest - least * (count - 1)
    while rest > 0:
        free = [i for i in range(1, count) if given[i] < largest] or [i for i in range(1, count) if given[i] < reach]
        mass, budget = sum([portions[i] for i in free]), rest
        for i in free:
            addition = min(reach - given[i], max(1, budget * portions[i] // mass), rest)
            given[i] = given[i] + addition
            rest = rest - addition
    return np.array(given)


def normal_values(key, extent, width, reach, shards=(), held_as=jnp.bfloat16):
    values = jax.random.normal(key, extent, jnp.float32) * width
    if len(shards) > 0:
        values = level_of(key, extent, shards, -0.22, 0.18) * values
    return jnp.clip(values, min=-reach, max=reach).astype(held_as)


def setup_inputs(seed: int = 0) -> dict:
    key_list = jax.random.split(jax.random.key(seed), 9)
    histories = normal_values(key_list[0], (HIST, L, D), 1.0, 6.0, ((0, 128),))
    weight_in = normal_values(key_list[1], (D, 4 * D), D ** -0.5, 0.25)
    weight_out = normal_values(key_list[2], (D, D), D ** -0.5, 0.25)
    candidates = normal_values(key_list[3], (IMP, D), 1.0, 6.0, ((0, 128),))
    cotangent = normal_values(key_list[4], (IMP, D), 1.0, 6.0, ((0, 128),))
    owner_ids_keys = jax.random.split(jax.random.fold_in(key_list[5], 1), IMP // IMP_DEV)
    owner_ids_turns = jax.random.permutation(jax.random.fold_in(key_list[5], 3), IMP // IMP_DEV)
    owner_ids = jax.vmap(lambda own, number: shared_out(jax.random.fold_in(key_list[5], 2), own, number, IMP_DEV, DEVICES, 1, CAP, 2))(owner_ids_keys, owner_ids_turns).reshape((IMP, 1))
    hist_slot = touch_ends(jax.random.randint(key_list[6], (IMP,), 0, HIST_DEV), jax.random.fold_in(key_list[6], 1), 0, HIST_DEV - 1).astype(jnp.int32)
    lengths = touch_ends(jax.random.randint(key_list[7], (IMP,), 1, L + 1), jax.random.fold_in(key_list[7], 1), 1, L).astype(jnp.int32)
    return {"histories": histories, "weight_in": weight_in, "weight_out": weight_out, "candidates": candidates, "cotangent": cotangent, "owner_ids": owner_ids, "hist_slot": hist_slot, "lengths": lengths}


norm_eps = 1e-05

def silu_grad(argument):
    sigmoid_v = jax.nn.sigmoid(argument)
    return sigmoid_v * (1.0 + argument * (1.0 - sigmoid_v))

def contract_rows(left_mat, right_mat):
    return lax.dot_general(left_mat, right_mat, (((0,), (0,)), ((), ())), preferred_element_type=jnp.float32)

def contract_cols(left_mat, right_mat):
    return lax.dot_general(left_mat, right_mat, (((1,), (1,)), ((), ())), preferred_element_type=jnp.float32)

def rounded(argument):
    return lax.optimization_barrier(argument.astype(jnp.bfloat16)).astype(jnp.float32)

def causal_table(seq_len):
    positions = jnp.arange(seq_len, dtype=jnp.int32)
    return (positions[:, None] >= positions[None, :]).astype(jnp.float32) / seq_len

def layer_forward(inputs, weight_in, weight_out):
    num_hist, seq_len, model_width = inputs.shape
    head_dim = model_width // HEADS
    flat_rows = inputs.reshape(num_hist * seq_len, model_width)
    pre_act = jnp.dot(flat_rows, weight_in, preferred_element_type=jnp.float32)
    activated = jax.nn.silu(pre_act)
    gate_u = activated[:, :model_width]
    proj_f = rounded(activated[:, model_width:])
    head_shape = (num_hist, seq_len, HEADS, head_dim)
    values = proj_f[:, :model_width].reshape(head_shape)
    queries = proj_f[:, model_width:2 * model_width].reshape(head_shape)
    keys_f = proj_f[:, 2 * model_width:].reshape(head_shape)
    score_scale = head_dim ** (-0.5)
    scores = jnp.einsum('bqhe,bkhe->bhqk', queries, keys_f) * score_scale
    attn_f = rounded(jax.nn.silu(scores) * causal_table(seq_len))
    mixed_rows = jnp.einsum('bhqk,bkhe->bqhe', attn_f, values).reshape(num_hist * seq_len, model_width)
    centred = mixed_rows - lax.optimization_barrier(jnp.mean(mixed_rows, axis=1, keepdims=True))
    inv_std = lax.rsqrt(lax.optimization_barrier(jnp.mean(centred * centred, axis=1, keepdims=True)) + norm_eps)
    normed = centred * inv_std
    merged = (normed * gate_u).astype(jnp.bfloat16)
    output = flat_rows.astype(jnp.float32) + jnp.dot(merged, weight_out, preferred_element_type=jnp.float32)
    saved_state = (pre_act, gate_u, values, queries, keys_f, scores, attn_f, normed, inv_std, merged)
    return (output.astype(jnp.bfloat16).reshape(inputs.shape), saved_state)

def layer_backward(inputs, weight_in, weight_out, saved_state, d_out):
    num_hist, seq_len, model_width = inputs.shape
    head_dim = model_width // HEADS
    flat_count = num_hist * seq_len
    pre_act, gate_u, values, queries, keys_f, scores, attn_f, normed, inv_std, merged = saved_state
    flat_rows = inputs.reshape(flat_count, model_width)
    d_rows = d_out.reshape(flat_count, model_width)
    w_out_part = contract_rows(merged, d_rows)
    d_merged = contract_cols(d_rows, weight_out)
    d_gate = d_merged * normed
    d_norm = d_merged * gate_u
    d_mixed = inv_std * (d_norm - lax.optimization_barrier(jnp.mean(d_norm, axis=1, keepdims=True)) - normed * lax.optimization_barrier(jnp.mean(d_norm * normed, axis=1, keepdims=True)))
    d_mixed_f = rounded(d_mixed).reshape(num_hist, seq_len, HEADS, head_dim)
    d_attn = jnp.einsum('bqhe,bkhe->bhqk', d_mixed_f, values)
    d_values = jnp.einsum('bhqk,bqhe->bkhe', attn_f, d_mixed_f)
    score_scale = head_dim ** (-0.5)
    d_scores = rounded(d_attn * silu_grad(scores) * causal_table(seq_len) * score_scale)
    d_queries = jnp.einsum('bhqk,bkhe->bqhe', d_scores, keys_f)
    d_keys = jnp.einsum('bhqk,bqhe->bkhe', d_scores, queries)
    d_act = jnp.concatenate([d_gate, d_values.reshape(flat_count, model_width), d_queries.reshape(flat_count, model_width), d_keys.reshape(flat_count, model_width)], axis=1)
    d_pre = (d_act * silu_grad(pre_act)).astype(jnp.bfloat16)
    w_in_part = contract_rows(flat_rows, d_pre)
    d_inputs = (d_rows.astype(jnp.float32) + contract_cols(d_pre, weight_in)).astype(jnp.bfloat16)
    return (d_inputs.reshape(inputs.shape), w_in_part, w_out_part)

def reference(histories, weight_in, weight_out, candidates, cotangent, owner_ids, hist_slot, lengths):
    groups = HIST // HIST_DEV
    grouped = histories.reshape(groups, HIST_DEV, L, D)
    encoded = lax.map(lambda block_in: layer_forward(block_in, weight_in, weight_out)[0], grouped)
    encoded = encoded.reshape(HIST, L, D)
    hist_index = (owner_ids[:, 0] * HIST_DEV + hist_slot).astype(jnp.int32)
    block_rows = min(128, IMP)
    block_count = IMP // block_rows
    positions = jnp.arange(L, dtype=jnp.int32)
    score_scale = HEAD_DIM ** (-0.5)

    def target_block(running, block_in):
        index_b, cand_b, cot_b, len_b = block_in
        keys_b = encoded[index_b].astype(jnp.float32).reshape(block_rows, L, HEADS, HEAD_DIM)
        query_b = cand_b.astype(jnp.float32).reshape(block_rows, HEADS, HEAD_DIM)
        grad_b = cot_b.astype(jnp.float32).reshape(block_rows, HEADS, HEAD_DIM)
        inverse = 1.0 / len_b.astype(jnp.float32)
        weight_b = (positions[None, :] < len_b[:, None]).astype(jnp.float32) * inverse[:, None]
        weight_b = weight_b[:, None, :]
        scores_b = jnp.einsum('bhe,blhe->bhl', query_b, keys_b) * score_scale
        attn_b = rounded(jax.nn.silu(scores_b) * weight_b)
        d_attn_b = jnp.einsum('bhe,blhe->bhl', grad_b, keys_b)
        d_scores_b = rounded(d_attn_b * silu_grad(scores_b) * weight_b * score_scale)
        d_query_b = jnp.einsum('bhl,blhe->bhe', d_scores_b, keys_b).reshape(block_rows, D).astype(jnp.bfloat16)
        d_keys_b = jnp.einsum('bhl,bhe->blhe', attn_b, grad_b) + jnp.einsum('bhl,bhe->blhe', d_scores_b, query_b)
        running = running.at[index_b].add(d_keys_b.reshape(block_rows, L, D))
        return (running, d_query_b)
    blocks = (hist_index.reshape(block_count, block_rows), candidates.reshape(block_count, block_rows, D), cotangent.reshape(block_count, block_rows, D), lengths.reshape(block_count, block_rows))
    d_encoded, cand_grads = lax.scan(target_block, jnp.zeros((HIST, L, D), jnp.float32), blocks)
    d_encoded = d_encoded.astype(jnp.bfloat16).reshape(groups, HIST_DEV, L, D)

    def layer_block(running, block_in):
        inputs_b, d_out_b = block_in
        _, saved_state = layer_forward(inputs_b, weight_in, weight_out)
        d_inputs, w_in_part, w_out_part = layer_backward(inputs_b, weight_in, weight_out, saved_state, d_out_b)
        return ((running[0] + w_in_part, running[1] + w_out_part), d_inputs)
    start = (jnp.zeros((D, 4 * D), jnp.float32), jnp.zeros((D, D), jnp.float32))
    (w_in_total, w_out_total), history_grad = lax.scan(layer_block, start, (grouped, d_encoded))
    return (history_grad.reshape(HIST, L, D), cand_grads.reshape(IMP, D), w_in_total, w_out_total)
```

```python
import functools

import jax
import jax.numpy as jnp
from jax import lax
from jax.experimental import pallas as pl
from jax.experimental.pallas import tpu as pltpu
from jax.sharding import PartitionSpec as P

HEADS = 8
HEAD_DIM = 64
PAIR = 128
EPS = 1e-05
BF = jnp.bfloat16
F32 = jnp.float32
AXES = ("hash", "dp")
VMEM_LIMIT = 48 * 1024 * 1024


def dot_nn(a, b):
    return lax.dot_general(a, b, (((1,), (0,)), ((), ())), preferred_element_type=F32)


def dot_nt(a, b):
    return lax.dot_general(a, b, (((1,), (1,)), ((), ())), preferred_element_type=F32)


def dot_tn(a, b):
    return lax.dot_general(a, b, (((0,), (0,)), ((), ())), preferred_element_type=F32)


def iota(shape, dim):
    return lax.broadcasted_iota(jnp.int32, shape, dim)


def silu_parts(half):
    t = jnp.tanh(half)
    plus = 1.0 + t
    return half * plus, plus * (1.0 + half * (1.0 - t))


def head_rows(scale):
    lanes = iota((1, PAIR), 1)
    first = jnp.where(lanes < HEAD_DIM, scale, 0.0).astype(BF)
    second = jnp.where(lanes < HEAD_DIM, 0.0, scale).astype(BF)
    return first, second


def slot_of(owner_col):
    rows = owner_col.shape[0]
    i, j = iota((rows, rows), 0), iota((rows, rows), 1)
    owner_row = jnp.sum(jnp.where(i == j, owner_col, 0), axis=0, keepdims=True)
    same = owner_col == owner_row
    place_col = jnp.sum(jnp.where(same & (j < i), 1, 0), axis=1, keepdims=True)
    place_row = jnp.sum(jnp.where(same & (i < j), 1, 0), axis=0, keepdims=True)
    return owner_col, place_col, owner_row, place_row


def pack_kernel(capacity, owner_ref, slot_ref, len_ref, cand_ref, cot_ref, out_ref):
    rows, width = cand_ref.shape
    slots = out_ref.shape[0]
    _, _, owner_row, place_row = slot_of(owner_ref[...])
    target_row = owner_row * capacity + place_row
    chosen = jnp.where(iota((slots, rows), 0) == target_row, 1.0, 0.0).astype(BF)
    out_ref[:, :width] = dot_nn(chosen, cand_ref[...]).astype(BF)
    out_ref[:, width : 2 * width] = dot_nn(chosen, cot_ref[...]).astype(BF)
    i, j = iota((rows, rows), 0), iota((rows, rows), 1)
    slot_col = jnp.sum(jnp.where(i == j, slot_ref[...], 0), axis=1, keepdims=True)
    len_col = jnp.sum(jnp.where(i == j, len_ref[...], 0), axis=1, keepdims=True)
    lane = iota((rows, PAIR), 1)
    meta = jnp.where(lane == 0, slot_col, jnp.where(lane == 1, len_col, 0))
    out_ref[:, 2 * width :] = dot_nn(chosen, meta.astype(F32).astype(BF)).astype(BF)


def unpack_kernel(capacity, owner_ref, ret_ref, out_ref):
    rows = out_ref.shape[0]
    slots = ret_ref.shape[0]
    owner_col, place_col, _, _ = slot_of(owner_ref[...])
    target_col = owner_col * capacity + place_col
    chosen = jnp.where(iota((rows, slots), 1) == target_col, 1.0, 0.0).astype(BF)
    out_ref[...] = dot_nn(chosen, ret_ref[...]).astype(BF)


def forward_kernel(x_ref, win_ref, wout_ref, enc_ref, sg_ref, gate_ref, vqk_ref, nrm_ref, inv_ref, mix_s):
    seq, width = x_ref.shape[1:]
    x = x_ref[0]
    xh = x * 0.5
    for part in range(4):
        cols = slice(part * width, (part + 1) * width)
        act, grad2 = silu_parts(dot_nn(xh, win_ref[:, cols]))
        sg_ref[0, :, cols] = (0.5 * grad2).astype(BF)
        if part == 0:
            gate_ref[0] = act.astype(BF)
        else:
            vqk_ref[0, :, (part - 1) * width : part * width] = act.astype(BF)
    causal = iota((seq, seq), 0) >= iota((seq, seq), 1)
    half_scale = head_rows(0.5 * HEAD_DIM**-0.5)
    inv_seq = head_rows(1.0 / seq)
    for pair in range(width // PAIR):
        cols = slice(pair * PAIR, (pair + 1) * PAIR)
        v = vqk_ref[0, :, cols]
        q = vqk_ref[0, :, width + pair * PAIR : width + (pair + 1) * PAIR]
        k = vqk_ref[0, :, 2 * width + pair * PAIR : 2 * width + (pair + 1) * PAIR]
        total = None
        for h in range(2):
            half = dot_nt(q * half_scale[h], k)
            attn = jnp.where(causal, half * (1.0 + jnp.tanh(half)), 0.0).astype(BF)
            term = dot_nn(attn, v * inv_seq[h])
            total = term if total is None else total + term
        mix_s[:, cols] = total
    mixed = mix_s[...]
    centred = mixed - jnp.mean(mixed, axis=1, keepdims=True)
    inv = lax.rsqrt(jnp.mean(centred * centred, axis=1, keepdims=True) + EPS)
    normed = centred * inv
    nrm_ref[0] = normed.astype(BF)
    inv_ref[0] = jnp.broadcast_to(inv, (seq, PAIR))
    merged = (normed * gate_ref[0].astype(F32)).astype(BF)
    enc_ref[0] = (x.astype(F32) + dot_nn(merged, wout_ref[...])).astype(BF)


def backward_kernel(
    x_ref, win_ref, wout_ref, sg_ref, gate_ref, vqk_ref, nrm_ref, inv_ref, denc_ref,
    hg_ref, wg_ref, x_s, de_s, mg_s, dp_s, dm_s,
):
    step = pl.program_id(0)
    seq, width = x_ref.shape[1:]
    rows = pl.ds(pl.multiple_of(step * seq, seq), seq)
    d_rows = denc_ref[0]
    normed = nrm_ref[0].astype(F32)
    gate = gate_ref[0].astype(F32)
    inv = inv_ref[0][:, :1]
    x_s[rows, :] = x_ref[0]
    de_s[rows, :] = d_rows
    mg_s[rows, :] = (normed * gate).astype(BF)
    d_merged = dot_nt(d_rows, wout_ref[...])
    d_pre0 = (d_merged * normed * sg_ref[0, :, :width].astype(F32)).astype(BF)
    dp_s[rows, :width] = d_pre0
    d_norm = d_merged * gate
    m1 = jnp.mean(d_norm, axis=1, keepdims=True)
    m2 = jnp.mean(d_norm * normed, axis=1, keepdims=True)
    dm_s[...] = (inv * (d_norm - m1 - normed * m2)).astype(BF)
    causal = iota((seq, seq), 0) >= iota((seq, seq), 1)
    half_scale = head_rows(0.5 * HEAD_DIM**-0.5)
    one = head_rows(1.0)
    inv_seq = head_rows(1.0 / seq)
    ds_scale = head_rows(0.5 * HEAD_DIM**-0.5 / seq)
    for pair in range(width // PAIR):
        lanes = [slice(b * width + pair * PAIR, b * width + (pair + 1) * PAIR) for b in range(4)]
        v = vqk_ref[0, :, lanes[0]]
        q = vqk_ref[0, :, lanes[1]]
        k = vqk_ref[0, :, lanes[2]]
        dm = dm_s[:, lanes[0]]
        dv = dq = dk = None
        for h in range(2):
            half = dot_nt(q * half_scale[h], k)
            act, grad2 = silu_parts(half)
            attn = jnp.where(causal, act, 0.0).astype(BF)
            d_attn = dot_nt(dm * one[h], v)
            ds = jnp.where(causal, d_attn * grad2, 0.0).astype(BF)
            tv = dot_tn(attn, dm * inv_seq[h])
            tq = dot_nn(ds, k * ds_scale[h])
            tk = dot_tn(ds, q * ds_scale[h])
            dv = tv if dv is None else dv + tv
            dq = tq if dq is None else dq + tq
            dk = tk if dk is None else dk + tk
        for b, value in ((1, dv), (2, dq), (3, dk)):
            dp_s[rows, lanes[b]] = (value * sg_ref[0, :, lanes[b]].astype(F32)).astype(BF)
    hg_ref[0] = (d_rows.astype(F32) + dot_nt(dp_s[rows, :], win_ref[...])).astype(BF)

    @pl.when(step == pl.num_programs(0) - 1)
    def _():
        xt = x_s[...]
        for part in range(4):
            cols = slice(part * width, (part + 1) * width)
            wg_ref[:, cols] = dot_tn(xt, dp_s[:, cols]).astype(BF)
        wg_ref[:, 4 * width :] = dot_tn(mg_s[...], de_s[...]).astype(BF)


def target_kernel(rows_ref, enc_ref, dq_ref, denc_ref, dq_s):
    hists, seq, width = enc_ref.shape
    slots = rows_ref.shape[0]
    meta = rows_ref[:, 2 * width :].astype(F32)
    hist_row = jnp.transpose(meta)[0:1, :]
    len_row = jnp.transpose(meta)[1:2, :]
    inverse = 1.0 / jnp.maximum(len_row, 1.0)
    positions = iota((seq, slots), 0).astype(F32)
    half_scale = head_rows(0.5 * HEAD_DIM**-0.5)
    one = head_rows(1.0)
    for own in range(hists):
        weight = jnp.where((positions < len_row) & (hist_row == float(own)), inverse, 0.0)
        for pair in range(width // PAIR):
            cols = slice(pair * PAIR, (pair + 1) * PAIR)
            enc = enc_ref[own, :, cols]
            q = rows_ref[:, cols]
            g = rows_ref[:, width + pair * PAIR : width + (pair + 1) * PAIR]
            d_enc = d_q = None
            for h in range(2):
                half = dot_nt(enc, q * half_scale[h])
                d_a = dot_nt(enc, g * one[h])
                act, grad2 = silu_parts(half)
                a = (act * weight).astype(BF)
                d_s = (d_a * grad2 * weight).astype(BF)
                te = dot_nn(a, g * one[h]) + dot_nn(d_s, q * half_scale[h])
                tq = dot_tn(d_s, enc * half_scale[h])
                d_enc = te if d_enc is None else d_enc + te
                d_q = tq if d_q is None else d_q + tq
            denc_ref[own, :, cols] = d_enc.astype(BF)
            if own == 0:
                dq_s[:, cols] = d_q
            else:
                dq_s[:, cols] += d_q
    dq_ref[...] = dq_s[...].astype(BF)


def whole(shape):
    return pl.BlockSpec(shape, lambda i: (0,) * len(shape))


def per_hist(*shape):
    return pl.BlockSpec((1,) + shape, lambda i: (i, 0, 0))


def params():
    return pltpu.CompilerParams(vmem_limit_bytes=VMEM_LIMIT)


def forward(histories, weight_in, weight_out):
    hists, seq, width = histories.shape
    widths = [(width, BF), (4 * width, BF), (width, BF), (3 * width, BF), (width, BF), (PAIR, F32)]
    return pl.pallas_call(
        forward_kernel,
        grid=(hists,),
        in_specs=[per_hist(seq, width), whole(weight_in.shape), whole(weight_out.shape)],
        out_specs=[per_hist(seq, w) for w, _ in widths],
        out_shape=[jax.ShapeDtypeStruct((hists, seq, w), t) for w, t in widths],
        scratch_shapes=[pltpu.VMEM((seq, width), F32)],
        compiler_params=params(),
        cost_estimate=pl.CostEstimate(flops=8_000_000_000, bytes_accessed=12_000_000, transcendentals=4_000_000),
        name="layer_forward",
    )(histories, weight_in, weight_out)


def backward(histories, weight_in, weight_out, saved, d_enc):
    hists, seq, width = histories.shape
    total = hists * seq
    sg, gate, vqk, normed, inv = saved
    return pl.pallas_call(
        backward_kernel,
        grid=(hists,),
        in_specs=[
            per_hist(seq, width), whole(weight_in.shape), whole(weight_out.shape),
            per_hist(seq, 4 * width), per_hist(seq, width), per_hist(seq, 3 * width),
            per_hist(seq, width), per_hist(seq, PAIR), per_hist(seq, width),
        ],
        out_specs=[per_hist(seq, width), whole((width, 5 * width))],
        out_shape=[
            jax.ShapeDtypeStruct((hists, seq, width), BF),
            jax.ShapeDtypeStruct((width, 5 * width), BF),
        ],
        scratch_shapes=[
            pltpu.VMEM((total, width), BF),
            pltpu.VMEM((total, width), BF),
            pltpu.VMEM((total, width), BF),
            pltpu.VMEM((total, 4 * width), BF),
            pltpu.VMEM((seq, width), BF),
        ],
        compiler_params=params(),
        cost_estimate=pl.CostEstimate(flops=16_000_000_000, bytes_accessed=18_000_000, transcendentals=2_000_000),
        name="layer_backward",
    )(histories, weight_in, weight_out, sg, gate, vqk, normed, inv, d_enc)


def target(recv, encoded):
    hists, seq, width = encoded.shape
    slots = recv.shape[0]
    return pl.pallas_call(
        target_kernel,
        out_shape=[
            jax.ShapeDtypeStruct((slots, width), BF),
            jax.ShapeDtypeStruct((hists, seq, width), BF),
        ],
        scratch_shapes=[pltpu.VMEM((slots, width), F32)],
        compiler_params=params(),
        name="target_backward",
    )(recv, encoded)


def pack(capacity, slots, owner_ids, hist_slot, lengths, candidates, cotangent):
    width = candidates.shape[1]
    return pl.pallas_call(
        functools.partial(pack_kernel, capacity),
        out_shape=jax.ShapeDtypeStruct((slots, 2 * width + PAIR), BF),
        compiler_params=params(),
        name="pack_impressions",
    )(owner_ids, hist_slot[None, :], lengths[None, :], candidates, cotangent)


def unpack(capacity, owner_ids, returned, rows):
    return pl.pallas_call(
        functools.partial(unpack_kernel, capacity),
        out_shape=jax.ShapeDtypeStruct((rows, returned.shape[1]), BF),
        compiler_params=params(),
        name="unpack_grads",
    )(owner_ids, returned)


def exchange(x, devices):
    rows, width = x.shape
    got = lax.all_to_all(
        x.reshape(devices, rows // devices, width), AXES, split_axis=0, concat_axis=0, tiled=True
    )
    return got


def local(histories, weight_in, weight_out, candidates, cotangent, owner_ids, hist_slot, lengths):
    devices = lax.axis_size(AXES)
    imp_rows, width = candidates.shape
    capacity = max(2, 2 * imp_rows // devices)
    slots = devices * capacity
    send = pack(capacity, slots, owner_ids, hist_slot, lengths, candidates, cotangent)
    recv = exchange(send, devices).reshape(slots, 2 * width + PAIR)
    encoded, *saved = forward(histories, weight_in, weight_out)
    d_query, d_encoded = target(recv, encoded)
    returned = exchange(d_query, devices).reshape(slots, width)
    history_grad, parts = backward(histories, weight_in, weight_out, saved, d_encoded)
    sums = jnp.sum(exchange(parts, devices).astype(F32), axis=0)
    candidate_grad = unpack(capacity, owner_ids, returned, imp_rows)
    return history_grad, candidate_grad, sums[:, : 4 * width], sums[:, 4 * width :]


def solution(mesh):
    return jax.shard_map(
        local,
        mesh=mesh,
        in_specs=(
            P(AXES, None, None),
            P(),
            P(),
            P(AXES, None),
            P(AXES, None),
            P(AXES, None),
            P(AXES),
            P(AXES),
        ),
        out_specs=(P(AXES, None, None), P(AXES, None), P(AXES, None), P(AXES, None)),
        check_vma=False,
    )
```

```python
import functools

import jax
import jax.numpy as jnp
from jax import lax
from jax.experimental import pallas as pl
from jax.experimental.pallas import tpu as pltpu
from jax.sharding import PartitionSpec as P

HEADS = 8
HEAD_DIM = 64
PAIR = 128
EPS = 1e-05
BF = jnp.bfloat16
F32 = jnp.float32
AXES = ("hash", "dp")
VMEM_LIMIT = 60 * 1024 * 1024
MESH = pl.DeviceIdType.MESH
SIDE = 4
ORDERS = ("xyz", "yzx", "xyz", "yzx", "zxy")


def dot_nn(a, b):
    return lax.dot_general(a, b, (((1,), (0,)), ((), ())), preferred_element_type=F32)


def dot_nt(a, b):
    return lax.dot_general(a, b, (((1,), (1,)), ((), ())), preferred_element_type=F32)


def dot_tn(a, b):
    return lax.dot_general(a, b, (((0,), (0,)), ((), ())), preferred_element_type=F32)


def iota(shape, dim):
    return lax.broadcasted_iota(jnp.int32, shape, dim)


def silu_parts(half):
    t = jnp.tanh(half)
    plus = 1.0 + t
    return half * plus, plus * (1.0 + half * (1.0 - t))


def head_rows(scale):
    lanes = iota((1, PAIR), 1)
    first = jnp.where(lanes < HEAD_DIM, scale, 0.0).astype(BF)
    second = jnp.where(lanes < HEAD_DIM, 0.0, scale).astype(BF)
    return first, second


def slot_of(owner_col):
    rows = owner_col.shape[0]
    i, j = iota((rows, rows), 0), iota((rows, rows), 1)
    owner_row = jnp.sum(jnp.where(i == j, owner_col, 0), axis=0, keepdims=True)
    same = owner_col == owner_row
    place_col = jnp.sum(jnp.where(same & (j < i), 1, 0), axis=1, keepdims=True)
    place_row = jnp.sum(jnp.where(same & (i < j), 1, 0), axis=0, keepdims=True)
    return owner_col, place_col, owner_row, place_row


def pack_kernel(capacity, owner_ref, slot_ref, len_ref, cand_ref, cot_ref, out_ref):
    rows, width = cand_ref.shape
    slots = out_ref.shape[0]
    _, _, owner_row, place_row = slot_of(owner_ref[...])
    target_row = owner_row * capacity + place_row
    chosen = jnp.where(iota((slots, rows), 0) == target_row, 1.0, 0.0).astype(BF)
    out_ref[:, :width] = dot_nn(chosen, cand_ref[...]).astype(BF)
    out_ref[:, width : 2 * width] = dot_nn(chosen, cot_ref[...]).astype(BF)
    i, j = iota((rows, rows), 0), iota((rows, rows), 1)
    slot_col = jnp.sum(jnp.where(i == j, slot_ref[...], 0), axis=1, keepdims=True)
    len_col = jnp.sum(jnp.where(i == j, len_ref[...], 0), axis=1, keepdims=True)
    lane = iota((rows, PAIR), 1)
    meta = jnp.where(lane == 0, slot_col, jnp.where(lane == 1, len_col, 0))
    out_ref[:, 2 * width :] = dot_nn(chosen, meta.astype(F32).astype(BF)).astype(BF)


def unpack_kernel(capacity, owner_ref, ret_ref, out_ref):
    rows = out_ref.shape[0]
    slots = ret_ref.shape[0]
    owner_col, place_col, _, _ = slot_of(owner_ref[...])
    target_col = owner_col * capacity + place_col
    chosen = jnp.where(iota((rows, slots), 1) == target_col, 1.0, 0.0).astype(BF)
    out_ref[...] = dot_nn(chosen, ret_ref[...]).astype(BF)


def forward_kernel(x_ref, win_ref, wout_ref, enc_ref, sg_ref, gate_ref, vqk_ref, nrm_ref, inv_ref, mix_s):
    seq, width = x_ref.shape[1:]
    x = x_ref[0]
    xh = x * 0.5
    for part in range(4):
        cols = slice(part * width, (part + 1) * width)
        act, grad2 = silu_parts(dot_nn(xh, win_ref[:, cols]))
        sg_ref[0, :, cols] = (0.5 * grad2).astype(BF)
        if part == 0:
            gate_ref[0] = act.astype(BF)
        else:
            vqk_ref[0, :, (part - 1) * width : part * width] = act.astype(BF)
    cut = seq // 2
    seen = iota((cut, seq), 0) + cut >= iota((cut, seq), 1)
    half_scale = head_rows(0.5 * HEAD_DIM**-0.5)
    inv_seq = head_rows(1.0 / seq)
    for pair in range(width // PAIR):
        cols = slice(pair * PAIR, (pair + 1) * PAIR)
        v = vqk_ref[0, :, cols]
        q = vqk_ref[0, :, width + pair * PAIR : width + (pair + 1) * PAIR]
        k = vqk_ref[0, :, 2 * width + pair * PAIR : 2 * width + (pair + 1) * PAIR]
        total = None
        for h in range(2):
            qs, vs = q * half_scale[h], v * inv_seq[h]
            half = dot_nt(qs[:cut], k[:cut])
            first = jnp.where(seen[:, cut:], half * (1.0 + jnp.tanh(half)), 0.0).astype(BF)
            half = dot_nt(qs[cut:], k)
            second = jnp.where(seen, half * (1.0 + jnp.tanh(half)), 0.0).astype(BF)
            terms = (dot_nn(first, vs[:cut]), dot_nn(second, vs))
            total = terms if total is None else [a + b for a, b in zip(total, terms)]
        mix_s[:cut, cols] = total[0]
        mix_s[cut:, cols] = total[1]
    mixed = mix_s[...]
    centred = mixed - jnp.mean(mixed, axis=1, keepdims=True)
    inv = lax.rsqrt(jnp.mean(centred * centred, axis=1, keepdims=True) + EPS)
    normed = centred * inv
    nrm_ref[0] = normed.astype(BF)
    inv_ref[0] = jnp.broadcast_to(inv, (seq, PAIR))
    merged = (normed * gate_ref[0].astype(F32)).astype(BF)
    enc_ref[0] = (x.astype(F32) + dot_nn(merged, wout_ref[...])).astype(BF)


def place():
    hash_i, dp_i = lax.axis_index("hash"), lax.axis_index("dp")
    return {"y": hash_i // 2, "core": hash_i % 2, "x": dp_i // SIDE, "z": dp_i % SIDE}


def device_at(at):
    return (at["y"] * 2 + at["core"], at["x"] * SIDE + at["z"])


def partner(me, axis, jump):
    size = 2 if axis == "core" else SIDE
    at = dict(me)
    at[axis] = (me[axis] + jump) % size
    return at


def partners(me):
    return [partner(me, "core", 1)] + [partner(me, a, j) for a in "xyz" for j in (1, 2, 3)]


def along(ref, axes, axis, index):
    return ref.at[tuple(index if a == axis else slice(None) for a in axes)]


class Reduction:
    def __init__(self, parts, bufs, last, send, recv):
        self.me = place()
        self.parts, self.bufs, self.last = parts, bufs, last
        self.send, self.recv = send, recv

    def enter(self):
        barrier = pltpu.get_barrier_semaphore()
        others = partners(self.me)
        for other in others:
            pl.semaphore_signal(barrier, inc=1, device_id=device_at(other), device_id_type=MESH)
        pl.semaphore_wait(barrier, len(others))

    def copy(self, src, dst, number, other):
        return pltpu.make_async_remote_copy(
            src_ref=src, dst_ref=dst, send_sem=self.send.at[number], recv_sem=self.recv.at[number],
            device_id=device_at(other), device_id_type=MESH,
        )

    def kept(self, t, stage):
        axes = "zyx"
        for axis in ORDERS[t][: stage - 1]:
            axes = axes.replace(axis, "")
        return axes

    def copies(self, t, stage):
        if stage == 0:
            mate = partner(self.me, "core", 1)
            src = self.parts.at[t, :, :, mate["core"]]
            return [self.copy(src, self.bufs["r0"].at[t], t * 10, mate)]
        axis = ORDERS[t][stage - 1]
        src, dst = self.bufs["b%d" % stage].at[t], self.bufs["r%d" % stage].at[t]
        out = []
        for j in (1, 2, 3):
            other = partner(self.me, axis, j)
            number = t * 10 + 3 * (stage - 1) + j
            out.append(self.copy(along(src, self.kept(t, stage), axis, other[axis]), dst.at[j - 1], number, other))
        return out

    def start(self, t, stage):
        for c in self.copies(t, stage):
            c.start()

    def finish(self, t, stage):
        for c in self.copies(t, stage):
            c.wait_recv()
        got = self.bufs["r%d" % stage]
        if stage == 0:
            total = self.parts[t, :, :, self.me["core"]].astype(F32) + got[t].astype(F32)
        else:
            axis = ORDERS[t][stage - 1]
            own = along(self.bufs["b%d" % stage].at[t], self.kept(t, stage), axis, self.me[axis])
            total = own[...].astype(F32)
            for j in range(3):
                total = total + got[t, j].astype(F32)
        if stage < 3:
            self.bufs["b%d" % (stage + 1)][t] = total.astype(BF)
        else:
            self.last[0, :, t * PAIR : (t + 1) * PAIR] = total

    def advance(self, blocks, stage):
        for t in blocks:
            self.finish(t, stage)
            if stage < 3:
                self.start(t, stage + 1)

    def end_copies(self):
        base = 10 * len(ORDERS)
        return [
            self.copy(self.last.at[0], self.last.at[j], base + j - 1, partner(self.me, "z", j)) for j in (1, 2, 3)
        ]

    def end(self, win_ref, wout_ref):
        copies = self.end_copies()
        for c in copies:
            c.start()
        rows = []
        for j in range(SIDE):
            if j:
                copies[j - 1].wait_recv()
            value = self.last[j]
            mine = jnp.zeros((SIDE, value.shape[1]), F32)
            for z in range(SIDE):
                mine = jnp.where(self.me["z"] == z, value[z * SIDE : (z + 1) * SIDE], mine)
            rows.append(mine)
        for q in range(SIDE):
            mine = rows[0]
            for j in (1, 2, 3):
                mine = jnp.where((self.me["z"] + SIDE - j) % SIDE == q, rows[j], mine)
            for t in range(len(ORDERS)):
                ref, col = (wout_ref, 0) if t == 1 else (win_ref, 512 * max(0, t - 1))
                ref[:, col + q * PAIR : col + (q + 1) * PAIR] = mine[:, t * PAIR : (t + 1) * PAIR]
        for t in range(len(ORDERS)):
            for stage in range(4):
                for c in self.copies(t, stage):
                    c.wait_send()
        for c in copies:
            c.wait_send()


class Nothing:
    def __getattr__(self, name):
        return lambda *args: None


def backward_kernel(
    alone,
    x_hbm, win_hbm, wout_hbm, sg_hbm, gate_hbm, vqk_hbm, nrm_hbm, inv_hbm, denc_hbm,
    hg_ref, gin_ref, gout_ref,
    x_s, win_s, wout_s, sg_s, gate_s, vqk_s, nrm_s, inv_s, denc_s, load,
    xt_s, mg_s, dp_s, dm_s, parts_s, r0, r1, r2, r3, b1, b2, b3, last, send, recv,
):
    hists, seq, width = hg_ref.shape
    sources = (denc_hbm, wout_hbm, nrm_hbm, gate_hbm, inv_hbm, sg_hbm, x_hbm, vqk_hbm, win_hbm)
    places = (denc_s, wout_s, nrm_s, gate_s, inv_s, sg_s, x_s, vqk_s, win_s)
    loads = [pltpu.make_async_copy(a, b, load.at[i]) for i, (a, b) in enumerate(zip(sources, places))]
    for c in loads:
        c.start()
    bufs = {"r0": r0, "r1": r1, "r2": r2, "r3": r3, "b1": b1, "b2": b2, "b3": b3}
    comm = Nothing() if alone else Reduction(parts_s, bufs, last, send, recv)
    comm.enter()

    def rows_of(h):
        return pl.ds(pl.multiple_of(h * seq, seq), seq)

    def store_part(t, value):
        for z in range(SIDE):
            block = value[:, z * PAIR : (z + 1) * PAIR].astype(BF)
            parts_s[t, z] = block.reshape(parts_s.shape[2:])

    for c in loads[:7]:
        c.wait()

    def gate_step(h, carry):
        rows = rows_of(h)
        normed = nrm_s[h].astype(F32)
        gate = gate_s[h].astype(F32)
        mg_s[rows, :] = (normed * gate).astype(BF)
        d_merged = dot_nt(denc_s[h], wout_s[...])
        dp_s[rows, :width] = (d_merged * normed * sg_s[h, :, :width].astype(F32)).astype(BF)
        d_norm = d_merged * gate
        m1 = jnp.mean(d_norm, axis=1, keepdims=True)
        m2 = jnp.mean(d_norm * normed, axis=1, keepdims=True)
        dm_s[rows, :] = (inv_s[h][:, :1] * (d_norm - m1 - normed * m2)).astype(BF)
        xt_s[:, rows] = x_s[h].T
        return carry

    lax.fori_loop(0, hists, gate_step, 0)
    store_part(0, dot_nn(xt_s[...], dp_s[:, :width]))
    comm.start(0, 0)
    store_part(1, dot_tn(mg_s[...], denc_s[...].reshape(hists * seq, width)))
    comm.start(1, 0)
    loads[7].wait()

    cut = seq // 2
    seen = iota((cut, seq), 0) <= iota((cut, seq), 1)
    half_scale = head_rows(0.5 * HEAD_DIM**-0.5)
    one = head_rows(1.0)
    scales = (1.0 / seq, 0.5 * HEAD_DIM**-0.5 / seq, 1.0 / seq)

    def attn_step(h, carry):
        rows = rows_of(h)
        for pair in range(width // PAIR):
            lanes = [slice(b * width + pair * PAIR, b * width + (pair + 1) * PAIR) for b in range(4)]
            v = vqk_s[h, :, lanes[0]]
            q = vqk_s[h, :, lanes[1]]
            k = vqk_s[h, :, lanes[2]]
            dm = dm_s[rows, lanes[0]]
            sums = [None] * 6
            for head in range(2):
                qs, dms, ks = q * half_scale[head], dm * one[head], k * one[head]
                act, grad2 = silu_parts(dot_nt(k[:cut], qs))
                a0 = jnp.where(seen, act, 0.0).astype(BF)
                s0 = jnp.where(seen, dot_nt(v[:cut], dms) * grad2, 0.0).astype(BF)
                act, grad2 = silu_parts(dot_nt(k[cut:], qs[cut:]))
                a1 = jnp.where(seen[:, :cut], act, 0.0).astype(BF)
                s1 = jnp.where(seen[:, :cut], dot_nt(v[cut:], dms[cut:]) * grad2, 0.0).astype(BF)
                terms = (
                    dot_nn(a0, dms), dot_nn(a1, dms[cut:]),
                    dot_tn(s0[:, :cut], ks[:cut]), dot_tn(jnp.concatenate([s0[:, cut:], s1], axis=0), ks),
                    dot_nn(s0, qs), dot_nn(s1, qs[cut:]),
                )
                sums = [t if total is None else total + t for total, t in zip(sums, terms)]
            for i, value in enumerate(sums):
                b, part = 1 + i // 2, i % 2
                at = pl.ds(pl.multiple_of(h * seq + part * cut, cut), cut)
                sg = sg_s[h, part * cut : (part + 1) * cut, lanes[b]].astype(F32) * scales[b - 1]
                dp_s[at, lanes[b]] = (value * sg).astype(BF)
        for stage in range(4):
            @pl.when(h == stage)
            def _():
                comm.advance((0, 1), stage)
        return carry

    lax.fori_loop(0, hists, attn_step, 0)
    for t in (2, 3, 4):
        store_part(t, dot_nn(xt_s[...], dp_s[:, (t - 1) * width : t * width]))
        comm.start(t, 0)
    loads[8].wait()
    late = (2, 3, 4)

    def grads(lo, hi):
        for h in range(lo, hi):
            prod = dot_nt(dp_s[h * seq : (h + 1) * seq, :], win_s[...])
            hg_ref[h] = (denc_s[h].astype(F32) + prod).astype(BF)

    grads(0, hists // 2)
    comm.advance(late, 0)
    grads(hists // 2, hists)
    comm.advance(late, 1)
    comm.advance(late, 2)
    comm.advance(late, 3)
    comm.end(gin_ref, gout_ref)


def target_kernel(rows_ref, enc_ref, dq_ref, denc_ref, dq_s):
    hists, seq, width = enc_ref.shape
    slots = rows_ref.shape[0]
    meta = rows_ref[:, 2 * width :].astype(F32)
    hist_row = jnp.transpose(meta)[0:1, :]
    len_row = jnp.transpose(meta)[1:2, :]
    inverse = 1.0 / jnp.maximum(len_row, 1.0)
    positions = iota((seq, slots), 0).astype(F32)
    half_scale = head_rows(0.5 * HEAD_DIM**-0.5)
    one = head_rows(1.0)
    for own in range(hists):
        weight = jnp.where((positions < len_row) & (hist_row == float(own)), inverse, 0.0)
        for pair in range(width // PAIR):
            cols = slice(pair * PAIR, (pair + 1) * PAIR)
            enc = enc_ref[own, :, cols]
            q = rows_ref[:, cols]
            g = rows_ref[:, width + pair * PAIR : width + (pair + 1) * PAIR]
            d_enc = d_q = None
            for h in range(2):
                half = dot_nt(enc, q * half_scale[h])
                d_a = dot_nt(enc, g * one[h])
                act, grad2 = silu_parts(half)
                a = (act * weight).astype(BF)
                d_s = (d_a * grad2 * weight).astype(BF)
                te = dot_nn(a, g * one[h]) + dot_nn(d_s, q * half_scale[h])
                tq = dot_tn(d_s, enc * half_scale[h])
                d_enc = te if d_enc is None else d_enc + te
                d_q = tq if d_q is None else d_q + tq
            denc_ref[own, :, cols] = d_enc.astype(BF)
            if own == 0:
                dq_s[:, cols] = d_q
            else:
                dq_s[:, cols] += d_q
    dq_ref[...] = dq_s[...].astype(BF)


def whole(shape):
    return pl.BlockSpec(shape, lambda i: (0,) * len(shape))


def per_hist(*shape):
    return pl.BlockSpec((1,) + shape, lambda i: (i, 0, 0))


def params():
    return pltpu.CompilerParams(vmem_limit_bytes=VMEM_LIMIT)


def forward(histories, weight_in, weight_out):
    hists, seq, width = histories.shape
    widths = [(width, BF), (4 * width, BF), (width, BF), (3 * width, BF), (width, BF), (PAIR, F32)]
    return pl.pallas_call(
        forward_kernel,
        grid=(hists,),
        in_specs=[per_hist(seq, width), whole(weight_in.shape), whole(weight_out.shape)],
        out_specs=[per_hist(seq, w) for w, _ in widths],
        out_shape=[jax.ShapeDtypeStruct((hists, seq, w), t) for w, t in widths],
        scratch_shapes=[pltpu.VMEM((seq, width), F32)],
        compiler_params=params(),
        cost_estimate=pl.CostEstimate(flops=8_000_000_000, bytes_accessed=12_000_000, transcendentals=4_000_000),
        name="layer_forward",
    )(histories, weight_in, weight_out)


def backward(histories, weight_in, weight_out, saved, d_enc, alone=False):
    hists, seq, width = histories.shape
    total = hists * seq
    sg, gate, vqk, normed, inv = saved
    operands = (histories, weight_in, weight_out, sg, gate, vqk, normed, inv, d_enc)
    tile = width // 32
    block = (tile, PAIR)
    n = len(ORDERS)
    lead = [(SIDE,) * 3, (3,) + (SIDE,) * 2, (3, SIDE), (3,), (SIDE,) * 3, (SIDE,) * 2, (SIDE,)]
    scratch = [pltpu.VMEM(o.shape, o.dtype) for o in operands]
    scratch += [
        pltpu.SemaphoreType.DMA((len(operands),)),
        pltpu.VMEM((width, total), BF),
        pltpu.VMEM((total, width), BF),
        pltpu.VMEM((total, 4 * width), BF),
        pltpu.VMEM((total, width), BF),
        pltpu.VMEM((n, SIDE, SIDE, 2, SIDE) + block, BF),
    ]
    scratch += [pltpu.VMEM((n,) + dims + block, BF) for dims in lead]
    scratch += [
        pltpu.VMEM((SIDE, tile, n * PAIR), F32),
        pltpu.SemaphoreType.DMA((10 * n + 3,)),
        pltpu.SemaphoreType.DMA((10 * n + 3,)),
    ]
    more = {} if alone else {"collective_id": 0, "has_side_effects": True}
    return pl.pallas_call(
        functools.partial(backward_kernel, alone),
        in_specs=[pl.BlockSpec(memory_space=pl.ANY)] * len(operands),
        out_specs=[pl.BlockSpec(memory_space=pltpu.VMEM)] * 3,
        out_shape=[
            jax.ShapeDtypeStruct((hists, seq, width), BF),
            jax.ShapeDtypeStruct((SIDE, 4 * width), F32),
            jax.ShapeDtypeStruct((SIDE, width), F32),
        ],
        scratch_shapes=scratch,
        compiler_params=pltpu.CompilerParams(vmem_limit_bytes=VMEM_LIMIT, **more),
        cost_estimate=pl.CostEstimate(flops=16_000_000_000, bytes_accessed=18_000_000, transcendentals=2_000_000),
        name="layer_backward",
    )(*operands)


def target(recv, encoded):
    hists, seq, width = encoded.shape
    slots = recv.shape[0]
    return pl.pallas_call(
        target_kernel,
        out_shape=[
            jax.ShapeDtypeStruct((slots, width), BF),
            jax.ShapeDtypeStruct((hists, seq, width), BF),
        ],
        scratch_shapes=[pltpu.VMEM((slots, width), F32)],
        compiler_params=params(),
        name="target_backward",
    )(recv, encoded)


def pack(capacity, slots, owner_ids, hist_slot, lengths, candidates, cotangent):
    width = candidates.shape[1]
    return pl.pallas_call(
        functools.partial(pack_kernel, capacity),
        out_shape=jax.ShapeDtypeStruct((slots, 2 * width + PAIR), BF),
        compiler_params=params(),
        name="pack_impressions",
    )(owner_ids, hist_slot[None, :], lengths[None, :], candidates, cotangent)


def unpack(capacity, owner_ids, returned, rows):
    return pl.pallas_call(
        functools.partial(unpack_kernel, capacity),
        out_shape=jax.ShapeDtypeStruct((rows, returned.shape[1]), BF),
        compiler_params=params(),
        name="unpack_grads",
    )(owner_ids, returned)


def exchange(x, devices):
    rows, width = x.shape
    got = lax.all_to_all(
        x.reshape(devices, rows // devices, width), AXES, split_axis=0, concat_axis=0, tiled=True
    )
    return got


def local(histories, weight_in, weight_out, candidates, cotangent, owner_ids, hist_slot, lengths):
    devices = lax.axis_size(AXES)
    imp_rows, width = candidates.shape
    capacity = max(2, 2 * imp_rows // devices)
    slots = devices * capacity
    send = pack(capacity, slots, owner_ids, hist_slot, lengths, candidates, cotangent)
    recv = exchange(send, devices).reshape(slots, 2 * width + PAIR)
    encoded, *saved = forward(histories, weight_in, weight_out)
    d_query, d_encoded = target(recv, encoded)
    returned = exchange(d_query, devices).reshape(slots, width)
    history_grad, in_grad, out_grad = backward(histories, weight_in, weight_out, saved, d_encoded)
    candidate_grad = unpack(capacity, owner_ids, returned, imp_rows)
    return history_grad, candidate_grad, in_grad, out_grad


def solution(mesh):
    return jax.shard_map(
        local,
        mesh=mesh,
        in_specs=(
            P(AXES, None, None),
            P(),
            P(),
            P(AXES, None),
            P(AXES, None),
            P(AXES, None),
            P(AXES),
            P(AXES),
        ),
        out_specs=(P(AXES, None, None), P(AXES, None), P(AXES, None), P(AXES, None)),
        check_vma=False,
    )
```

```python
import functools

import jax
import jax.numpy as jnp
from jax import lax
from jax.experimental import pallas as pl
from jax.experimental.pallas import tpu as pltpu
from jax.sharding import PartitionSpec as P

HEADS = 8
HEAD_DIM = 64
PAIR = 128
EPS = 1e-05
BF = jnp.bfloat16
F32 = jnp.float32
AXES = ("hash", "dp")
VMEM_LIMIT = 60 * 1024 * 1024
MESH = pl.DeviceIdType.MESH
SIDE = 4
ORDERS = ("xyz", "yzx", "xyz", "yzx", "zxy")


def dot_nn(a, b):
    return lax.dot_general(a, b, (((1,), (0,)), ((), ())), preferred_element_type=F32)


def dot_nt(a, b):
    return lax.dot_general(a, b, (((1,), (1,)), ((), ())), preferred_element_type=F32)


def dot_tn(a, b):
    return lax.dot_general(a, b, (((0,), (0,)), ((), ())), preferred_element_type=F32)


def iota(shape, dim):
    return lax.broadcasted_iota(jnp.int32, shape, dim)


def silu_parts(half):
    t = jnp.tanh(half)
    plus = 1.0 + t
    return half * plus, plus * (1.0 + half * (1.0 - t))


def head_rows(scale):
    lanes = iota((1, PAIR), 1)
    first = jnp.where(lanes < HEAD_DIM, scale, 0.0).astype(BF)
    second = jnp.where(lanes < HEAD_DIM, 0.0, scale).astype(BF)
    return first, second


def lower_half(shape):
    return iota(shape, 1) < SIDE


def turn(x):
    return pltpu.roll(x, SIDE, 1)


def chunk_at(device, devices):
    return device % 2 * (devices // 2) + device // 2


def to_chunks(ref, value):
    rows, lanes = value.shape
    v = value.reshape(rows // 8, 8, lanes)
    low = lower_half((rows // 8, 8, PAIR))
    for pos in range(0, lanes // PAIR, 4):
        even, odd = [], []
        for g in (pos, pos + 2):
            first, second = v[:, :, g * PAIR : (g + 1) * PAIR], v[:, :, (g + 1) * PAIR : (g + 2) * PAIR]
            even.append(jnp.where(low, first, turn(second)))
            odd.append(jnp.where(low, turn(first), second))
        ref[: rows // 8, pos * SIDE : (pos + 4) * SIDE, :] = jnp.concatenate(even, axis=1).astype(BF)
        ref[rows // 8 :, pos * SIDE : (pos + 4) * SIDE, :] = jnp.concatenate(odd, axis=1).astype(BF)


def from_chunks(ref, block):
    half = ref.shape[0] // 2
    low = lower_half((half, 8, PAIR))
    at = block // 2 * 8
    tile = at // 16 * 16
    first = ref[:half, tile : tile + 16, :].astype(F32)[:, at - tile : at - tile + 8]
    second = ref[half:, tile : tile + 16, :].astype(F32)[:, at - tile : at - tile + 8]
    if block % 2 == 0:
        rows = jnp.where(low, first, turn(second))
    else:
        rows = jnp.where(low, turn(first), second)
    return rows.reshape(half * 8, PAIR).astype(BF)


def as_column(row):
    rows = row.shape[1]
    same = iota((rows, rows), 0) == iota((rows, rows), 1)
    return jnp.sum(jnp.where(same, row, 0), axis=1, keepdims=True)


def slot_of(owner_row):
    rows = owner_row.shape[1]
    i, j = iota((rows, rows), 0), iota((rows, rows), 1)
    owner_col = as_column(owner_row)
    same = owner_col == owner_row
    place_col = jnp.sum(jnp.where(same & (j < i), 1, 0), axis=1, keepdims=True)
    place_row = jnp.sum(jnp.where(same & (i < j), 1, 0), axis=0, keepdims=True)
    return owner_col, place_col, owner_row, place_row


def unpack_kernel(capacity, owner_ref, ret_ref, out_ref):
    rows = out_ref.shape[0]
    slots = ret_ref.shape[0]
    owner_col, place_col, _, _ = slot_of(owner_ref[...])
    target_col = owner_col * capacity + place_col
    chosen = jnp.where(iota((rows, slots), 1) == target_col, 1.0, 0.0).astype(BF)
    out_ref[...] = dot_nn(chosen, ret_ref[...]).astype(BF)


def place():
    hash_i, dp_i = lax.axis_index("hash"), lax.axis_index("dp")
    return {"y": hash_i // 2, "core": hash_i % 2, "x": dp_i // SIDE, "z": dp_i % SIDE}


def device_at(at):
    return (at["y"] * 2 + at["core"], at["x"] * SIDE + at["z"])


def partner(me, axis, jump):
    size = 2 if axis == "core" else SIDE
    at = dict(me)
    at[axis] = (me[axis] + jump) % size
    return at


def partners(me):
    return [partner(me, "core", 1)] + [partner(me, a, j) for a in "xyz" for j in (1, 2, 3)]


def facts_by_owner(owner_row, place_row, slot_row, length_row, devices, capacity):
    rows = owner_row.shape[1]
    slot, length = as_column(slot_row), as_column(length_row)
    lane = iota((rows, PAIR), 1)
    total = jnp.zeros((devices, PAIR), F32)
    for p in range(capacity):
        chosen = (iota((devices, rows), 0) == owner_row) & (place_row == p)
        value = jnp.where(lane == p, slot, jnp.where(lane == capacity + p, length, 0))
        total += dot_nn(jnp.where(chosen, 1.0, 0.0).astype(BF), value.astype(F32).astype(BF))
    return total


def received(facts, shape):
    devices, slots = facts.shape[0], shape[1]
    capacity = slots // devices
    lane, source = iota((devices, slots), 1), iota((devices, slots), 0)
    rows = []
    for first in (0, capacity):
        total = jnp.zeros((devices, slots), F32)
        for p in range(capacity):
            total = jnp.where(lane == source * capacity + p, facts[:, first + p : first + p + 1], total)
        rows.append(jnp.sum(total, axis=0, keepdims=True))
    return jnp.where(iota(shape, 0) == 0, rows[0], rows[1])


def forward_kernel(
    alone, capacity,
    owner_ref, slot_ref, length_ref, cand_ref, cot_ref, x_hbm, win_hbm, wout_hbm,
    facts_ref, recv_hbm, enc_hbm, sg_hbm, gate_hbm, vqk_hbm, nrm_hbm, inv_hbm,
    x_s, win_s, wout_s, load, send_s, enc_s, sg_s, gate_s, vqk_s, nrm_s, inv_s, save, mix_s, send, recv, own, tell_s, told_s, tell, told,
):
    hists, seq, width = x_s.shape
    rows = cand_ref.shape[0]
    loads = [
        pltpu.make_async_copy(a, b, load.at[i])
        for i, (a, b) in enumerate(((x_hbm, x_s), (win_hbm, win_s), (wout_hbm, wout_s)))
    ]
    for c in loads:
        c.start()
    devices = send_s.shape[0]
    if not alone:
        hash_i, dp_i = lax.axis_index("hash"), lax.axis_index("dp")
        ring = lax.axis_size("dp")
        me = hash_i * ring + dp_i
        barrier = pltpu.get_barrier_semaphore()

        def greet(jump, carry):
            to = lax.rem(me + jump, devices)
            pl.semaphore_signal(barrier, inc=1, device_id=(to // ring, to % ring), device_id_type=MESH)
            return carry

        lax.fori_loop(1, devices, greet, 0)
    _, _, owner_row, place_row = slot_of(owner_ref[...])
    slots = devices * capacity
    chosen = jnp.where(iota((slots, rows), 0) == owner_row * capacity + place_row, 1.0, 0.0).astype(BF)
    facts = facts_by_owner(owner_row, place_row, slot_ref[...], length_ref[...], devices, capacity)
    tell_s[...] = facts.reshape(devices, 1, PAIR)
    sent_rows = width // PAIR * SIDE
    for i, value in enumerate((cand_ref[...], cot_ref[...])):
        to_chunks(send_s.at[:, i * sent_rows : (i + 1) * sent_rows], dot_nn(chosen, value))
    if not alone:
        pl.semaphore_wait(barrier, devices - 1)

        def push(jump, carry):
            to = lax.rem(me + lax.rem(jump * 37, devices), devices)
            pltpu.make_async_remote_copy(
                src_ref=send_s.at[chunk_at(to, devices)], dst_ref=recv_hbm.at[chunk_at(me, devices)],
                send_sem=send, recv_sem=recv, device_id=(to // ring, to % ring), device_id_type=MESH,
            ).start()
            pltpu.make_async_remote_copy(
                src_ref=tell_s.at[to], dst_ref=told_s.at[me],
                send_sem=tell, recv_sem=told, device_id=(to // ring, to % ring), device_id_type=MESH,
            ).start()
            return carry

        lax.fori_loop(1, devices, push, 0)
        keep = pltpu.make_async_copy(send_s.at[chunk_at(me, devices)], recv_hbm.at[chunk_at(me, devices)], own)
        keep.start()
        told_s[me] = tell_s[me]
    for c in loads:
        c.wait()
    cut = seq // 2
    seen = iota((cut, seq), 0) + cut >= iota((cut, seq), 1)
    half_scale = head_rows(0.5 * HEAD_DIM**-0.5)
    inv_seq = head_rows(1.0 / seq)
    outs = ((enc_s, enc_hbm), (sg_s, sg_hbm), (gate_s, gate_hbm), (vqk_s, vqk_hbm), (nrm_s, nrm_hbm), (inv_s, inv_hbm))

    def saves(h):
        return [pltpu.make_async_copy(a.at[h], b.at[h], save.at[i, h]) for i, (a, b) in enumerate(outs)]

    def one(hist, carry):
        x = x_s[hist]
        xh = x * 0.5
        for part in range(4):
            cols = slice(part * width, (part + 1) * width)
            act, grad2 = silu_parts(dot_nn(xh, win_s[:, cols]))
            sg_s[hist, :, cols] = (0.5 * grad2).astype(BF)
            if part == 0:
                gate_s[hist] = act.astype(BF)
            else:
                vqk_s[hist, :, (part - 1) * width : part * width] = act.astype(BF)
        for pair in range(width // PAIR):
            lanes = [slice(b * width + pair * PAIR, b * width + (pair + 1) * PAIR) for b in range(3)]
            v = vqk_s[hist, :, lanes[0]]
            q = vqk_s[hist, :, lanes[1]]
            k = vqk_s[hist, :, lanes[2]]
            total = None
            for h in range(2):
                qs, vs = q * half_scale[h], v * inv_seq[h]
                half = dot_nt(qs[:cut], k[:cut])
                first = jnp.where(seen[:, cut:], half * (1.0 + jnp.tanh(half)), 0.0).astype(BF)
                half = dot_nt(qs[cut:], k)
                second = jnp.where(seen, half * (1.0 + jnp.tanh(half)), 0.0).astype(BF)
                terms = (dot_nn(first, vs[:cut]), dot_nn(second, vs))
                total = terms if total is None else [a + b for a, b in zip(total, terms)]
            mix_s[:cut, lanes[0]] = total[0]
            mix_s[cut:, lanes[0]] = total[1]
        mixed = mix_s[...]
        centred = mixed - jnp.mean(mixed, axis=1, keepdims=True)
        inv = lax.rsqrt(jnp.mean(centred * centred, axis=1, keepdims=True) + EPS)
        normed = centred * inv
        nrm_s[hist] = normed.astype(BF)
        inv_s[hist] = jnp.broadcast_to(inv, (seq, PAIR))
        merged = (normed * gate_s[hist].astype(F32)).astype(BF)
        enc_s[hist] = (x.astype(F32) + dot_nn(merged, wout_s[...])).astype(BF)
        for c in saves(hist):
            c.start()
        return carry

    lax.fori_loop(0, hists, one, 0)
    for h in range(hists):
        for c in saves(h):
            c.wait()
    if not alone:
        keep.wait()
        all_but_one = pl.ds(0, devices - 1)
        pltpu.make_async_remote_copy(
            src_ref=send_s.at[all_but_one], dst_ref=recv_hbm.at[all_but_one], send_sem=send, recv_sem=recv,
            device_id=(lax.rem(hash_i + 1, devices // ring), dp_i), device_id_type=MESH,
        ).wait()
        pltpu.make_async_remote_copy(
            src_ref=tell_s.at[all_but_one], dst_ref=told_s.at[all_but_one], send_sem=tell, recv_sem=told,
            device_id=(lax.rem(hash_i + 1, devices // ring), dp_i), device_id_type=MESH,
        ).wait()
        facts_ref[...] = received(told_s[...].reshape(devices, PAIR), facts_ref.shape)


def along(ref, axes, axis, index):
    return ref.at[tuple(index if a == axis else slice(None) for a in axes)]


class Reduction:
    def __init__(self, parts, bufs, last, send, recv):
        self.me = place()
        self.parts, self.bufs, self.last = parts, bufs, last
        self.send, self.recv = send, recv

    def enter(self):
        barrier = pltpu.get_barrier_semaphore()
        others = partners(self.me)
        for other in others:
            pl.semaphore_signal(barrier, inc=1, device_id=device_at(other), device_id_type=MESH)
        pl.semaphore_wait(barrier, len(others))

    def copy(self, src, dst, number, other):
        return pltpu.make_async_remote_copy(
            src_ref=src, dst_ref=dst, send_sem=self.send.at[number], recv_sem=self.recv.at[number],
            device_id=device_at(other), device_id_type=MESH,
        )

    def kept(self, t, stage):
        axes = "zyx"
        for axis in ORDERS[t][: stage - 1]:
            axes = axes.replace(axis, "")
        return axes

    def copies(self, t, stage):
        if stage == 0:
            mate = partner(self.me, "core", 1)
            src = self.parts.at[t, :, :, mate["core"]]
            return [self.copy(src, self.bufs["r0"].at[t], t * 10, mate)]
        axis = ORDERS[t][stage - 1]
        src, dst = self.bufs["b%d" % stage].at[t], self.bufs["r%d" % stage].at[t]
        out = []
        for j in (1, 2, 3):
            other = partner(self.me, axis, j)
            number = t * 10 + 3 * (stage - 1) + j
            out.append(self.copy(along(src, self.kept(t, stage), axis, other[axis]), dst.at[j - 1], number, other))
        return out

    def start(self, t, stage):
        for c in self.copies(t, stage):
            c.start()

    def finish(self, t, stage):
        for c in self.copies(t, stage):
            c.wait_recv()
        got = self.bufs["r%d" % stage]
        if stage == 0:
            total = self.parts[t, :, :, self.me["core"]].astype(F32) + got[t].astype(F32)
        else:
            axis = ORDERS[t][stage - 1]
            own = along(self.bufs["b%d" % stage].at[t], self.kept(t, stage), axis, self.me[axis])
            total = own[...].astype(F32)
            for j in range(3):
                total = total + got[t, j].astype(F32)
        if stage < 3:
            self.bufs["b%d" % (stage + 1)][t] = total.astype(BF)
        else:
            self.last[0, :, t * PAIR : (t + 1) * PAIR] = total

    def advance(self, blocks, stage):
        for t in blocks:
            self.finish(t, stage)
            if stage < 3:
                self.start(t, stage + 1)

    def end_copies(self):
        base = 10 * len(ORDERS)
        return [
            self.copy(self.last.at[0], self.last.at[j], base + j - 1, partner(self.me, "z", j)) for j in (1, 2, 3)
        ]

    def end(self, win_ref, wout_ref):
        copies = self.end_copies()
        for c in copies:
            c.start()
        rows = []
        for j in range(SIDE):
            if j:
                copies[j - 1].wait_recv()
            value = self.last[j]
            mine = jnp.zeros((SIDE, value.shape[1]), F32)
            for z in range(SIDE):
                mine = jnp.where(self.me["z"] == z, value[z * SIDE : (z + 1) * SIDE], mine)
            rows.append(mine)
        for q in range(SIDE):
            mine = rows[0]
            for j in (1, 2, 3):
                mine = jnp.where((self.me["z"] + SIDE - j) % SIDE == q, rows[j], mine)
            for t in range(len(ORDERS)):
                ref, col = (wout_ref, 0) if t == 1 else (win_ref, 512 * max(0, t - 1))
                ref[:, col + q * PAIR : col + (q + 1) * PAIR] = mine[:, t * PAIR : (t + 1) * PAIR]
        for t in range(len(ORDERS)):
            for stage in range(4):
                for c in self.copies(t, stage):
                    c.wait_send()
        for c in copies:
            c.wait_send()


class Nothing:
    def __getattr__(self, name):
        return lambda *args: None


def backward_kernel(
    alone,
    x_hbm, win_hbm, wout_hbm, sg_hbm, gate_hbm, vqk_hbm, nrm_hbm, inv_hbm, denc_hbm,
    hg_ref, gin_ref, gout_ref,
    x_s, win_s, wout_s, sg_s, gate_s, vqk_s, nrm_s, inv_s, denc_s, load,
    xt_s, mg_s, dp_s, dm_s, parts_s, r0, r1, r2, r3, b1, b2, b3, last, send, recv,
):
    hists, seq, width = hg_ref.shape
    sources = (denc_hbm, wout_hbm, nrm_hbm, gate_hbm, inv_hbm, sg_hbm, x_hbm, vqk_hbm, win_hbm)
    places = (denc_s, wout_s, nrm_s, gate_s, inv_s, sg_s, x_s, vqk_s, win_s)
    loads = [pltpu.make_async_copy(a, b, load.at[i]) for i, (a, b) in enumerate(zip(sources, places))]
    for c in loads:
        c.start()
    bufs = {"r0": r0, "r1": r1, "r2": r2, "r3": r3, "b1": b1, "b2": b2, "b3": b3}
    comm = Nothing() if alone else Reduction(parts_s, bufs, last, send, recv)
    comm.enter()

    def rows_of(h):
        return pl.ds(pl.multiple_of(h * seq, seq), seq)

    def store_part(t, value):
        for z in range(SIDE):
            block = value[:, z * PAIR : (z + 1) * PAIR].astype(BF)
            parts_s[t, z] = block.reshape(parts_s.shape[2:])

    for c in loads[:7]:
        c.wait()

    def gate_step(h, carry):
        rows = rows_of(h)
        normed = nrm_s[h].astype(F32)
        gate = gate_s[h].astype(F32)
        mg_s[rows, :] = (normed * gate).astype(BF)
        d_merged = dot_nt(denc_s[h], wout_s[...])
        dp_s[rows, :width] = (d_merged * normed * sg_s[h, :, :width].astype(F32)).astype(BF)
        d_norm = d_merged * gate
        m1 = jnp.mean(d_norm, axis=1, keepdims=True)
        m2 = jnp.mean(d_norm * normed, axis=1, keepdims=True)
        dm_s[rows, :] = (inv_s[h][:, :1] * (d_norm - m1 - normed * m2)).astype(BF)
        xt_s[:, rows] = x_s[h].T
        return carry

    lax.fori_loop(0, hists, gate_step, 0)
    store_part(0, dot_nn(xt_s[...], dp_s[:, :width]))
    comm.start(0, 0)
    store_part(1, dot_tn(mg_s[...], denc_s[...].reshape(hists * seq, width)))
    comm.start(1, 0)
    loads[7].wait()

    cut = seq // 2
    seen = iota((cut, seq), 0) <= iota((cut, seq), 1)
    half_scale = head_rows(0.5 * HEAD_DIM**-0.5)
    one = head_rows(1.0)
    scales = (1.0 / seq, 0.5 * HEAD_DIM**-0.5 / seq, 1.0 / seq)

    def attn_step(h, carry):
        rows = rows_of(h)
        for pair in range(width // PAIR):
            lanes = [slice(b * width + pair * PAIR, b * width + (pair + 1) * PAIR) for b in range(4)]
            v = vqk_s[h, :, lanes[0]]
            q = vqk_s[h, :, lanes[1]]
            k = vqk_s[h, :, lanes[2]]
            dm = dm_s[rows, lanes[0]]
            sums = [None] * 6
            for head in range(2):
                qs, dms, ks = q * half_scale[head], dm * one[head], k * one[head]
                act, grad2 = silu_parts(dot_nt(k[:cut], qs))
                a0 = jnp.where(seen, act, 0.0).astype(BF)
                s0 = jnp.where(seen, dot_nt(v[:cut], dms) * grad2, 0.0).astype(BF)
                act, grad2 = silu_parts(dot_nt(k[cut:], qs[cut:]))
                a1 = jnp.where(seen[:, :cut], act, 0.0).astype(BF)
                s1 = jnp.where(seen[:, :cut], dot_nt(v[cut:], dms[cut:]) * grad2, 0.0).astype(BF)
                terms = (
                    dot_nn(a0, dms), dot_nn(a1, dms[cut:]),
                    dot_tn(s0[:, :cut], ks[:cut]), dot_tn(jnp.concatenate([s0[:, cut:], s1], axis=0), ks),
                    dot_nn(s0, qs), dot_nn(s1, qs[cut:]),
                )
                sums = [t if total is None else total + t for total, t in zip(sums, terms)]
            for i, value in enumerate(sums):
                b, part = 1 + i // 2, i % 2
                at = pl.ds(pl.multiple_of(h * seq + part * cut, cut), cut)
                sg = sg_s[h, part * cut : (part + 1) * cut, lanes[b]].astype(F32) * scales[b - 1]
                dp_s[at, lanes[b]] = (value * sg).astype(BF)
        for stage in range(4):
            @pl.when(h == stage)
            def _():
                comm.advance((0, 1), stage)
        return carry

    lax.fori_loop(0, hists, attn_step, 0)
    for t in (2, 3, 4):
        store_part(t, dot_nn(xt_s[...], dp_s[:, (t - 1) * width : t * width]))
        comm.start(t, 0)
    loads[8].wait()
    late = (2, 3, 4)

    def grads(lo, hi):
        for h in range(lo, hi):
            prod = dot_nt(dp_s[h * seq : (h + 1) * seq, :], win_s[...])
            hg_ref[h] = (denc_s[h].astype(F32) + prod).astype(BF)

    grads(0, hists // 2)
    comm.advance(late, 0)
    grads(hists // 2, hists)
    comm.advance(late, 1)
    comm.advance(late, 2)
    comm.advance(late, 3)
    comm.end(gin_ref, gout_ref)


def target_kernel(facts_ref, recv_ref, enc_ref, dq_ref, denc_ref, dq_s):
    hists, seq, width = enc_ref.shape
    slots = dq_ref.shape[0]
    blocks = width // PAIR
    hist_row, len_row = facts_ref[0:1], facts_ref[1:2]
    inverse = 1.0 / jnp.maximum(len_row, 1.0)
    positions = iota((seq, slots), 0).astype(F32)
    half_scale = head_rows(0.5 * HEAD_DIM**-0.5)
    one = head_rows(1.0)
    queries = [from_chunks(recv_ref, b) for b in range(2 * blocks)]
    for own in range(hists):
        weight = jnp.where((positions < len_row) & (hist_row == float(own)), inverse, 0.0)
        for pair in range(blocks):
            cols = slice(pair * PAIR, (pair + 1) * PAIR)
            enc = enc_ref[own, :, cols]
            q, g = queries[pair], queries[blocks + pair]
            d_enc = d_q = None
            for h in range(2):
                half = dot_nt(enc, q * half_scale[h])
                d_a = dot_nt(enc, g * one[h])
                act, grad2 = silu_parts(half)
                a = (act * weight).astype(BF)
                d_s = (d_a * grad2 * weight).astype(BF)
                te = dot_nn(a, g * one[h]) + dot_nn(d_s, q * half_scale[h])
                tq = dot_tn(d_s, enc * half_scale[h])
                d_enc = te if d_enc is None else d_enc + te
                d_q = tq if d_q is None else d_q + tq
            denc_ref[own, :, cols] = d_enc.astype(BF)
            if own == 0:
                dq_s[:, cols] = d_q
            else:
                dq_s[:, cols] += d_q
    dq_ref[...] = dq_s[...].astype(BF)


def forward(histories, weight_in, weight_out, routing, candidates, cotangent, devices, capacity, alone=False):
    hists, seq, width = histories.shape
    chunk = (devices, 2 * width // PAIR * SIDE, PAIR)
    widths = [(width, BF), (4 * width, BF), (width, BF), (3 * width, BF), (width, BF), (PAIR, F32)]
    kept = [((hists, seq, w), t) for w, t in widths]
    scratch = [pltpu.VMEM(o.shape, o.dtype) for o in (histories, weight_in, weight_out)]
    scratch += [pltpu.SemaphoreType.DMA((3,)), pltpu.VMEM(chunk, BF)]
    scratch += [pltpu.VMEM(*k) for k in kept]
    scratch += [pltpu.SemaphoreType.DMA((len(kept), hists)), pltpu.VMEM((seq, width), F32)]
    scratch += [pltpu.SemaphoreType.DMA] * 3
    scratch += [pltpu.VMEM((devices, 1, PAIR), F32)] * 2 + [pltpu.SemaphoreType.DMA] * 2
    vmem = pl.BlockSpec(memory_space=pltpu.VMEM)
    hbm = pl.BlockSpec(memory_space=pl.ANY)
    return pl.pallas_call(
        functools.partial(forward_kernel, alone, capacity),
        in_specs=[vmem] * 5 + [hbm] * 3,
        out_specs=[vmem] + [hbm] * (1 + len(kept)),
        out_shape=[jax.ShapeDtypeStruct((8, devices * capacity), F32), jax.ShapeDtypeStruct(chunk, BF)] + [jax.ShapeDtypeStruct(*k) for k in kept],
        scratch_shapes=scratch,
        compiler_params=pltpu.CompilerParams(vmem_limit_bytes=VMEM_LIMIT, **({} if alone else {"collective_id": 1, "has_side_effects": True})),
        cost_estimate=pl.CostEstimate(flops=8_000_000_000, bytes_accessed=12_000_000, transcendentals=4_000_000),
        name="route_and_forward",
    )(*routing, candidates, cotangent, histories, weight_in, weight_out)


def backward(histories, weight_in, weight_out, saved, d_enc, alone=False):
    hists, seq, width = histories.shape
    total = hists * seq
    sg, gate, vqk, normed, inv = saved
    operands = (histories, weight_in, weight_out, sg, gate, vqk, normed, inv, d_enc)
    tile = width // 32
    block = (tile, PAIR)
    n = len(ORDERS)
    lead = [(SIDE,) * 3, (3,) + (SIDE,) * 2, (3, SIDE), (3,), (SIDE,) * 3, (SIDE,) * 2, (SIDE,)]
    scratch = [pltpu.VMEM(o.shape, o.dtype) for o in operands]
    scratch += [
        pltpu.SemaphoreType.DMA((len(operands),)),
        pltpu.VMEM((width, total), BF),
        pltpu.VMEM((total, width), BF),
        pltpu.VMEM((total, 4 * width), BF),
        pltpu.VMEM((total, width), BF),
        pltpu.VMEM((n, SIDE, SIDE, 2, SIDE) + block, BF),
    ]
    scratch += [pltpu.VMEM((n,) + dims + block, BF) for dims in lead]
    scratch += [
        pltpu.VMEM((SIDE, tile, n * PAIR), F32),
        pltpu.SemaphoreType.DMA((10 * n + 3,)),
        pltpu.SemaphoreType.DMA((10 * n + 3,)),
    ]
    more = {} if alone else {"collective_id": 0, "has_side_effects": True}
    return pl.pallas_call(
        functools.partial(backward_kernel, alone),
        in_specs=[pl.BlockSpec(memory_space=pl.ANY)] * len(operands),
        out_specs=[pl.BlockSpec(memory_space=pltpu.VMEM)] * 3,
        out_shape=[
            jax.ShapeDtypeStruct((hists, seq, width), BF),
            jax.ShapeDtypeStruct((SIDE, 4 * width), F32),
            jax.ShapeDtypeStruct((SIDE, width), F32),
        ],
        scratch_shapes=scratch,
        compiler_params=pltpu.CompilerParams(vmem_limit_bytes=VMEM_LIMIT, **more),
        cost_estimate=pl.CostEstimate(flops=16_000_000_000, bytes_accessed=18_000_000, transcendentals=2_000_000),
        name="layer_backward",
    )(*operands)


def target(facts, recv, encoded, slots):
    hists, seq, width = encoded.shape
    vmem = pl.BlockSpec(memory_space=pltpu.VMEM)
    return pl.pallas_call(
        target_kernel,
        in_specs=[vmem] * 3,
        out_shape=[
            jax.ShapeDtypeStruct((slots, width), BF),
            jax.ShapeDtypeStruct((hists, seq, width), BF),
        ],
        scratch_shapes=[pltpu.VMEM((slots, width), F32)],
        compiler_params=pltpu.CompilerParams(vmem_limit_bytes=VMEM_LIMIT),
        cost_estimate=pl.CostEstimate(flops=8_000_000_000, bytes_accessed=4_000_000, transcendentals=4_000_000),
        name="target_backward",
    )(facts, recv, encoded)


def unpack(capacity, owner_ids, returned, rows):
    return pl.pallas_call(
        functools.partial(unpack_kernel, capacity),
        out_shape=jax.ShapeDtypeStruct((rows, returned.shape[1]), BF),
        compiler_params=pltpu.CompilerParams(vmem_limit_bytes=VMEM_LIMIT),
        name="unpack_grads",
    )(owner_ids, returned)


def exchange(x, devices):
    rows, width = x.shape
    got = lax.all_to_all(
        x.reshape(devices, rows // devices, width), AXES, split_axis=0, concat_axis=0, tiled=True
    )
    return got


def local(histories, weight_in, weight_out, candidates, cotangent, owner_ids, hist_slot, lengths):
    devices = lax.axis_size(AXES)
    imp_rows, width = candidates.shape
    capacity = max(2, 2 * imp_rows // devices)
    slots = devices * capacity
    routing = [r.reshape(1, imp_rows) for r in (owner_ids, hist_slot, lengths)]
    facts, recv, encoded, *saved = forward(
        histories, weight_in, weight_out, routing, candidates, cotangent, devices, capacity
    )
    d_query, d_encoded = target(facts, recv, encoded, slots)
    returned = exchange(d_query, devices).reshape(slots, width)
    history_grad, in_grad, out_grad = backward(histories, weight_in, weight_out, saved, d_encoded)
    candidate_grad = unpack(capacity, routing[0], returned, imp_rows)
    return history_grad, candidate_grad, in_grad, out_grad


def solution(mesh):
    return jax.shard_map(
        local,
        mesh=mesh,
        in_specs=(
            P(AXES, None, None),
            P(),
            P(),
            P(AXES, None),
            P(AXES, None),
            P(AXES, None),
            P(AXES),
            P(AXES),
        ),
        out_specs=(P(AXES, None, None), P(AXES, None), P(AXES, None), P(AXES, None)),
        check_vma=False,
    )
```

```python
import functools

import jax
import jax.numpy as jnp
from jax import lax
from jax.experimental import pallas as pl
from jax.experimental.pallas import tpu as pltpu
from jax.sharding import PartitionSpec as P

HEADS = 8
HEAD_DIM = 64
PAIR = 128
EPS = 1e-05
BF = jnp.bfloat16
F32 = jnp.float32
AXES = ("hash", "dp")
VMEM_LIMIT = 60 * 1024 * 1024
MESH = pl.DeviceIdType.MESH
SIDE = 4
ORDERS = ("xyz", "yzx", "zxy")
GROUPS = 5
TILE = 128
PLAN = (
    (((0, 0),), 1),
    (((1, 0),), 2),
    (((0, 1), (2, 0)), 3),
    (((1, 1), (0, 2)), 4),
)
DIMS = "lyxh"


def dot_nn(a, b):
    return lax.dot_general(a, b, (((1,), (0,)), ((), ())), preferred_element_type=F32)


def dot_nt(a, b):
    return lax.dot_general(a, b, (((1,), (1,)), ((), ())), preferred_element_type=F32)


def dot_tn(a, b):
    return lax.dot_general(a, b, (((0,), (0,)), ((), ())), preferred_element_type=F32)


def iota(shape, dim):
    return lax.broadcasted_iota(jnp.int32, shape, dim)


def silu_parts(half):
    t = jnp.tanh(half)
    plus = 1.0 + t
    return half * plus, plus * (1.0 + half * (1.0 - t))


def head_rows(scale):
    lanes = iota((1, PAIR), 1)
    first = jnp.where(lanes < HEAD_DIM, scale, 0.0).astype(BF)
    second = jnp.where(lanes < HEAD_DIM, 0.0, scale).astype(BF)
    return first, second


def lower_half(shape):
    return iota(shape, 1) < SIDE


def turn(x):
    return pltpu.roll(x, SIDE, 1)


def chunk_at(device, devices):
    return device % 2 * (devices // 2) + device // 2


def four_blocks(value):
    rows = value.shape[0]
    v = value.reshape(rows // 8, 8, 4 * PAIR)
    low = lower_half((rows // 8, 8, PAIR))
    even, odd = [], []
    for g in (0, 2):
        first, second = v[:, :, g * PAIR : (g + 1) * PAIR], v[:, :, (g + 1) * PAIR : (g + 2) * PAIR]
        even.append(jnp.where(low, first, turn(second)))
        odd.append(jnp.where(low, turn(first), second))
    return [jnp.concatenate(half, axis=1).astype(BF) for half in (even, odd)]


def to_chunks(ref, value):
    half = value.shape[0] // 8
    for pos in range(0, value.shape[1] // PAIR, 4):
        even, odd = four_blocks(value[:, pos * PAIR : (pos + 4) * PAIR])
        ref[:half, pos * SIDE : (pos + 4) * SIDE, :] = even
        ref[half:, pos * SIDE : (pos + 4) * SIDE, :] = odd


def from_chunks(ref, block):
    half = ref.shape[0] // (2 if len(ref.shape) == 3 else 1)
    low = lower_half((half, 8, PAIR))
    at = block // 2 * 8
    tile = at // 16 * 16
    if len(ref.shape) == 4:
        first, second = ref[:, 0, tile : tile + 16, :], ref[:, 1, tile : tile + 16, :]
    else:
        first, second = ref[:half, tile : tile + 16, :], ref[half:, tile : tile + 16, :]
    first = first.astype(F32)[:, at - tile : at - tile + 8]
    second = second.astype(F32)[:, at - tile : at - tile + 8]
    if block % 2 == 0:
        rows = jnp.where(low, first, turn(second))
    else:
        rows = jnp.where(low, turn(first), second)
    return rows.reshape(half * 8, PAIR).astype(BF)


def as_column(row):
    rows = row.shape[1]
    same = iota((rows, rows), 0) == iota((rows, rows), 1)
    return jnp.sum(jnp.where(same, row, 0), axis=1, keepdims=True)


def slot_of(owner_row):
    rows = owner_row.shape[1]
    i, j = iota((rows, rows), 0), iota((rows, rows), 1)
    owner_col = as_column(owner_row)
    same = owner_col == owner_row
    place_col = jnp.sum(jnp.where(same & (j < i), 1, 0), axis=1, keepdims=True)
    place_row = jnp.sum(jnp.where(same & (i < j), 1, 0), axis=0, keepdims=True)
    return owner_col, place_col, owner_row, place_row


def finish_kernel(capacity, owner_ref, ret_ref, hist_ref, in_ref, out_ref, cand_o, hist_o, in_o, out_o, slots_s, sem):
    passed = pltpu.make_async_copy(hist_ref, hist_o, sem)
    passed.start()
    in_o[...] = in_ref[...]
    out_o[...] = out_ref[...]
    rows, width = cand_o.shape
    slots = slots_s.shape[0]
    owner_col, place_col, _, _ = slot_of(owner_ref[...])
    target_col = owner_col * capacity + place_col
    chosen = jnp.where(iota((rows, slots), 1) == target_col, 1.0, 0.0).astype(BF)
    for block in range(width // PAIR):
        slots_s[:, block * PAIR : (block + 1) * PAIR] = from_chunks(ret_ref, block)
    cand_o[...] = dot_nn(chosen, slots_s[...]).astype(BF)
    passed.wait()


def place():
    hash_i, dp_i = lax.axis_index("hash"), lax.axis_index("dp")
    return {"y": hash_i // 2, "core": hash_i % 2, "x": dp_i // SIDE, "z": dp_i % SIDE}


def device_at(at):
    return (at["y"] * 2 + at["core"], at["x"] * SIDE + at["z"])


def partner(me, axis, jump):
    size = 2 if axis == "core" else SIDE
    at = dict(me)
    at[axis] = (me[axis] + jump) % size
    return at


def partners(me):
    return [partner(me, "core", 1)] + [partner(me, a, j) for a in "xyz" for j in (1, 2, 3)]


def facts_by_owner(owner_row, place_row, slot_row, length_row, devices, capacity):
    rows = owner_row.shape[1]
    slot, length = as_column(slot_row), as_column(length_row)
    lane = iota((rows, PAIR), 1)
    total = jnp.zeros((devices, PAIR), F32)
    for p in range(capacity):
        chosen = (iota((devices, rows), 0) == owner_row) & (place_row == p)
        value = jnp.where(lane == p, slot, jnp.where(lane == capacity + p, length, 0))
        total += dot_nn(jnp.where(chosen, 1.0, 0.0).astype(BF), value.astype(F32).astype(BF))
    return total


def received(facts, shape):
    devices, slots = facts.shape[0], shape[1]
    capacity = slots // devices
    lane, source = iota((devices, slots), 1), iota((devices, slots), 0)
    rows = []
    for first in (0, capacity):
        total = jnp.zeros((devices, slots), F32)
        for p in range(capacity):
            total = jnp.where(lane == source * capacity + p, facts[:, first + p : first + p + 1], total)
        rows.append(jnp.sum(total, axis=0, keepdims=True))
    return jnp.where(iota(shape, 0) == 0, rows[0], rows[1])


def forward_kernel(
    alone, capacity,
    owner_ref, slot_ref, length_ref, cand_ref, cot_ref, x_hbm, win_hbm, wout_hbm,
    facts_ref, recv_hbm, enc_hbm, sg_hbm, gate_hbm, vqk_hbm, nrm_hbm, inv_hbm,
    x_s, win_s, wout_s, load, send_s, enc_s, sg_s, gate_s, vqk_s, nrm_s, inv_s, save, mix_s, send, recv, own, tell_s, told_s, tell, told,
):
    hists, seq, width = x_s.shape
    rows = cand_ref.shape[0]
    loads = [
        pltpu.make_async_copy(a, b, load.at[i])
        for i, (a, b) in enumerate(((x_hbm, x_s), (win_hbm, win_s), (wout_hbm, wout_s)))
    ]
    for c in loads:
        c.start()
    devices = send_s.shape[0]
    if not alone:
        hash_i, dp_i = lax.axis_index("hash"), lax.axis_index("dp")
        ring = lax.axis_size("dp")
        me = hash_i * ring + dp_i
        barrier = pltpu.get_barrier_semaphore()

        def greet(jump, carry):
            to = lax.rem(me + jump, devices)
            pl.semaphore_signal(barrier, inc=1, device_id=(to // ring, to % ring), device_id_type=MESH)
            return carry

        lax.fori_loop(1, devices, greet, 0)
    _, _, owner_row, place_row = slot_of(owner_ref[...])
    slots = devices * capacity
    chosen = jnp.where(iota((slots, rows), 0) == owner_row * capacity + place_row, 1.0, 0.0).astype(BF)
    facts = facts_by_owner(owner_row, place_row, slot_ref[...], length_ref[...], devices, capacity)
    tell_s[...] = facts.reshape(devices, 1, PAIR)
    sent_rows = width // PAIR * SIDE
    for i, value in enumerate((cand_ref[...], cot_ref[...])):
        to_chunks(send_s.at[:, i * sent_rows : (i + 1) * sent_rows], dot_nn(chosen, value))
    if not alone:
        pl.semaphore_wait(barrier, devices - 1)

        def push(jump, carry):
            to = lax.rem(me + lax.rem(jump * 37, devices), devices)
            pltpu.make_async_remote_copy(
                src_ref=send_s.at[chunk_at(to, devices)], dst_ref=recv_hbm.at[chunk_at(me, devices)],
                send_sem=send, recv_sem=recv, device_id=(to // ring, to % ring), device_id_type=MESH,
            ).start()
            pltpu.make_async_remote_copy(
                src_ref=tell_s.at[to], dst_ref=told_s.at[me],
                send_sem=tell, recv_sem=told, device_id=(to // ring, to % ring), device_id_type=MESH,
            ).start()
            return carry

        lax.fori_loop(1, devices, push, 0)
        keep = pltpu.make_async_copy(send_s.at[chunk_at(me, devices)], recv_hbm.at[chunk_at(me, devices)], own)
        keep.start()
        told_s[me] = tell_s[me]
    for c in loads:
        c.wait()
    cut = seq // 2
    seen = iota((cut, seq), 0) + cut >= iota((cut, seq), 1)
    half_scale = head_rows(0.5 * HEAD_DIM**-0.5)
    inv_seq = head_rows(1.0 / seq)
    outs = ((enc_s, enc_hbm), (sg_s, sg_hbm), (gate_s, gate_hbm), (vqk_s, vqk_hbm), (nrm_s, nrm_hbm), (inv_s, inv_hbm))

    def saves(h):
        return [pltpu.make_async_copy(a.at[h], b.at[h], save.at[i, h]) for i, (a, b) in enumerate(outs)]

    def one(hist, carry):
        x = x_s[hist]
        xh = x * 0.5
        for part in range(4):
            cols = slice(part * width, (part + 1) * width)
            act, grad2 = silu_parts(dot_nn(xh, win_s[:, cols]))
            sg_s[hist, :, cols] = (0.5 * grad2).astype(BF)
            if part == 0:
                gate_s[hist] = act.astype(BF)
            else:
                vqk_s[hist, :, (part - 1) * width : part * width] = act.astype(BF)
        for pair in range(width // PAIR):
            lanes = [slice(b * width + pair * PAIR, b * width + (pair + 1) * PAIR) for b in range(3)]
            v = vqk_s[hist, :, lanes[0]]
            q = vqk_s[hist, :, lanes[1]]
            k = vqk_s[hist, :, lanes[2]]
            total = None
            for h in range(2):
                qs, vs = q * half_scale[h], v * inv_seq[h]
                half = dot_nt(qs[:cut], k[:cut])
                first = jnp.where(seen[:, cut:], half * (1.0 + jnp.tanh(half)), 0.0).astype(BF)
                half = dot_nt(qs[cut:], k)
                second = jnp.where(seen, half * (1.0 + jnp.tanh(half)), 0.0).astype(BF)
                terms = (dot_nn(first, vs[:cut]), dot_nn(second, vs))
                total = terms if total is None else [a + b for a, b in zip(total, terms)]
            mix_s[:cut, lanes[0]] = total[0]
            mix_s[cut:, lanes[0]] = total[1]
        mixed = mix_s[...]
        centred = mixed - jnp.mean(mixed, axis=1, keepdims=True)
        inv = lax.rsqrt(jnp.mean(centred * centred, axis=1, keepdims=True) + EPS)
        normed = centred * inv
        nrm_s[hist] = normed.astype(BF)
        inv_s[hist] = jnp.broadcast_to(inv, (seq, PAIR))
        merged = (normed * gate_s[hist].astype(F32)).astype(BF)
        enc_s[hist] = (x.astype(F32) + dot_nn(merged, wout_s[...])).astype(BF)
        for c in saves(hist):
            c.start()
        return carry

    lax.fori_loop(0, hists, one, 0)
    for h in range(hists):
        for c in saves(h):
            c.wait()
    if not alone:
        keep.wait()
        all_but_one = pl.ds(0, devices - 1)
        pltpu.make_async_remote_copy(
            src_ref=send_s.at[all_but_one], dst_ref=recv_hbm.at[all_but_one], send_sem=send, recv_sem=recv,
            device_id=(lax.rem(hash_i + 1, devices // ring), dp_i), device_id_type=MESH,
        ).wait()
        pltpu.make_async_remote_copy(
            src_ref=tell_s.at[all_but_one], dst_ref=told_s.at[all_but_one], send_sem=tell, recv_sem=told,
            device_id=(lax.rem(hash_i + 1, devices // ring), dp_i), device_id_type=MESH,
        ).wait()
        facts_ref[...] = received(told_s[...].reshape(devices, PAIR), facts_ref.shape)


def without(dims, axis):
    return "".join(d for d in dims if d not in ("lh" if axis == "z" else axis))


def shape_of(dims):
    return tuple(2 if d in "lh" else SIDE for d in dims)


def along(ref, dims, axis, at):
    index = {"x": at["x"], "y": at["y"], "l": at["z"] % 2, "h": at["z"] // 2}
    gone = "lh" if axis == "z" else axis
    return ref.at[tuple(index[d] if d in gone else slice(None) for d in dims)]


class Reduction:
    def __init__(self, parts, first, staged, direct, sums, sems, direct_sems):
        self.me = place()
        self.parts, self.staged, self.direct, self.sums = parts, staged, direct, sums
        self.got0, self.pair = first
        self.send, self.recv = sems
        self.push_sem, self.land_sem = direct_sems

    def greet(self):
        barrier = pltpu.get_barrier_semaphore()
        me = self.me
        pl.semaphore_signal(
            barrier, inc=1, device_id=device_at(partner(me, "core", 1)), device_id_type=MESH
        )

        def one(jump, carry):
            pl.semaphore_signal(barrier, inc=1, device_id=device_at(self.chip(jump)), device_id_type=MESH)
            return carry

        lax.fori_loop(1, SIDE**3, one, 0)

    def enter(self):
        pl.semaphore_wait(pltpu.get_barrier_semaphore(), SIDE**3)

    def chip(self, jump):
        me = self.me
        q = lax.rem((me["y"] * SIDE + me["x"]) * SIDE + me["z"] + jump, SIDE**3)
        return {"y": q // SIDE**2, "x": q // SIDE % SIDE, "z": q % SIDE, "core": me["core"]}

    def copy(self, src, dst, number, other):
        return pltpu.make_async_remote_copy(
            src_ref=src, dst_ref=dst, send_sem=self.send.at[number], recv_sem=self.recv.at[number],
            device_id=device_at(other), device_id_type=MESH,
        )

    def dims(self, t, stage):
        dims = DIMS
        for axis in ORDERS[t][: stage - 1]:
            dims = without(dims, axis)
        return dims

    def copies(self, t, stage):
        if stage == 0:
            mate = partner(self.me, "core", 1)
            return [self.copy(self.parts.at[t, :, :, mate["core"]], self.got0.at[t], t, mate)]
        axis, dims = ORDERS[t][stage - 1], self.dims(t, stage)
        src = self.pair.at[t] if stage == 1 else self.staged[t][stage - 2][0]
        out = []
        for j in (1, 2, 3):
            other = partner(self.me, axis, j)
            number = GROUPS + t * 9 + 3 * (stage - 1) + j - 1
            dst = self.staged[t][stage - 1][1].at[j - 1]
            out.append(self.copy(along(src, dims, axis, other), dst, number, other))
        return out

    def start(self, t, stage):
        for c in self.copies(t, stage):
            c.start()

    def finish(self, t, stage):
        for c in self.copies(t, stage):
            c.wait_recv()
        if stage == 0:
            total = self.parts[t, :, :, self.me["core"]].astype(F32) + self.got0[t].astype(F32)
            self.pair[t] = total.astype(BF)
            return
        axis, dims = ORDERS[t][stage - 1], self.dims(t, stage)
        src = self.pair.at[t] if stage == 1 else self.staged[t][stage - 2][0]
        total = along(src, dims, axis, self.me)[...].astype(F32)
        for j in range(3):
            total = total + self.staged[t][stage - 1][1][j].astype(F32)
        if stage < 3:
            self.staged[t][stage - 1][0][...] = total.astype(BF)
        else:
            self.sums[t] = total

    def advance(self, t, stage):
        self.finish(t, stage)
        self.start(t, stage + 1)

    def push(self, t):
        d = t - len(ORDERS)

        def one(jump, carry):
            to = self.chip(jump)
            pltpu.make_async_remote_copy(
                src_ref=self.pair.at[t, to["z"] % 2, to["y"], to["x"], to["z"] // 2],
                dst_ref=self.direct.at[d, jump - 1],
                send_sem=self.push_sem.at[d], recv_sem=self.land_sem.at[d],
                device_id=device_at(to), device_id_type=MESH,
            ).start()
            return carry

        lax.fori_loop(1, SIDE**3, one, 0)

    def land(self, t):
        d = t - len(ORDERS)
        every = self.direct.at[d]
        pltpu.make_async_remote_copy(
            src_ref=every, dst_ref=every, send_sem=self.push_sem.at[d], recv_sem=self.land_sem.at[d],
            device_id=device_at(self.chip(1)), device_id_type=MESH,
        ).wait()
        me = self.me
        own = self.pair[t, me["z"] % 2, me["y"], me["x"], me["z"] // 2].astype(F32)
        self.sums[t] = own + jnp.sum(self.direct[d].astype(F32), axis=0)

    def end(self, win_ref, wout_ref):
        width = wout_ref.shape[1]
        for block in range(SIDE):
            rows = slice(block * SIDE, (block + 1) * SIDE)
            wout_ref[:, block * PAIR : (block + 1) * PAIR] = self.sums[0, rows]
            for pair in range(GROUPS - 1):
                at = (block + 1) % SIDE * width + pair * PAIR
                win_ref[:, at : at + PAIR] = self.sums[1 + pair, rows]
        for t in range(GROUPS):
            for stage in range(4 if t < len(ORDERS) else 1):
                for c in self.copies(t, stage):
                    c.wait_send()


class Nothing:
    def __getattr__(self, name):
        return lambda *args: None


def backward_kernel(
    alone,
    x_hbm, win_hbm, wout_hbm, sg_hbm, gate_hbm, vqk_hbm, nrm_hbm, inv_hbm, denc_hbm,
    hg_ref, gin_ref, gout_ref,
    x_s, win_s, wout_s, sg_s, gate_s, vqk_s, nrm_s, inv_s, denc_s, load,
    xt_s, mg_s, dp_s, dm_s, parts_s, got0, pair_s, direct, sums, send, recv, push, land, *stages,
):
    hists, seq, width = hg_ref.shape
    sources = (denc_hbm, wout_hbm, nrm_hbm, gate_hbm, inv_hbm, sg_hbm, x_hbm, vqk_hbm, win_hbm)
    places = (denc_s, wout_s, nrm_s, gate_s, inv_s, sg_s, x_s, vqk_s, win_s)
    loads = [pltpu.make_async_copy(a, b, load.at[i]) for i, (a, b) in enumerate(zip(sources, places))]
    for c in loads:
        c.start()
    staged = [
        [tuple(stages[6 * t + 2 * i : 6 * t + 2 * i + 2]) for i in range(3)] for t in range(len(ORDERS))
    ]
    comm = Nothing()
    if not alone:
        comm = Reduction(parts_s, (got0, pair_s), staged, direct, sums, (send, recv), (push, land))
    comm.greet()

    def rows_of(h):
        return pl.ds(pl.multiple_of(h * seq, seq), seq)

    def store_part(t, value):
        for i, half in enumerate(four_blocks(value)):
            parts_s[t, i] = half.reshape(parts_s.shape[2:])

    for c in loads[:7]:
        c.wait()

    def gate_step(h, carry):
        rows = rows_of(h)
        normed = nrm_s[h].astype(F32)
        gate = gate_s[h].astype(F32)
        mg_s[rows, :] = (normed * gate).astype(BF)
        d_merged = dot_nt(denc_s[h], wout_s[...])
        dp_s[rows, :width] = (d_merged * normed * sg_s[h, :, :width].astype(F32)).astype(BF)
        d_norm = d_merged * gate
        m1 = jnp.mean(d_norm, axis=1, keepdims=True)
        m2 = jnp.mean(d_norm * normed, axis=1, keepdims=True)
        dm_s[rows, :] = (inv_s[h][:, :1] * (d_norm - m1 - normed * m2)).astype(BF)
        xt_s[:, rows] = x_s[h].T
        return carry

    lax.fori_loop(0, hists, gate_step, 0)
    store_part(0, dot_tn(mg_s[...], denc_s[...].reshape(hists * seq, width)))
    comm.enter()
    comm.start(0, 0)
    loads[7].wait()

    cut = seq // 2
    seen = iota((cut, seq), 0) <= iota((cut, seq), 1)
    half_scale = head_rows(0.5 * HEAD_DIM**-0.5)
    one = head_rows(1.0)
    scales = (1.0 / seq, 0.5 * HEAD_DIM**-0.5 / seq, 1.0 / seq)

    def attn_step(pair, carry):
        lanes = [pl.ds(pl.multiple_of(b * width + pair * PAIR, PAIR), PAIR) for b in range(4)]
        for h in range(hists):
            v, q, k = (vqk_s[h, :, lanes[b]] for b in range(3))
            dm = dm_s[h * seq : (h + 1) * seq, lanes[0]]
            sums_ = [None] * 6
            for head in range(2):
                qs, dms, ks = q * half_scale[head], dm * one[head], k * one[head]
                act, grad2 = silu_parts(dot_nt(k[:cut], qs))
                a0 = jnp.where(seen, act, 0.0).astype(BF)
                s0 = jnp.where(seen, dot_nt(v[:cut], dms) * grad2, 0.0).astype(BF)
                act, grad2 = silu_parts(dot_nt(k[cut:], qs[cut:]))
                a1 = jnp.where(seen[:, :cut], act, 0.0).astype(BF)
                s1 = jnp.where(seen[:, :cut], dot_nt(v[cut:], dms[cut:]) * grad2, 0.0).astype(BF)
                terms = (
                    dot_nn(a0, dms), dot_nn(a1, dms[cut:]),
                    dot_tn(s0[:, :cut], ks[:cut]), dot_tn(jnp.concatenate([s0[:, cut:], s1], axis=0), ks),
                    dot_nn(s0, qs), dot_nn(s1, qs[cut:]),
                )
                sums_ = [t if total is None else total + t for total, t in zip(sums_, terms)]
            for i, value in enumerate(sums_):
                b, part = 1 + i // 2, i % 2
                at = slice(h * seq + part * cut, h * seq + (part + 1) * cut)
                sg = sg_s[h, part * cut : (part + 1) * cut, lanes[b]].astype(F32) * scales[b - 1]
                dp_s[at, lanes[b]] = (value * sg).astype(BF)
        d_pair = jnp.concatenate([dp_s[:, lanes[b]] for b in (1, 2, 3, 0)], axis=1)
        store_part(1 + pair, dot_nn(xt_s[...], d_pair))
        for now, (steps, started) in enumerate(PLAN):
            @pl.when(pair == now)
            def _():
                comm.start(started, 0)
                for t, stage in steps:
                    comm.advance(t, stage)
        return carry

    lax.fori_loop(0, width // PAIR, attn_step, 0)
    comm.finish(3, 0)
    comm.push(3)
    loads[8].wait()

    def grads(lo, hi):
        for h in range(lo, hi):
            prod = dot_nt(dp_s[h * seq : (h + 1) * seq, :], win_s[...])
            hg_ref[h] = (denc_s[h].astype(F32) + prod).astype(BF)

    grads(0, hists // 2)
    comm.finish(4, 0)
    comm.push(4)
    comm.advance(2, 1)
    grads(hists // 2, hists)
    comm.advance(1, 2)
    comm.advance(2, 2)
    for t in range(len(ORDERS)):
        comm.finish(t, 3)
    comm.land(3)
    comm.land(4)
    comm.end(gin_ref, gout_ref)


def sort_slots(facts_ref, hists):
    hist_row, len_row = facts_ref[0:1], facts_ref[1:2]
    slots = hist_row.shape[1]
    picked = jnp.where((iota((8, slots), 0).astype(F32) == hist_row) & (len_row > 0.0), 1.0, 0.0)
    before = jnp.where(iota((slots, slots), 0) < iota((slots, slots), 1), 1.0, 0.0).astype(BF)
    rank = dot_nn(picked.astype(BF), before)
    place_row = jnp.full((1, slots), -1.0, F32)
    first, runs = jnp.int32(0), []
    for own in range(hists):
        tiles = (jnp.sum(picked[own : own + 1]).astype(jnp.int32) + (TILE - 1)) // TILE
        here = rank[own : own + 1] + (first * TILE).astype(F32)
        place_row = jnp.where(picked[own : own + 1] > 0.0, here, place_row)
        runs.append((first, first + tiles))
        first = first + tiles
    return place_row, runs


def target_kernel(facts_ref, recv_ref, enc_ref, dq_ref, denc_ref, rows_s, sorted_s, len_s, de_s, dq_s):
    hists, seq, width = enc_ref.shape
    slots = rows_s.shape[0]
    room = sorted_s.shape[0]
    blocks = width // PAIR
    for block in range(2 * blocks):
        rows_s[:, block * PAIR : (block + 1) * PAIR] = from_chunks(recv_ref, block)
    place_row, runs = sort_slots(facts_ref, hists)
    chosen = jnp.where(iota((room, slots), 0).astype(F32) == place_row, 1.0, 0.0).astype(BF)
    for half in range(2):
        cols = slice(half * width, (half + 1) * width)
        sorted_s[:, cols] = dot_nn(chosen, rows_s[:, cols]).astype(BF)
    len_s[...] = dot_nt(facts_ref[...].astype(BF), chosen)
    de_s[...] = jnp.zeros(de_s.shape, F32)
    dq_s[...] = jnp.zeros(dq_s.shape, BF)
    scale = 0.5 * HEAD_DIM**-0.5
    half_scale = head_rows(scale)
    one = head_rows(1.0)
    positions = iota((seq, TILE), 0).astype(F32)
    low = iota((TILE, PAIR), 1) < HEAD_DIM
    for own in range(hists):

        def body(tile, carry):
            at = pl.ds(pl.multiple_of(tile * TILE, TILE), TILE)
            length = len_s[1:2, at]
            weight = jnp.where(positions < length, 1.0 / jnp.maximum(length, 1.0), 0.0)
            weight = jnp.concatenate([weight, weight], axis=1)
            for pair in range(blocks):
                cols = slice(pair * PAIR, (pair + 1) * PAIR)
                enc = enc_ref[own, :, cols]
                q, g = sorted_s[at, cols], sorted_s[at, width + pair * PAIR : width + (pair + 1) * PAIR]
                qq = jnp.concatenate([q * half_scale[0], q * half_scale[1]], axis=0)
                gg = jnp.concatenate([g * one[0], g * one[1]], axis=0)
                act, grad2 = silu_parts(dot_nt(enc, qq))
                a = (act * weight).astype(BF)
                d_s = (dot_nt(enc, gg) * grad2 * weight).astype(BF)
                de_s[own, :, cols] += dot_nn(a, gg) + dot_nn(d_s, qq)
                both = dot_tn(d_s, enc)
                dq_s[at, cols] = (jnp.where(low, both[:TILE], both[TILE:]) * scale).astype(BF)
            return carry

        lax.fori_loop(runs[own][0], runs[own][1], body, 0)
        denc_ref[own] = de_s[own].astype(BF)
    place_col = jnp.transpose(jnp.broadcast_to(place_row, (8, slots)))[:, 0:1]
    back = jnp.where(iota((slots, room), 1).astype(F32) == place_col, 1.0, 0.0).astype(BF)
    for i, half in enumerate(four_blocks(dot_nn(back, dq_s[...]))):
        dq_ref[:, i] = half


def forward(histories, weight_in, weight_out, routing, candidates, cotangent, devices, capacity, alone=False):
    hists, seq, width = histories.shape
    chunk = (devices, 2 * width // PAIR * SIDE, PAIR)
    widths = [(width, BF), (4 * width, BF), (width, BF), (3 * width, BF), (width, BF), (PAIR, F32)]
    kept = [((hists, seq, w), t) for w, t in widths]
    scratch = [pltpu.VMEM(o.shape, o.dtype) for o in (histories, weight_in, weight_out)]
    scratch += [pltpu.SemaphoreType.DMA((3,)), pltpu.VMEM(chunk, BF)]
    scratch += [pltpu.VMEM(*k) for k in kept]
    scratch += [pltpu.SemaphoreType.DMA((len(kept), hists)), pltpu.VMEM((seq, width), F32)]
    scratch += [pltpu.SemaphoreType.DMA] * 3
    scratch += [pltpu.VMEM((devices, 1, PAIR), F32)] * 2 + [pltpu.SemaphoreType.DMA] * 2
    vmem = pl.BlockSpec(memory_space=pltpu.VMEM)
    hbm = pl.BlockSpec(memory_space=pl.ANY)
    return pl.pallas_call(
        functools.partial(forward_kernel, alone, capacity),
        in_specs=[vmem] * 5 + [hbm] * 3,
        out_specs=[vmem] + [hbm] * (1 + len(kept)),
        out_shape=[jax.ShapeDtypeStruct((8, devices * capacity), F32), jax.ShapeDtypeStruct(chunk, BF)] + [jax.ShapeDtypeStruct(*k) for k in kept],
        scratch_shapes=scratch,
        compiler_params=pltpu.CompilerParams(vmem_limit_bytes=VMEM_LIMIT, **({} if alone else {"collective_id": 1, "has_side_effects": True})),
        cost_estimate=pl.CostEstimate(flops=8_000_000_000, bytes_accessed=12_000_000, transcendentals=4_000_000),
        name="route_and_forward",
    )(*routing, candidates, cotangent, histories, weight_in, weight_out)


def backward(histories, weight_in, weight_out, saved, d_enc, alone=False):
    hists, seq, width = histories.shape
    total = hists * seq
    sg, gate, vqk, normed, inv = saved
    operands = (histories, weight_in, weight_out, sg, gate, vqk, normed, inv, d_enc)
    tile = (SIDE * SIDE, PAIR)
    scratch = [pltpu.VMEM(o.shape, o.dtype) for o in operands]
    scratch += [
        pltpu.SemaphoreType.DMA((len(operands),)),
        pltpu.VMEM((width, total), BF),
        pltpu.VMEM((total, width), BF),
        pltpu.VMEM((total, 4 * width), BF),
        pltpu.VMEM((total, width), BF),
        pltpu.VMEM((GROUPS, 2, SIDE, 2, SIDE, 2) + tile, BF),
        pltpu.VMEM((GROUPS,) + shape_of(DIMS) + tile, BF),
        pltpu.VMEM((GROUPS,) + shape_of(DIMS) + tile, BF),
        pltpu.VMEM((GROUPS - len(ORDERS), SIDE**3 - 1) + tile, BF),
        pltpu.VMEM((GROUPS,) + tile, F32),
        pltpu.SemaphoreType.DMA((GROUPS + 9 * len(ORDERS),)),
        pltpu.SemaphoreType.DMA((GROUPS + 9 * len(ORDERS),)),
        pltpu.SemaphoreType.DMA((GROUPS - len(ORDERS),)),
        pltpu.SemaphoreType.DMA((GROUPS - len(ORDERS),)),
    ]
    for order in ORDERS:
        dims = DIMS
        for axis in order:
            dims = without(dims, axis)
            scratch += [pltpu.VMEM(shape_of(dims) + tile, BF), pltpu.VMEM((3,) + shape_of(dims) + tile, BF)]
    more = {} if alone else {"collective_id": 0, "has_side_effects": True}
    return pl.pallas_call(
        functools.partial(backward_kernel, alone),
        in_specs=[pl.BlockSpec(memory_space=pl.ANY)] * len(operands),
        out_specs=[pl.BlockSpec(memory_space=pltpu.VMEM)] * 3,
        out_shape=[
            jax.ShapeDtypeStruct((hists, seq, width), BF),
            jax.ShapeDtypeStruct((SIDE, 4 * width), F32),
            jax.ShapeDtypeStruct((SIDE, width), F32),
        ],
        scratch_shapes=scratch,
        compiler_params=pltpu.CompilerParams(vmem_limit_bytes=VMEM_LIMIT, **more),
        cost_estimate=pl.CostEstimate(flops=16_000_000_000, bytes_accessed=18_000_000, transcendentals=2_000_000),
        name="layer_backward",
    )(*operands)


def target(facts, recv, encoded, slots):
    hists, seq, width = encoded.shape
    room = (slots // TILE + hists - 1) * TILE
    vmem = pl.BlockSpec(memory_space=pltpu.VMEM)
    return pl.pallas_call(
        target_kernel,
        in_specs=[vmem] * 3,
        out_shape=[
            jax.ShapeDtypeStruct((slots // 8, 2, SIDE * SIDE, PAIR), BF),
            jax.ShapeDtypeStruct((hists, seq, width), BF),
        ],
        scratch_shapes=[
            pltpu.VMEM((slots, 2 * width), BF),
            pltpu.VMEM((room, 2 * width), BF),
            pltpu.VMEM((8, room), F32),
            pltpu.VMEM((hists, seq, width), F32),
            pltpu.VMEM((room, width), BF),
        ],
        compiler_params=pltpu.CompilerParams(vmem_limit_bytes=VMEM_LIMIT),
        cost_estimate=pl.CostEstimate(flops=8_000_000_000, bytes_accessed=4_000_000, transcendentals=4_000_000),
        name="target_backward",
    )(facts, recv, encoded)


def finish(capacity, owner_row, returned, history_grad, in_grad, out_grad):
    rows = owner_row.shape[1]
    slots = returned.shape[0] * 8
    width = history_grad.shape[2]
    vmem = pl.BlockSpec(memory_space=pltpu.VMEM)
    hbm = pl.BlockSpec(memory_space=pl.ANY)
    others = (history_grad, in_grad, out_grad)
    return pl.pallas_call(
        functools.partial(finish_kernel, capacity),
        in_specs=[vmem, vmem, hbm, vmem, vmem],
        out_specs=[vmem] * 4,
        out_shape=[jax.ShapeDtypeStruct((rows, width), BF)] + [jax.ShapeDtypeStruct(o.shape, o.dtype) for o in others],
        scratch_shapes=[pltpu.VMEM((slots, width), BF), pltpu.SemaphoreType.DMA],
        compiler_params=pltpu.CompilerParams(vmem_limit_bytes=VMEM_LIMIT),
        name="finish",
    )(owner_row, returned, *others)


def local(histories, weight_in, weight_out, candidates, cotangent, owner_ids, hist_slot, lengths):
    devices = lax.axis_size(AXES)
    imp_rows, width = candidates.shape
    capacity = max(2, 2 * imp_rows // devices)
    slots = devices * capacity
    routing = [r.reshape(1, imp_rows) for r in (owner_ids, hist_slot, lengths)]
    facts, recv, encoded, *saved = forward(
        histories, weight_in, weight_out, routing, candidates, cotangent, devices, capacity
    )
    d_query, d_encoded = target(facts, recv, encoded, slots)
    returned = lax.all_to_all(
        d_query.reshape(devices, SIDE * SIDE, PAIR), AXES, split_axis=0, concat_axis=0, tiled=True
    ).reshape(d_query.shape)
    history_grad, in_grad, out_grad = backward(histories, weight_in, weight_out, saved, d_encoded)
    candidate_grad, history_grad, in_grad, out_grad = finish(
        capacity, routing[0], returned, history_grad, in_grad, out_grad
    )
    return history_grad, candidate_grad, in_grad, out_grad


def solution(mesh):
    return jax.shard_map(
        local,
        mesh=mesh,
        in_specs=(
            P(AXES, None, None),
            P(),
            P(),
            P(AXES, None),
            P(AXES, None),
            P(AXES, None),
            P(AXES),
            P(AXES),
        ),
        out_specs=(P(AXES, None, None), P(AXES, None), P(AXES, None), P(AXES, None)),
        check_vma=False,
    )
```

```python
import functools

import jax
import jax.numpy as jnp
from jax import lax
from jax.experimental import pallas as pl
from jax.experimental.pallas import tpu as pltpu
from jax.sharding import PartitionSpec as P

HEADS = 8
HEAD_DIM = 64
PAIR = 128
EPS = 1e-05
BF = jnp.bfloat16
F32 = jnp.float32
AXES = ("hash", "dp")
VMEM_LIMIT = 60 * 1024 * 1024
MESH = pl.DeviceIdType.MESH
SIDE = 4
ORDERS = ("xyz", "yzx", "zxy", "xyz")
GROUPS = 5
TILE = 128
PLAN = ((1, (0,), ()), (2, (1,), ()), (3, (2,), (0,)), (4, (3,), (1,)))
DIMS = "lyxh"


def dot_nn(a, b):
    return lax.dot_general(a, b, (((1,), (0,)), ((), ())), preferred_element_type=F32)


def dot_nt(a, b):
    return lax.dot_general(a, b, (((1,), (1,)), ((), ())), preferred_element_type=F32)


def dot_tn(a, b):
    return lax.dot_general(a, b, (((0,), (0,)), ((), ())), preferred_element_type=F32)


def iota(shape, dim):
    return lax.broadcasted_iota(jnp.int32, shape, dim)


def silu_parts(half):
    t = jnp.tanh(half)
    plus = 1.0 + t
    return half * plus, plus * (1.0 + half * (1.0 - t))


def head_rows(scale):
    lanes = iota((1, PAIR), 1)
    first = jnp.where(lanes < HEAD_DIM, scale, 0.0).astype(BF)
    second = jnp.where(lanes < HEAD_DIM, 0.0, scale).astype(BF)
    return first, second


def lower_half(shape):
    return iota(shape, 1) < SIDE


def turn(x):
    return pltpu.roll(x, SIDE, 1)


def chunk_at(device, devices):
    return device % 2 * (devices // 2) + device // 2


def four_blocks(value):
    rows = value.shape[0]
    v = value.reshape(rows // 8, 8, 4 * PAIR)
    low = lower_half((rows // 8, 8, PAIR))
    even, odd = [], []
    for g in (0, 2):
        first, second = v[:, :, g * PAIR : (g + 1) * PAIR], v[:, :, (g + 1) * PAIR : (g + 2) * PAIR]
        even.append(jnp.where(low, first, turn(second)))
        odd.append(jnp.where(low, turn(first), second))
    return [jnp.concatenate(half, axis=1).astype(BF) for half in (even, odd)]


def to_chunks(ref, value):
    half = value.shape[0] // 8
    for pos in range(0, value.shape[1] // PAIR, 4):
        even, odd = four_blocks(value[:, pos * PAIR : (pos + 4) * PAIR])
        ref[:half, pos * SIDE : (pos + 4) * SIDE, :] = even
        ref[half:, pos * SIDE : (pos + 4) * SIDE, :] = odd


def from_chunks(ref, block):
    half = ref.shape[0] // (2 if len(ref.shape) == 3 else 1)
    low = lower_half((half, 8, PAIR))
    at = block // 2 * 8
    tile = at // 16 * 16
    if len(ref.shape) == 4:
        first, second = ref[:, 0, tile : tile + 16, :], ref[:, 1, tile : tile + 16, :]
    else:
        first, second = ref[:half, tile : tile + 16, :], ref[half:, tile : tile + 16, :]
    first = first.astype(F32)[:, at - tile : at - tile + 8]
    second = second.astype(F32)[:, at - tile : at - tile + 8]
    if block % 2 == 0:
        rows = jnp.where(low, first, turn(second))
    else:
        rows = jnp.where(low, turn(first), second)
    return rows.reshape(half * 8, PAIR).astype(BF)


def as_column(row):
    rows = row.shape[1]
    same = iota((rows, rows), 0) == iota((rows, rows), 1)
    return jnp.sum(jnp.where(same, row, 0), axis=1, keepdims=True)


def slot_of(owner_row):
    rows = owner_row.shape[1]
    i, j = iota((rows, rows), 0), iota((rows, rows), 1)
    owner_col = as_column(owner_row)
    same = owner_col == owner_row
    place_col = jnp.sum(jnp.where(same & (j < i), 1, 0), axis=1, keepdims=True)
    place_row = jnp.sum(jnp.where(same & (i < j), 1, 0), axis=0, keepdims=True)
    return owner_col, place_col, owner_row, place_row


def finish_kernel(capacity, owner_ref, ret_ref, hist_ref, in_ref, out_ref, cand_o, hist_o, in_o, out_o, slots_s, sem):
    passed = pltpu.make_async_copy(hist_ref, hist_o, sem)
    passed.start()
    in_o[...] = in_ref[...]
    out_o[...] = out_ref[...]
    rows, width = cand_o.shape
    slots = slots_s.shape[0]
    owner_col, place_col, _, _ = slot_of(owner_ref[...])
    target_col = owner_col * capacity + place_col
    chosen = jnp.where(iota((rows, slots), 1) == target_col, 1.0, 0.0).astype(BF)
    for block in range(width // PAIR):
        slots_s[:, block * PAIR : (block + 1) * PAIR] = from_chunks(ret_ref, block)
    cand_o[...] = dot_nn(chosen, slots_s[...]).astype(BF)
    passed.wait()


def place():
    hash_i, dp_i = lax.axis_index("hash"), lax.axis_index("dp")
    return {"y": hash_i // 2, "core": hash_i % 2, "x": dp_i // SIDE, "z": dp_i % SIDE}


def device_at(at):
    return (at["y"] * 2 + at["core"], at["x"] * SIDE + at["z"])


def partner(me, axis, jump):
    size = 2 if axis == "core" else SIDE
    at = dict(me)
    at[axis] = (me[axis] + jump) % size
    return at


def partners(me):
    return [partner(me, "core", 1)] + [partner(me, a, j) for a in "xyz" for j in (1, 2, 3)]


def facts_by_owner(owner_row, place_row, slot_row, length_row, devices, capacity):
    rows = owner_row.shape[1]
    slot, length = as_column(slot_row), as_column(length_row)
    lane = iota((rows, PAIR), 1)
    total = jnp.zeros((devices, PAIR), F32)
    for p in range(capacity):
        chosen = (iota((devices, rows), 0) == owner_row) & (place_row == p)
        value = jnp.where(lane == p, slot, jnp.where(lane == capacity + p, length, 0))
        total += dot_nn(jnp.where(chosen, 1.0, 0.0).astype(BF), value.astype(F32).astype(BF))
    return total


def received(facts, shape):
    devices, slots = facts.shape[0], shape[1]
    capacity = slots // devices
    lane, source = iota((devices, slots), 1), iota((devices, slots), 0)
    rows = []
    for first in (0, capacity):
        total = jnp.zeros((devices, slots), F32)
        for p in range(capacity):
            total = jnp.where(lane == source * capacity + p, facts[:, first + p : first + p + 1], total)
        rows.append(jnp.sum(total, axis=0, keepdims=True))
    return jnp.where(iota(shape, 0) == 0, rows[0], rows[1])


def forward_kernel(
    alone, capacity,
    owner_ref, slot_ref, length_ref, cand_ref, cot_ref, x_hbm, win_hbm, wout_hbm,
    facts_ref, recv_hbm, enc_hbm, sg_hbm, gate_hbm, vqk_hbm, nrm_hbm, inv_hbm, act_hbm, slope_hbm, xt_hbm,
    x_s, win_s, wout_s, load, send_s, enc_s, sg_s, gate_s, vqk_s, nrm_s, inv_s, act_s, slope_s, xt_s, save, mix_s, send, recv, own, tell_s, told_s, tell, told,
):
    hists, seq, width = x_s.shape
    rows = cand_ref.shape[0]
    loads = [
        pltpu.make_async_copy(a, b, load.at[i])
        for i, (a, b) in enumerate(((x_hbm, x_s), (win_hbm, win_s), (wout_hbm, wout_s)))
    ]
    for c in loads:
        c.start()
    devices = send_s.shape[0]
    if not alone:
        hash_i, dp_i = lax.axis_index("hash"), lax.axis_index("dp")
        ring = lax.axis_size("dp")
        me = hash_i * ring + dp_i
        barrier = pltpu.get_barrier_semaphore()

        def greet(jump, carry):
            to = lax.rem(me + jump, devices)
            pl.semaphore_signal(barrier, inc=1, device_id=(to // ring, to % ring), device_id_type=MESH)
            return carry

        lax.fori_loop(1, devices, greet, 0)
    _, _, owner_row, place_row = slot_of(owner_ref[...])
    slots = devices * capacity
    chosen = jnp.where(iota((slots, rows), 0) == owner_row * capacity + place_row, 1.0, 0.0).astype(BF)
    facts = facts_by_owner(owner_row, place_row, slot_ref[...], length_ref[...], devices, capacity)
    tell_s[...] = facts.reshape(devices, 1, PAIR)
    sent_rows = width // PAIR * SIDE
    for i, value in enumerate((cand_ref[...], cot_ref[...])):
        to_chunks(send_s.at[:, i * sent_rows : (i + 1) * sent_rows], dot_nn(chosen, value))
    if not alone:
        pl.semaphore_wait(barrier, devices - 1)

        def push(jump, carry):
            to = lax.rem(me + lax.rem(jump * 37, devices), devices)
            pltpu.make_async_remote_copy(
                src_ref=send_s.at[chunk_at(to, devices)], dst_ref=recv_hbm.at[chunk_at(me, devices)],
                send_sem=send, recv_sem=recv, device_id=(to // ring, to % ring), device_id_type=MESH,
            ).start()
            pltpu.make_async_remote_copy(
                src_ref=tell_s.at[to], dst_ref=told_s.at[me],
                send_sem=tell, recv_sem=told, device_id=(to // ring, to % ring), device_id_type=MESH,
            ).start()
            return carry

        lax.fori_loop(1, devices, push, 0)
        keep = pltpu.make_async_copy(send_s.at[chunk_at(me, devices)], recv_hbm.at[chunk_at(me, devices)], own)
        keep.start()
        told_s[me] = tell_s[me]
    for c in loads:
        c.wait()
    cut = seq // 2
    seen = iota((cut, seq), 0) <= iota((cut, seq), 1)
    half_scale = head_rows(0.5 * HEAD_DIM**-0.5)
    inv_seq = head_rows(1.0 / seq)
    outs = (
        (enc_s, enc_hbm), (sg_s, sg_hbm), (gate_s, gate_hbm), (vqk_s, vqk_hbm), (nrm_s, nrm_hbm), (inv_s, inv_hbm),
        (act_s, act_hbm), (slope_s, slope_hbm),
    )

    def saves(h):
        return [pltpu.make_async_copy(a.at[h], b.at[h], save.at[i, h]) for i, (a, b) in enumerate(outs)]

    def one(hist, carry):
        x = x_s[hist]
        xh = x * 0.5
        xt_s[:, pl.ds(pl.multiple_of(hist * seq, seq), seq)] = x.T
        for part in range(4):
            cols = slice(part * width, (part + 1) * width)
            act, grad2 = silu_parts(dot_nn(xh, win_s[:, cols]))
            sg_s[hist, :, cols] = (0.5 * grad2).astype(BF)
            if part == 0:
                gate_s[hist] = act.astype(BF)
            else:
                vqk_s[hist, :, (part - 1) * width : part * width] = act.astype(BF)
        for pair in range(width // PAIR):
            lanes = [slice(b * width + pair * PAIR, b * width + (pair + 1) * PAIR) for b in range(3)]
            v = vqk_s[hist, :, lanes[0]]
            q = vqk_s[hist, :, lanes[1]]
            k = vqk_s[hist, :, lanes[2]]
            total = None
            for h in range(2):
                qs, vs = q * half_scale[h], v * inv_seq[h]
                act, grad2 = silu_parts(dot_nt(k[:cut], qs))
                a0 = jnp.where(seen, act, 0.0).astype(BF)
                g0 = jnp.where(seen, grad2, 0.0).astype(BF)
                act, grad2 = silu_parts(dot_nt(k[cut:], qs[cut:]))
                a1 = jnp.where(seen[:, :cut], act, 0.0).astype(BF)
                g1 = jnp.where(seen[:, :cut], grad2, 0.0).astype(BF)
                act_s[hist, 2 * pair + h] = jnp.concatenate([a0, a1], axis=1)
                slope_s[hist, 2 * pair + h] = jnp.concatenate([g0, g1], axis=1)
                later = jnp.concatenate([a0[:, cut:], a1], axis=0)
                terms = (dot_tn(a0[:, :cut], vs[:cut]), dot_tn(later, vs))
                total = terms if total is None else [a + b for a, b in zip(total, terms)]
            mix_s[:cut, lanes[0]] = total[0]
            mix_s[cut:, lanes[0]] = total[1]
        mixed = mix_s[...]
        centred = mixed - jnp.mean(mixed, axis=1, keepdims=True)
        inv = lax.rsqrt(jnp.mean(centred * centred, axis=1, keepdims=True) + EPS)
        normed = centred * inv
        nrm_s[hist] = normed.astype(BF)
        inv_s[hist] = jnp.broadcast_to(inv, (seq, PAIR))
        merged = (normed * gate_s[hist].astype(F32)).astype(BF)
        enc_s[hist] = (x.astype(F32) + dot_nn(merged, wout_s[...])).astype(BF)
        for c in saves(hist):
            c.start()
        return carry

    lax.fori_loop(0, hists, one, 0)
    turned = pltpu.make_async_copy(xt_s, xt_hbm, load.at[0])
    turned.start()
    for h in range(hists):
        for c in saves(h):
            c.wait()
    turned.wait()
    if not alone:
        keep.wait()
        all_but_one = pl.ds(0, devices - 1)
        pltpu.make_async_remote_copy(
            src_ref=send_s.at[all_but_one], dst_ref=recv_hbm.at[all_but_one], send_sem=send, recv_sem=recv,
            device_id=(lax.rem(hash_i + 1, devices // ring), dp_i), device_id_type=MESH,
        ).wait()
        pltpu.make_async_remote_copy(
            src_ref=tell_s.at[all_but_one], dst_ref=told_s.at[all_but_one], send_sem=tell, recv_sem=told,
            device_id=(lax.rem(hash_i + 1, devices // ring), dp_i), device_id_type=MESH,
        ).wait()
        facts_ref[...] = received(told_s[...].reshape(devices, PAIR), facts_ref.shape)


def without(dims, axis):
    return "".join(d for d in dims if d not in ("lh" if axis == "z" else axis))


def shape_of(dims):
    return tuple(2 if d in "lh" else SIDE for d in dims)


def along(ref, dims, axis, at):
    index = {"x": at["x"], "y": at["y"], "l": at["z"] % 2, "h": at["z"] // 2}
    gone = "lh" if axis == "z" else axis
    return ref.at[tuple(index[d] if d in gone else slice(None) for d in dims)]


class Reduction:
    def __init__(self, parts, got0, pair, axis_got, axis_sum, landed, sums, sems, push_sems):
        self.me = place()
        self.parts, self.got0, self.pair = parts, got0, pair
        self.axis_got, self.axis_sum, self.landed, self.sums = axis_got, axis_sum, landed, sums
        self.send, self.recv = sems
        self.push_sem, self.land_sem = push_sems

    def device(self, jump):
        ring = lax.axis_size("dp")
        to = lax.rem(self.index() + jump, lax.axis_size(AXES))
        return (to // ring, to % ring), to

    def index(self):
        return lax.axis_index("hash") * lax.axis_size("dp") + lax.axis_index("dp")

    def greet(self):
        barrier = pltpu.get_barrier_semaphore()

        def one(jump, carry):
            pl.semaphore_signal(barrier, inc=1, device_id=self.device(jump)[0], device_id_type=MESH)
            return carry

        lax.fori_loop(1, lax.axis_size(AXES), one, 0)

    def enter(self):
        pl.semaphore_wait(pltpu.get_barrier_semaphore(), lax.axis_size(AXES) - 1)

    def give_back(self, grads, returned, sems, own):
        me = self.index()

        def one(jump, carry):
            device_id, to = self.device(jump)
            pltpu.make_async_remote_copy(
                src_ref=grads.at[to], dst_ref=returned.at[me], send_sem=sems.at[0], recv_sem=sems.at[1],
                device_id=device_id, device_id_type=MESH,
            ).start()
            return carry

        lax.fori_loop(1, lax.axis_size(AXES), one, 0)
        pltpu.make_async_copy(grads.at[me], returned.at[me], own).start()

    def take_back(self, grads, returned, sems, own):
        me = self.index()
        others = pl.ds(0, lax.axis_size(AXES) - 1)
        pltpu.make_async_remote_copy(
            src_ref=grads.at[others], dst_ref=returned.at[others], send_sem=sems.at[0], recv_sem=sems.at[1],
            device_id=self.device(1)[0], device_id_type=MESH,
        ).wait()
        pltpu.make_async_copy(grads.at[me], returned.at[me], own).wait()

    def chip(self, jump):
        me = self.me
        q = lax.rem((me["y"] * SIDE + me["x"]) * SIDE + me["z"] + jump, SIDE**3)
        return {"y": q // SIDE**2, "x": q // SIDE % SIDE, "z": q % SIDE, "core": me["core"]}

    def copy(self, src, dst, number, other):
        return pltpu.make_async_remote_copy(
            src_ref=src, dst_ref=dst, send_sem=self.send.at[number], recv_sem=self.recv.at[number],
            device_id=device_at(other), device_id_type=MESH,
        )

    def copies(self, t, stage):
        if stage == 0:
            mate = partner(self.me, "core", 1)
            return [self.copy(self.parts.at[t, :, :, mate["core"]], self.got0.at[t], t, mate)]
        out = []
        for j in (1, 2, 3):
            other = partner(self.me, ORDERS[t][0], j)
            src = along(self.pair.at[t], DIMS, ORDERS[t][0], other)
            out.append(self.copy(src, self.axis_got[t].at[j - 1], GROUPS + 3 * t + j - 1, other))
        return out

    def start(self, t, stage):
        for c in self.copies(t, stage):
            c.start()

    def finish(self, t, stage):
        for c in self.copies(t, stage):
            c.wait_recv()
        if stage == 0:
            total = self.parts[t, :, :, self.me["core"]].astype(F32) + self.got0[t].astype(F32)
            self.pair[t] = total.astype(BF)
            return
        total = along(self.pair.at[t], DIMS, ORDERS[t][0], self.me)[...].astype(F32)
        for j in range(3):
            total = total + self.axis_got[t][j].astype(F32)
        self.axis_sum[t][...] = total.astype(BF)

    def advance(self, t, stage):
        self.finish(t, stage)
        if stage == 0 and t < len(ORDERS):
            self.start(t, 1)
        else:
            self.push(t)

    def others(self, t):
        return (SIDE**2 if t < len(ORDERS) else SIDE**3) - 1

    def member(self, t, jump):
        if t == len(ORDERS):
            return self.chip(jump)
        a, b = ORDERS[t][1:]
        q = lax.rem(self.me[a] * SIDE + self.me[b] + jump, SIDE**2)
        return {**self.me, a: q // SIDE, b: q % SIDE}

    def chunk(self, t, at):
        index = {"x": at["x"], "y": at["y"], "l": at["z"] % 2, "h": at["z"] // 2}
        if t == len(ORDERS):
            return self.pair.at[(t,) + tuple(index[d] for d in DIMS)]
        return self.axis_sum[t].at[tuple(index[d] for d in without(DIMS, ORDERS[t][0]))]

    def push(self, t):
        def one(jump, carry):
            to = self.member(t, jump)
            pltpu.make_async_remote_copy(
                src_ref=self.chunk(t, to), dst_ref=self.landed[t].at[jump - 1],
                send_sem=self.push_sem.at[t], recv_sem=self.land_sem.at[t],
                device_id=device_at(to), device_id_type=MESH,
            ).start()
            return carry

        lax.fori_loop(1, self.others(t) + 1, one, 0)

    def land(self, t):
        every = self.landed[t]
        pltpu.make_async_remote_copy(
            src_ref=every, dst_ref=every, send_sem=self.push_sem.at[t], recv_sem=self.land_sem.at[t],
            device_id=device_at(self.member(t, 1)), device_id_type=MESH,
        ).wait()
        own = self.chunk(t, self.me)[...].astype(F32)
        self.sums[t] = own + jnp.sum(every[...].astype(F32), axis=0)

    def end(self, win_ref, wout_ref):
        width = wout_ref.shape[1]
        for block in range(SIDE):
            rows = slice(block * SIDE, (block + 1) * SIDE)
            wout_ref[:, block * PAIR : (block + 1) * PAIR] = self.sums[0, rows]
            for pair in range(GROUPS - 1):
                at = (block + 1) % SIDE * width + pair * PAIR
                win_ref[:, at : at + PAIR] = self.sums[1 + pair, rows]
        for t in range(GROUPS):
            for stage in range(2 if t < len(ORDERS) else 1):
                for c in self.copies(t, stage):
                    c.wait_send()


class Nothing:
    def __getattr__(self, name):
        return lambda *args: None


def backward_kernel(
    alone,
    win_hbm, wout_hbm, sg_hbm, gate_hbm, vqk_hbm, nrm_hbm, inv_hbm, act_hbm, slope_hbm, xt_hbm, denc_hbm, grads_hbm,
    hg_ref, gin_ref, gout_ref, ret_hbm,
    win_s, wout_s, sg_s, gate_s, vqk_s, nrm_s, inv_s, act_s, slope_s, xt_s, denc_s, load, load_pair, back, own,
    mg_s, dp_s, dm_s, parts_s, got0, pair_s, sums, send, recv, push, land, *bufs,
):
    hists, seq, width = hg_ref.shape
    gate_cols, other_cols = pl.ds(0, width), pl.ds(width, 3 * width)
    moves = (
        (denc_hbm, denc_s), (wout_hbm, wout_s), (nrm_hbm, nrm_s), (gate_hbm, gate_s), (inv_hbm, inv_s),
        (sg_hbm.at[:, :, gate_cols], sg_s.at[:, :, gate_cols]),
        (vqk_hbm, vqk_s), (sg_hbm.at[:, :, other_cols], sg_s.at[:, :, other_cols]), (xt_hbm, xt_s), (win_hbm, win_s),
    )
    loads = [pltpu.make_async_copy(a, b, load.at[i]) for i, (a, b) in enumerate(moves)]

    def pair_loads(pair):
        heads = pl.ds(2 * pair, 2)
        return [
            pltpu.make_async_copy(a.at[:, heads], b.at[:, heads], load_pair.at[i, pair])
            for i, (a, b) in enumerate(((act_hbm, act_s), (slope_hbm, slope_s)))
        ]

    for c in loads[:6]:
        c.start()
    n = len(ORDERS)
    comm = Nothing()
    if not alone:
        comm = Reduction(
            parts_s, got0, pair_s, bufs[:n], bufs[n : 2 * n], bufs[2 * n :], sums, (send, recv), (push, land)
        )
    comm.greet()

    def rows_of(h):
        return pl.ds(pl.multiple_of(h * seq, seq), seq)

    def store_part(t, value):
        for i, half in enumerate(four_blocks(value)):
            parts_s[t, i] = half.reshape(parts_s.shape[2:])

    for c in loads[:6]:
        c.wait()
    for c in loads[6:8] + pair_loads(0) + loads[8:9]:
        c.start()
    for pair in range(1, width // PAIR):
        for c in pair_loads(pair):
            c.start()
    loads[9].start()

    def gate_step(h, carry):
        rows = rows_of(h)
        normed = nrm_s[h].astype(F32)
        gate = gate_s[h].astype(F32)
        mg_s[rows, :] = (normed * gate).astype(BF)
        d_merged = dot_nt(denc_s[h], wout_s[...])
        dp_s[rows, :width] = (d_merged * normed * sg_s[h, :, :width].astype(F32)).astype(BF)
        d_norm = d_merged * gate
        m1 = jnp.mean(d_norm, axis=1, keepdims=True)
        m2 = jnp.mean(d_norm * normed, axis=1, keepdims=True)
        dm_s[rows, :] = (inv_s[h][:, :1] * (d_norm - m1 - normed * m2)).astype(BF)
        return carry

    lax.fori_loop(0, hists, gate_step, 0)
    comm.enter()
    comm.give_back(grads_hbm, ret_hbm, back, own)
    store_part(0, dot_tn(mg_s[...], denc_s[...].reshape(hists * seq, width)))
    comm.start(0, 0)
    for c in loads[6:9]:
        c.wait()

    cut = seq // 2
    half_scale = head_rows(0.5 * HEAD_DIM**-0.5)
    one = head_rows(1.0)
    scales = (1.0 / seq, 0.5 * HEAD_DIM**-0.5 / seq, 1.0 / seq)

    def attn_step(pair, carry):
        lanes = [pl.ds(pl.multiple_of(b * width + pair * PAIR, PAIR), PAIR) for b in range(4)]
        for c in pair_loads(pair):
            c.wait()
        for h in range(hists):
            v, q, k = (vqk_s[h, :, lanes[b]] for b in range(3))
            dm = dm_s[h * seq : (h + 1) * seq, lanes[0]]
            sums_ = [None] * 6
            for head in range(2):
                qs, dms, ks = q * half_scale[head], dm * one[head], k * one[head]
                a, g = act_s[h, 2 * pair + head], slope_s[h, 2 * pair + head].astype(F32)
                a0, a1 = a[:, :seq], a[:, seq:]
                s0 = (dot_nt(v[:cut], dms) * g[:, :seq]).astype(BF)
                s1 = (dot_nt(v[cut:], dms[cut:]) * g[:, seq:]).astype(BF)
                terms = (
                    dot_nn(a0, dms), dot_nn(a1, dms[cut:]),
                    dot_tn(s0[:, :cut], ks[:cut]), dot_tn(jnp.concatenate([s0[:, cut:], s1], axis=0), ks),
                    dot_nn(s0, qs), dot_nn(s1, qs[cut:]),
                )
                sums_ = [t if total is None else total + t for total, t in zip(sums_, terms)]
            for i, value in enumerate(sums_):
                b, part = 1 + i // 2, i % 2
                at = slice(h * seq + part * cut, h * seq + (part + 1) * cut)
                sg = sg_s[h, part * cut : (part + 1) * cut, lanes[b]].astype(F32) * scales[b - 1]
                dp_s[at, lanes[b]] = (value * sg).astype(BF)
        d_pair = jnp.concatenate([dp_s[:, lanes[b]] for b in (1, 2, 3, 0)], axis=1)
        store_part(1 + pair, dot_nn(xt_s[...], d_pair))
        for now, (started, paired, summed) in enumerate(PLAN):
            @pl.when(pair == now)
            def _():
                comm.start(started, 0)
                for t in paired:
                    comm.advance(t, 0)
                for t in summed:
                    comm.advance(t, 1)
        return carry

    lax.fori_loop(0, width // PAIR, attn_step, 0)
    loads[9].wait()

    def grads(lo, hi):
        for h in range(lo, hi):
            prod = dot_nt(dp_s[h * seq : (h + 1) * seq, :], win_s[...])
            hg_ref[h] = (denc_s[h].astype(F32) + prod).astype(BF)

    grads(0, hists // 2)
    comm.advance(4, 0)
    comm.advance(2, 1)
    grads(hists // 2, hists)
    comm.advance(3, 1)
    comm.take_back(grads_hbm, ret_hbm, back, own)
    for t in range(GROUPS):
        comm.land(t)
    comm.end(gin_ref, gout_ref)


def sort_slots(facts_ref, hists):
    hist_row, len_row = facts_ref[0:1], facts_ref[1:2]
    slots = hist_row.shape[1]
    picked = jnp.where((iota((8, slots), 0).astype(F32) == hist_row) & (len_row > 0.0), 1.0, 0.0)
    before = jnp.where(iota((slots, slots), 0) < iota((slots, slots), 1), 1.0, 0.0).astype(BF)
    rank = dot_nn(picked.astype(BF), before)
    place_row = jnp.full((1, slots), -1.0, F32)
    first, runs = jnp.int32(0), []
    for own in range(hists):
        tiles = (jnp.sum(picked[own : own + 1]).astype(jnp.int32) + (TILE - 1)) // TILE
        here = rank[own : own + 1] + (first * TILE).astype(F32)
        place_row = jnp.where(picked[own : own + 1] > 0.0, here, place_row)
        runs.append((first, first + tiles))
        first = first + tiles
    return place_row, runs


def target_kernel(facts_ref, recv_ref, enc_ref, dq_ref, denc_ref, rows_s, sorted_s, len_s, de_s, dq_s):
    hists, seq, width = enc_ref.shape
    slots = rows_s.shape[0]
    room = sorted_s.shape[0]
    blocks = width // PAIR
    for block in range(2 * blocks):
        rows_s[:, block * PAIR : (block + 1) * PAIR] = from_chunks(recv_ref, block)
    place_row, runs = sort_slots(facts_ref, hists)
    chosen = jnp.where(iota((room, slots), 0).astype(F32) == place_row, 1.0, 0.0).astype(BF)
    for half in range(2):
        cols = slice(half * width, (half + 1) * width)
        sorted_s[:, cols] = dot_nn(chosen, rows_s[:, cols]).astype(BF)
    len_s[...] = dot_nt(facts_ref[...].astype(BF), chosen)
    de_s[...] = jnp.zeros(de_s.shape, F32)
    dq_s[...] = jnp.zeros(dq_s.shape, BF)
    scale = 0.5 * HEAD_DIM**-0.5
    half_scale = head_rows(scale)
    one = head_rows(1.0)
    positions = iota((seq, TILE), 0).astype(F32)
    low = iota((TILE, PAIR), 1) < HEAD_DIM
    for own in range(hists):

        def body(tile, carry):
            at = pl.ds(pl.multiple_of(tile * TILE, TILE), TILE)
            length = len_s[1:2, at]
            weight = jnp.where(positions < length, 1.0 / jnp.maximum(length, 1.0), 0.0)
            weight = jnp.concatenate([weight, weight], axis=1)
            for pair in range(blocks):
                cols = slice(pair * PAIR, (pair + 1) * PAIR)
                enc = enc_ref[own, :, cols]
                q, g = sorted_s[at, cols], sorted_s[at, width + pair * PAIR : width + (pair + 1) * PAIR]
                qq = jnp.concatenate([q * half_scale[0], q * half_scale[1]], axis=0)
                gg = jnp.concatenate([g * one[0], g * one[1]], axis=0)
                act, grad2 = silu_parts(dot_nt(enc, qq))
                a = (act * weight).astype(BF)
                d_s = (dot_nt(enc, gg) * grad2 * weight).astype(BF)
                de_s[own, :, cols] += dot_nn(a, gg) + dot_nn(d_s, qq)
                both = dot_tn(d_s, enc)
                dq_s[at, cols] = (jnp.where(low, both[:TILE], both[TILE:]) * scale).astype(BF)
            return carry

        lax.fori_loop(runs[own][0], runs[own][1], body, 0)
        denc_ref[own] = de_s[own].astype(BF)
    place_col = jnp.transpose(jnp.broadcast_to(place_row, (8, slots)))[:, 0:1]
    back = jnp.where(iota((slots, room), 1).astype(F32) == place_col, 1.0, 0.0).astype(BF)
    for i, half in enumerate(four_blocks(dot_nn(back, dq_s[...]))):
        dq_ref[:, i] = half


def forward(histories, weight_in, weight_out, routing, candidates, cotangent, devices, capacity, alone=False):
    hists, seq, width = histories.shape
    chunk = (devices, 2 * width // PAIR * SIDE, PAIR)
    widths = [(width, BF), (4 * width, BF), (width, BF), (3 * width, BF), (width, BF), (PAIR, F32)]
    kept = [((hists, seq, w), t) for w, t in widths]
    kept += [((hists, HEADS, seq // 2, seq // 2 * 3), BF)] * 2 + [((width, hists * seq), BF)]
    scratch = [pltpu.VMEM(o.shape, o.dtype) for o in (histories, weight_in, weight_out)]
    scratch += [pltpu.SemaphoreType.DMA((3,)), pltpu.VMEM(chunk, BF)]
    scratch += [pltpu.VMEM(*k) for k in kept]
    scratch += [pltpu.SemaphoreType.DMA((len(kept) - 1, hists)), pltpu.VMEM((seq, width), F32)]
    scratch += [pltpu.SemaphoreType.DMA] * 3
    scratch += [pltpu.VMEM((devices, 1, PAIR), F32)] * 2 + [pltpu.SemaphoreType.DMA] * 2
    vmem = pl.BlockSpec(memory_space=pltpu.VMEM)
    hbm = pl.BlockSpec(memory_space=pl.ANY)
    return pl.pallas_call(
        functools.partial(forward_kernel, alone, capacity),
        in_specs=[vmem] * 5 + [hbm] * 3,
        out_specs=[vmem] + [hbm] * (1 + len(kept)),
        out_shape=[jax.ShapeDtypeStruct((8, devices * capacity), F32), jax.ShapeDtypeStruct(chunk, BF)] + [jax.ShapeDtypeStruct(*k) for k in kept],
        scratch_shapes=scratch,
        compiler_params=pltpu.CompilerParams(vmem_limit_bytes=VMEM_LIMIT, **({} if alone else {"collective_id": 1, "has_side_effects": True})),
        cost_estimate=pl.CostEstimate(flops=8_000_000_000, bytes_accessed=12_000_000, transcendentals=4_000_000),
        name="route_and_forward",
    )(*routing, candidates, cotangent, histories, weight_in, weight_out)


def backward(histories, weight_in, weight_out, saved, d_enc, d_query, alone=False):
    hists, seq, width = histories.shape
    total = hists * seq
    operands = (weight_in, weight_out, *saved, d_enc)
    tile = (SIDE * SIDE, PAIR)
    scratch = [pltpu.VMEM(o.shape, o.dtype) for o in operands]
    operands += (d_query,)
    scratch += [
        pltpu.SemaphoreType.DMA((10,)),
        pltpu.SemaphoreType.DMA((2, width // PAIR)),
        pltpu.SemaphoreType.DMA((2,)),
        pltpu.SemaphoreType.DMA,
        pltpu.VMEM((total, width), BF),
        pltpu.VMEM((total, 4 * width), BF),
        pltpu.VMEM((total, width), BF),
        pltpu.VMEM((GROUPS, 2, SIDE, 2, SIDE, 2) + tile, BF),
        pltpu.VMEM((GROUPS,) + shape_of(DIMS) + tile, BF),
        pltpu.VMEM((GROUPS,) + shape_of(DIMS) + tile, BF),
        pltpu.VMEM((GROUPS,) + tile, F32),
        pltpu.SemaphoreType.DMA((GROUPS + 3 * len(ORDERS),)),
        pltpu.SemaphoreType.DMA((GROUPS + 3 * len(ORDERS),)),
        pltpu.SemaphoreType.DMA((GROUPS,)),
        pltpu.SemaphoreType.DMA((GROUPS,)),
    ]
    rest = [shape_of(without(DIMS, order[0])) for order in ORDERS]
    scratch += [pltpu.VMEM((SIDE - 1,) + dims + tile, BF) for dims in rest]
    scratch += [pltpu.VMEM(dims + tile, BF) for dims in rest]
    scratch += [pltpu.VMEM((SIDE**2 - 1,) + tile, BF)] * len(ORDERS) + [pltpu.VMEM((SIDE**3 - 1,) + tile, BF)]
    more = {} if alone else {"collective_id": 0, "has_side_effects": True}
    return pl.pallas_call(
        functools.partial(backward_kernel, alone),
        in_specs=[pl.BlockSpec(memory_space=pl.ANY)] * len(operands),
        out_specs=[pl.BlockSpec(memory_space=pltpu.VMEM)] * 3 + [pl.BlockSpec(memory_space=pl.ANY)],
        out_shape=[
            jax.ShapeDtypeStruct((hists, seq, width), BF),
            jax.ShapeDtypeStruct((SIDE, 4 * width), F32),
            jax.ShapeDtypeStruct((SIDE, width), F32),
            jax.ShapeDtypeStruct(d_query.shape, BF),
        ],
        scratch_shapes=scratch,
        compiler_params=pltpu.CompilerParams(vmem_limit_bytes=VMEM_LIMIT, **more),
        cost_estimate=pl.CostEstimate(flops=16_000_000_000, bytes_accessed=18_000_000, transcendentals=2_000_000),
        name="layer_backward",
    )(*operands)


def target(facts, recv, encoded, slots):
    hists, seq, width = encoded.shape
    room = (slots // TILE + hists - 1) * TILE
    vmem = pl.BlockSpec(memory_space=pltpu.VMEM)
    return pl.pallas_call(
        target_kernel,
        in_specs=[vmem] * 3,
        out_shape=[
            jax.ShapeDtypeStruct((slots // 8, 2, SIDE * SIDE, PAIR), BF),
            jax.ShapeDtypeStruct((hists, seq, width), BF),
        ],
        scratch_shapes=[
            pltpu.VMEM((slots, 2 * width), BF),
            pltpu.VMEM((room, 2 * width), BF),
            pltpu.VMEM((8, room), F32),
            pltpu.VMEM((hists, seq, width), F32),
            pltpu.VMEM((room, width), BF),
        ],
        compiler_params=pltpu.CompilerParams(vmem_limit_bytes=VMEM_LIMIT),
        cost_estimate=pl.CostEstimate(flops=8_000_000_000, bytes_accessed=4_000_000, transcendentals=4_000_000),
        name="target_backward",
    )(facts, recv, encoded)


def finish(capacity, owner_row, returned, history_grad, in_grad, out_grad):
    rows = owner_row.shape[1]
    slots = returned.shape[0] * 8
    width = history_grad.shape[2]
    vmem = pl.BlockSpec(memory_space=pltpu.VMEM)
    hbm = pl.BlockSpec(memory_space=pl.ANY)
    others = (history_grad, in_grad, out_grad)
    return pl.pallas_call(
        functools.partial(finish_kernel, capacity),
        in_specs=[vmem, vmem, hbm, vmem, vmem],
        out_specs=[vmem] * 4,
        out_shape=[jax.ShapeDtypeStruct((rows, width), BF)] + [jax.ShapeDtypeStruct(o.shape, o.dtype) for o in others],
        scratch_shapes=[pltpu.VMEM((slots, width), BF), pltpu.SemaphoreType.DMA],
        compiler_params=pltpu.CompilerParams(vmem_limit_bytes=VMEM_LIMIT),
        name="finish",
    )(owner_row, returned, *others)


def local(histories, weight_in, weight_out, candidates, cotangent, owner_ids, hist_slot, lengths):
    devices = lax.axis_size(AXES)
    imp_rows, width = candidates.shape
    capacity = max(2, 2 * imp_rows // devices)
    slots = devices * capacity
    routing = [r.reshape(1, imp_rows) for r in (owner_ids, hist_slot, lengths)]
    facts, recv, encoded, *saved = forward(
        histories, weight_in, weight_out, routing, candidates, cotangent, devices, capacity
    )
    d_query, d_encoded = target(facts, recv, encoded, slots)
    history_grad, in_grad, out_grad, returned = backward(
        histories, weight_in, weight_out, saved, d_encoded, d_query.reshape(devices, SIDE * SIDE, PAIR)
    )
    returned = returned.reshape(d_query.shape)
    candidate_grad, history_grad, in_grad, out_grad = finish(
        capacity, routing[0], returned, history_grad, in_grad, out_grad
    )
    return history_grad, candidate_grad, in_grad, out_grad


def solution(mesh):
    return jax.shard_map(
        local,
        mesh=mesh,
        in_specs=(
            P(AXES, None, None),
            P(),
            P(),
            P(AXES, None),
            P(AXES, None),
            P(AXES, None),
            P(AXES),
            P(AXES),
        ),
        out_specs=(P(AXES, None, None), P(AXES, None), P(AXES, None), P(AXES, None)),
        check_vma=False,
    )
```

```python
import functools

import jax
import jax.numpy as jnp
from jax import lax
from jax.experimental import pallas as pl
from jax.experimental.pallas import tpu as pltpu
from jax.sharding import PartitionSpec as P

HEADS = 8
HEAD_DIM = 64
PAIR = 128
EPS = 1e-05
BF = jnp.bfloat16
F32 = jnp.float32
AXES = ("hash", "dp")
VMEM_LIMIT = 60 * 1024 * 1024
MESH = pl.DeviceIdType.MESH
SIDE = 4
ORDERS = ("xyz", "yzx", "zxy", "xyz")
GROUPS = 5
TILE = 128
PLAN = ((1, (0,), ()), (2, (1,), ()), (3, (2,), (0,)), (4, (3,), (1,)))
DIMS = "lyxh"


def dot_nn(a, b):
    return lax.dot_general(a, b, (((1,), (0,)), ((), ())), preferred_element_type=F32)


def dot_nt(a, b):
    return lax.dot_general(a, b, (((1,), (1,)), ((), ())), preferred_element_type=F32)


def dot_tn(a, b):
    return lax.dot_general(a, b, (((0,), (0,)), ((), ())), preferred_element_type=F32)


def iota(shape, dim):
    return lax.broadcasted_iota(jnp.int32, shape, dim)


def silu_parts(half):
    t = jnp.tanh(half)
    plus = 1.0 + t
    return half * plus, plus * (1.0 + half * (1.0 - t))


def head_rows(scale):
    lanes = iota((1, PAIR), 1)
    first = jnp.where(lanes < HEAD_DIM, scale, 0.0).astype(BF)
    second = jnp.where(lanes < HEAD_DIM, 0.0, scale).astype(BF)
    return first, second


def lower_half(shape):
    return iota(shape, 1) < SIDE


def turn(x):
    return pltpu.roll(x, SIDE, 1)


def chunk_at(device, devices):
    return device % 2 * (devices // 2) + device // 2


def four_blocks(value):
    rows = value.shape[0]
    v = value.reshape(rows // 8, 8, 4 * PAIR)
    low = lower_half((rows // 8, 8, PAIR))
    even, odd = [], []
    for g in (0, 2):
        first, second = v[:, :, g * PAIR : (g + 1) * PAIR], v[:, :, (g + 1) * PAIR : (g + 2) * PAIR]
        even.append(jnp.where(low, first, turn(second)))
        odd.append(jnp.where(low, turn(first), second))
    return [jnp.concatenate(half, axis=1).astype(BF) for half in (even, odd)]


def to_chunks(ref, value):
    half = value.shape[0] // 8
    for pos in range(0, value.shape[1] // PAIR, 4):
        even, odd = four_blocks(value[:, pos * PAIR : (pos + 4) * PAIR])
        ref[:half, pos * SIDE : (pos + 4) * SIDE, :] = even
        ref[half:, pos * SIDE : (pos + 4) * SIDE, :] = odd


def from_chunks(ref, block):
    half = ref.shape[0] // 2
    low = lower_half((half, 8, PAIR))
    at = block // 2 * 8
    tile = at // 16 * 16
    first, second = ref[:half, tile : tile + 16, :], ref[half:, tile : tile + 16, :]
    first = first.astype(F32)[:, at - tile : at - tile + 8]
    second = second.astype(F32)[:, at - tile : at - tile + 8]
    if block % 2 == 0:
        rows = jnp.where(low, first, turn(second))
    else:
        rows = jnp.where(low, turn(first), second)
    return rows.reshape(half * 8, PAIR).astype(BF)


def as_column(row):
    rows = row.shape[1]
    same = iota((rows, rows), 0) == iota((rows, rows), 1)
    return jnp.sum(jnp.where(same, row, 0), axis=1, keepdims=True)


def slot_of(owner_row):
    rows = owner_row.shape[1]
    i, j = iota((rows, rows), 0), iota((rows, rows), 1)
    owner_col = as_column(owner_row)
    same = owner_col == owner_row
    place_col = jnp.sum(jnp.where(same & (j < i), 1, 0), axis=1, keepdims=True)
    place_row = jnp.sum(jnp.where(same & (i < j), 1, 0), axis=0, keepdims=True)
    return owner_col, place_col, owner_row, place_row


def finish_kernel(*refs):
    n = len(refs) // 3
    sources, results, buffers, sems = refs[:n], refs[n : 2 * n], refs[2 * n : 3 * n], refs[3 * n]
    ins = [pltpu.make_async_copy(a, b, sems.at[0, i]) for i, (a, b) in enumerate(zip(sources, buffers))]
    outs = [pltpu.make_async_copy(a, b, sems.at[1, i]) for i, (a, b) in enumerate(zip(buffers, results))]
    for c in ins:
        c.start()
    for c, d in zip(ins, outs):
        c.wait()
        d.start()
    for d in outs:
        d.wait()


def place():
    hash_i, dp_i = lax.axis_index("hash"), lax.axis_index("dp")
    return {"y": hash_i // 2, "core": hash_i % 2, "x": dp_i // SIDE, "z": dp_i % SIDE}


def device_at(at):
    return (at["y"] * 2 + at["core"], at["x"] * SIDE + at["z"])


def partner(me, axis, jump):
    size = 2 if axis == "core" else SIDE
    at = dict(me)
    at[axis] = (me[axis] + jump) % size
    return at


def partners(me):
    return [partner(me, "core", 1)] + [partner(me, a, j) for a in "xyz" for j in (1, 2, 3)]


def facts_by_owner(owner_row, place_row, slot_row, length_row, devices, capacity):
    rows = owner_row.shape[1]
    slot, length = as_column(slot_row), as_column(length_row)
    lane = iota((rows, PAIR), 1)
    total = jnp.zeros((devices, PAIR), F32)
    for p in range(capacity):
        chosen = (iota((devices, rows), 0) == owner_row) & (place_row == p)
        value = jnp.where(lane == p, slot, jnp.where(lane == capacity + p, length, 0))
        total += dot_nn(jnp.where(chosen, 1.0, 0.0).astype(BF), value.astype(F32).astype(BF))
    return total


def received(facts, shape):
    devices, slots = facts.shape[0], shape[1]
    capacity = slots // devices
    lane, source = iota((devices, slots), 1), iota((devices, slots), 0)
    rows = []
    for first in (0, capacity):
        total = jnp.zeros((devices, slots), F32)
        for p in range(capacity):
            total = jnp.where(lane == source * capacity + p, facts[:, first + p : first + p + 1], total)
        rows.append(jnp.sum(total, axis=0, keepdims=True))
    return jnp.where(iota(shape, 0) == 0, rows[0], rows[1])


def forward_kernel(
    alone, capacity,
    owner_ref, slot_ref, length_ref, cand_ref, cot_ref, x_hbm, win_hbm, wout_hbm,
    facts_ref, recv_hbm, enc_hbm, sg_hbm, gate_hbm, vqk_hbm, nrm_hbm, inv_hbm, act_hbm, slope_hbm, xt_hbm,
    x_s, win_s, wout_s, load, send_s, enc_s, sg_s, gate_s, vqk_s, nrm_s, inv_s, act_s, slope_s, xt_s, save, mix_s, send, recv, own, tell_s, told_s, tell, told,
):
    hists, seq, width = x_s.shape
    rows = cand_ref.shape[0]
    loads = [
        pltpu.make_async_copy(a, b, load.at[i])
        for i, (a, b) in enumerate(((x_hbm, x_s), (win_hbm, win_s), (wout_hbm, wout_s)))
    ]
    for c in loads:
        c.start()
    devices = send_s.shape[0]
    if not alone:
        hash_i, dp_i = lax.axis_index("hash"), lax.axis_index("dp")
        ring = lax.axis_size("dp")
        me = hash_i * ring + dp_i
        barrier = pltpu.get_barrier_semaphore()

        def greet(jump, carry):
            to = lax.rem(me + jump, devices)
            pl.semaphore_signal(barrier, inc=1, device_id=(to // ring, to % ring), device_id_type=MESH)
            return carry

        lax.fori_loop(1, devices, greet, 0)
    _, _, owner_row, place_row = slot_of(owner_ref[...])
    slots = devices * capacity
    chosen = jnp.where(iota((slots, rows), 0) == owner_row * capacity + place_row, 1.0, 0.0).astype(BF)
    facts = facts_by_owner(owner_row, place_row, slot_ref[...], length_ref[...], devices, capacity)
    tell_s[...] = facts.reshape(devices, 1, PAIR)
    sent_rows = width // PAIR * SIDE
    for i, value in enumerate((cand_ref[...], cot_ref[...])):
        to_chunks(send_s.at[:, i * sent_rows : (i + 1) * sent_rows], dot_nn(chosen, value))
    if not alone:
        pl.semaphore_wait(barrier, devices - 1)

        def push(jump, carry):
            to = lax.rem(me + lax.rem(jump * 37, devices), devices)
            pltpu.make_async_remote_copy(
                src_ref=send_s.at[chunk_at(to, devices)], dst_ref=recv_hbm.at[chunk_at(me, devices)],
                send_sem=send, recv_sem=recv, device_id=(to // ring, to % ring), device_id_type=MESH,
            ).start()
            pltpu.make_async_remote_copy(
                src_ref=tell_s.at[to], dst_ref=told_s.at[me],
                send_sem=tell, recv_sem=told, device_id=(to // ring, to % ring), device_id_type=MESH,
            ).start()
            return carry

        lax.fori_loop(1, devices, push, 0)
        keep = pltpu.make_async_copy(send_s.at[chunk_at(me, devices)], recv_hbm.at[chunk_at(me, devices)], own)
        keep.start()
        told_s[me] = tell_s[me]
    for c in loads:
        c.wait()
    cut = seq // 2
    seen = iota((cut, seq), 0) <= iota((cut, seq), 1)
    half_scale = head_rows(0.5 * HEAD_DIM**-0.5)
    inv_seq = head_rows(1.0 / seq)
    outs = (
        (enc_s, enc_hbm), (sg_s, sg_hbm), (gate_s, gate_hbm), (vqk_s, vqk_hbm), (nrm_s, nrm_hbm), (inv_s, inv_hbm),
        (act_s, act_hbm), (slope_s, slope_hbm),
    )

    def saves(h):
        return [pltpu.make_async_copy(a.at[h], b.at[h], save.at[i, h]) for i, (a, b) in enumerate(outs)]

    def one(hist, carry):
        x = x_s[hist]
        xh = x * 0.5
        xt_s[:, pl.ds(pl.multiple_of(hist * seq, seq), seq)] = x.T
        for part in range(4):
            cols = slice(part * width, (part + 1) * width)
            act, grad2 = silu_parts(dot_nn(xh, win_s[:, cols]))
            sg_s[hist, :, cols] = (0.5 * grad2).astype(BF)
            if part == 0:
                gate_s[hist] = act.astype(BF)
            else:
                vqk_s[hist, :, (part - 1) * width : part * width] = act.astype(BF)
        for pair in range(width // PAIR):
            lanes = [slice(b * width + pair * PAIR, b * width + (pair + 1) * PAIR) for b in range(3)]
            v = vqk_s[hist, :, lanes[0]]
            q = vqk_s[hist, :, lanes[1]]
            k = vqk_s[hist, :, lanes[2]]
            total = None
            for h in range(2):
                qs, vs = q * half_scale[h], v * inv_seq[h]
                act, grad2 = silu_parts(dot_nt(k[:cut], qs))
                a0 = jnp.where(seen, act, 0.0).astype(BF)
                g0 = jnp.where(seen, grad2, 0.0).astype(BF)
                act, grad2 = silu_parts(dot_nt(k[cut:], qs[cut:]))
                a1 = jnp.where(seen[:, :cut], act, 0.0).astype(BF)
                g1 = jnp.where(seen[:, :cut], grad2, 0.0).astype(BF)
                act_s[hist, 2 * pair + h] = jnp.concatenate([a0, a1], axis=1)
                slope_s[hist, 2 * pair + h] = jnp.concatenate([g0, g1], axis=1)
                later = jnp.concatenate([a0[:, cut:], a1], axis=0)
                terms = (dot_tn(a0[:, :cut], vs[:cut]), dot_tn(later, vs))
                total = terms if total is None else [a + b for a, b in zip(total, terms)]
            mix_s[:cut, lanes[0]] = total[0]
            mix_s[cut:, lanes[0]] = total[1]
        mixed = mix_s[...]
        centred = mixed - jnp.mean(mixed, axis=1, keepdims=True)
        inv = lax.rsqrt(jnp.mean(centred * centred, axis=1, keepdims=True) + EPS)
        normed = centred * inv
        nrm_s[hist] = normed.astype(BF)
        inv_s[hist] = jnp.broadcast_to(inv, (seq, PAIR))
        merged = (normed * gate_s[hist].astype(F32)).astype(BF)
        enc_s[hist] = (x.astype(F32) + dot_nn(merged, wout_s[...])).astype(BF)
        for c in saves(hist):
            c.start()
        return carry

    lax.fori_loop(0, hists, one, 0)
    turned = pltpu.make_async_copy(xt_s, xt_hbm, load.at[0])
    turned.start()
    for h in range(hists):
        for c in saves(h):
            c.wait()
    turned.wait()
    if not alone:
        keep.wait()
        all_but_one = pl.ds(0, devices - 1)
        pltpu.make_async_remote_copy(
            src_ref=send_s.at[all_but_one], dst_ref=recv_hbm.at[all_but_one], send_sem=send, recv_sem=recv,
            device_id=(lax.rem(hash_i + 1, devices // ring), dp_i), device_id_type=MESH,
        ).wait()
        pltpu.make_async_remote_copy(
            src_ref=tell_s.at[all_but_one], dst_ref=told_s.at[all_but_one], send_sem=tell, recv_sem=told,
            device_id=(lax.rem(hash_i + 1, devices // ring), dp_i), device_id_type=MESH,
        ).wait()
        facts_ref[...] = received(told_s[...].reshape(devices, PAIR), facts_ref.shape)


def without(dims, axis):
    return "".join(d for d in dims if d not in ("lh" if axis == "z" else axis))


def shape_of(dims):
    return tuple(2 if d in "lh" else SIDE for d in dims)


def along(ref, dims, axis, at):
    index = {"x": at["x"], "y": at["y"], "l": at["z"] % 2, "h": at["z"] // 2}
    gone = "lh" if axis == "z" else axis
    return ref.at[tuple(index[d] if d in gone else slice(None) for d in dims)]


class Reduction:
    def __init__(self, parts, got0, pair, axis_got, axis_sum, landed, sums, sems, push_sems):
        self.me = place()
        self.parts, self.got0, self.pair = parts, got0, pair
        self.axis_got, self.axis_sum, self.landed, self.sums = axis_got, axis_sum, landed, sums
        self.send, self.recv = sems
        self.push_sem, self.land_sem = push_sems

    def device(self, jump):
        ring = lax.axis_size("dp")
        to = lax.rem(self.index() + jump, lax.axis_size(AXES))
        return (to // ring, to % ring), to

    def index(self):
        return lax.axis_index("hash") * lax.axis_size("dp") + lax.axis_index("dp")

    def greet(self):
        barrier = pltpu.get_barrier_semaphore()

        def one(jump, carry):
            pl.semaphore_signal(barrier, inc=1, device_id=self.device(jump)[0], device_id_type=MESH)
            return carry

        lax.fori_loop(1, lax.axis_size(AXES), one, 0)

    def enter(self):
        pl.semaphore_wait(pltpu.get_barrier_semaphore(), lax.axis_size(AXES) - 1)

    def give_back(self, grads, returned, sems, own):
        me = chunk_at(self.index(), lax.axis_size(AXES))

        def one(jump, carry):
            device_id, to = self.device(jump)
            pltpu.make_async_remote_copy(
                src_ref=grads.at[chunk_at(to, lax.axis_size(AXES))], dst_ref=returned.at[me], send_sem=sems.at[0], recv_sem=sems.at[1],
                device_id=device_id, device_id_type=MESH,
            ).start()
            return carry

        lax.fori_loop(1, lax.axis_size(AXES), one, 0)
        pltpu.make_async_copy(grads.at[me], returned.at[me], own).start()

    def take_back(self, grads, returned, sems, own):
        me = chunk_at(self.index(), lax.axis_size(AXES))
        others = pl.ds(0, lax.axis_size(AXES) - 1)
        pltpu.make_async_remote_copy(
            src_ref=grads.at[others], dst_ref=returned.at[others], send_sem=sems.at[0], recv_sem=sems.at[1],
            device_id=self.device(1)[0], device_id_type=MESH,
        ).wait()
        pltpu.make_async_copy(grads.at[me], returned.at[me], own).wait()

    def chip(self, jump):
        me = self.me
        q = lax.rem((me["y"] * SIDE + me["x"]) * SIDE + me["z"] + jump, SIDE**3)
        return {"y": q // SIDE**2, "x": q // SIDE % SIDE, "z": q % SIDE, "core": me["core"]}

    def copy(self, src, dst, number, other):
        return pltpu.make_async_remote_copy(
            src_ref=src, dst_ref=dst, send_sem=self.send.at[number], recv_sem=self.recv.at[number],
            device_id=device_at(other), device_id_type=MESH,
        )

    def copies(self, t, stage):
        if stage == 0:
            mate = partner(self.me, "core", 1)
            return [self.copy(self.parts.at[t, :, :, mate["core"]], self.got0.at[t], t, mate)]
        out = []
        for j in (1, 2, 3):
            other = partner(self.me, ORDERS[t][0], j)
            src = along(self.pair.at[t], DIMS, ORDERS[t][0], other)
            out.append(self.copy(src, self.axis_got[t].at[j - 1], GROUPS + 3 * t + j - 1, other))
        return out

    def start(self, t, stage):
        for c in self.copies(t, stage):
            c.start()

    def finish(self, t, stage):
        for c in self.copies(t, stage):
            c.wait_recv()
        if stage == 0:
            total = self.parts[t, :, :, self.me["core"]].astype(F32) + self.got0[t].astype(F32)
            self.pair[t] = total.astype(BF)
            return
        total = along(self.pair.at[t], DIMS, ORDERS[t][0], self.me)[...].astype(F32)
        for j in range(3):
            total = total + self.axis_got[t][j].astype(F32)
        self.axis_sum[t][...] = total.astype(BF)

    def advance(self, t, stage):
        self.finish(t, stage)
        if stage == 0 and t < len(ORDERS):
            self.start(t, 1)
        else:
            self.push(t)

    def others(self, t):
        return (SIDE**2 if t < len(ORDERS) else SIDE**3) - 1

    def member(self, t, jump):
        if t == len(ORDERS):
            return self.chip(jump)
        a, b = ORDERS[t][1:]
        q = lax.rem(self.me[a] * SIDE + self.me[b] + jump, SIDE**2)
        return {**self.me, a: q // SIDE, b: q % SIDE}

    def chunk(self, t, at):
        index = {"x": at["x"], "y": at["y"], "l": at["z"] % 2, "h": at["z"] // 2}
        if t == len(ORDERS):
            return self.pair.at[(t,) + tuple(index[d] for d in DIMS)]
        return self.axis_sum[t].at[tuple(index[d] for d in without(DIMS, ORDERS[t][0]))]

    def push(self, t):
        def one(jump, carry):
            to = self.member(t, jump)
            pltpu.make_async_remote_copy(
                src_ref=self.chunk(t, to), dst_ref=self.landed[t].at[jump - 1],
                send_sem=self.push_sem.at[t], recv_sem=self.land_sem.at[t],
                device_id=device_at(to), device_id_type=MESH,
            ).start()
            return carry

        lax.fori_loop(1, self.others(t) + 1, one, 0)

    def land(self, t):
        every = self.landed[t]
        pltpu.make_async_remote_copy(
            src_ref=every, dst_ref=every, send_sem=self.push_sem.at[t], recv_sem=self.land_sem.at[t],
            device_id=device_at(self.member(t, 1)), device_id_type=MESH,
        ).wait()
        own = self.chunk(t, self.me)[...].astype(F32)
        self.sums[t] = own + jnp.sum(every[...].astype(F32), axis=0)

    def end(self, win_ref, wout_ref):
        width = wout_ref.shape[1]
        for block in range(SIDE):
            rows = slice(block * SIDE, (block + 1) * SIDE)
            wout_ref[:, block * PAIR : (block + 1) * PAIR] = self.sums[0, rows]
            for pair in range(GROUPS - 1):
                at = (block + 1) % SIDE * width + pair * PAIR
                win_ref[:, at : at + PAIR] = self.sums[1 + pair, rows]
        for t in range(GROUPS):
            for stage in range(2 if t < len(ORDERS) else 1):
                for c in self.copies(t, stage):
                    c.wait_send()


class Nothing:
    def __getattr__(self, name):
        return lambda *args: None


def backward_kernel(
    alone,
    win_hbm, wout_hbm, sg_hbm, gate_hbm, vqk_hbm, nrm_hbm, inv_hbm, act_hbm, slope_hbm, xt_hbm, denc_hbm, grads_hbm, owner_ref,
    hg_ref, gin_ref, gout_ref, cand_ref,
    win_s, wout_s, sg_s, gate_s, vqk_s, nrm_s, inv_s, act_s, slope_s, xt_s, denc_s, load, load_pair, back, own, ret_s, slots_s,
    mg_s, dp_s, dm_s, parts_s, got0, pair_s, sums, send, recv, push, land, *bufs,
):
    hists, seq, width = hg_ref.shape
    gate_cols, other_cols = pl.ds(0, width), pl.ds(width, 3 * width)
    moves = (
        (denc_hbm, denc_s), (wout_hbm, wout_s), (nrm_hbm, nrm_s), (gate_hbm, gate_s), (inv_hbm, inv_s),
        (sg_hbm.at[:, :, gate_cols], sg_s.at[:, :, gate_cols]),
        (vqk_hbm, vqk_s), (sg_hbm.at[:, :, other_cols], sg_s.at[:, :, other_cols]), (xt_hbm, xt_s), (win_hbm, win_s),
    )
    loads = [pltpu.make_async_copy(a, b, load.at[i]) for i, (a, b) in enumerate(moves)]

    def pair_loads(pair):
        heads = pl.ds(2 * pair, 2)
        return [
            pltpu.make_async_copy(a.at[:, heads], b.at[:, heads], load_pair.at[i, pair])
            for i, (a, b) in enumerate(((act_hbm, act_s), (slope_hbm, slope_s)))
        ]

    for c in loads[:6]:
        c.start()
    n = len(ORDERS)
    comm = Nothing()
    if not alone:
        comm = Reduction(
            parts_s, got0, pair_s, bufs[:n], bufs[n : 2 * n], bufs[2 * n :], sums, (send, recv), (push, land)
        )
    comm.greet()

    def rows_of(h):
        return pl.ds(pl.multiple_of(h * seq, seq), seq)

    def store_part(t, value):
        for i, half in enumerate(four_blocks(value)):
            parts_s[t, i] = half.reshape(parts_s.shape[2:])

    for c in loads[:6]:
        c.wait()
    for c in loads[6:8] + pair_loads(0) + loads[8:9]:
        c.start()
    for pair in range(1, width // PAIR):
        for c in pair_loads(pair):
            c.start()
    loads[9].start()

    def gate_step(h, carry):
        rows = rows_of(h)
        normed = nrm_s[h].astype(F32)
        gate = gate_s[h].astype(F32)
        mg_s[rows, :] = (normed * gate).astype(BF)
        d_merged = dot_nt(denc_s[h], wout_s[...])
        dp_s[rows, :width] = (d_merged * normed * sg_s[h, :, :width].astype(F32)).astype(BF)
        d_norm = d_merged * gate
        m1 = jnp.mean(d_norm, axis=1, keepdims=True)
        m2 = jnp.mean(d_norm * normed, axis=1, keepdims=True)
        dm_s[rows, :] = (inv_s[h][:, :1] * (d_norm - m1 - normed * m2)).astype(BF)
        return carry

    lax.fori_loop(0, hists, gate_step, 0)
    comm.enter()
    comm.give_back(grads_hbm, ret_s, back, own)
    store_part(0, dot_tn(mg_s[...], denc_s[...].reshape(hists * seq, width)))
    comm.start(0, 0)
    for c in loads[6:9]:
        c.wait()

    cut = seq // 2
    half_scale = head_rows(0.5 * HEAD_DIM**-0.5)
    one = head_rows(1.0)
    scales = (1.0 / seq, 0.5 * HEAD_DIM**-0.5 / seq, 1.0 / seq)

    def attn_step(pair, carry):
        lanes = [pl.ds(pl.multiple_of(b * width + pair * PAIR, PAIR), PAIR) for b in range(4)]
        for c in pair_loads(pair):
            c.wait()
        for h in range(hists):
            v, q, k = (vqk_s[h, :, lanes[b]] for b in range(3))
            dm = dm_s[h * seq : (h + 1) * seq, lanes[0]]
            sums_ = [None] * 6
            for head in range(2):
                qs, dms, ks = q * half_scale[head], dm * one[head], k * one[head]
                a, g = act_s[h, 2 * pair + head], slope_s[h, 2 * pair + head].astype(F32)
                a0, a1 = a[:, :seq], a[:, seq:]
                s0 = (dot_nt(v[:cut], dms) * g[:, :seq]).astype(BF)
                s1 = (dot_nt(v[cut:], dms[cut:]) * g[:, seq:]).astype(BF)
                terms = (
                    dot_nn(a0, dms), dot_nn(a1, dms[cut:]),
                    dot_tn(s0[:, :cut], ks[:cut]), dot_tn(jnp.concatenate([s0[:, cut:], s1], axis=0), ks),
                    dot_nn(s0, qs), dot_nn(s1, qs[cut:]),
                )
                sums_ = [t if total is None else total + t for total, t in zip(sums_, terms)]
            for i, value in enumerate(sums_):
                b, part = 1 + i // 2, i % 2
                at = slice(h * seq + part * cut, h * seq + (part + 1) * cut)
                sg = sg_s[h, part * cut : (part + 1) * cut, lanes[b]].astype(F32) * scales[b - 1]
                dp_s[at, lanes[b]] = (value * sg).astype(BF)
        d_pair = jnp.concatenate([dp_s[:, lanes[b]] for b in (1, 2, 3, 0)], axis=1)
        store_part(1 + pair, dot_nn(xt_s[...], d_pair))
        for now, (started, paired, summed) in enumerate(PLAN):
            @pl.when(pair == now)
            def _():
                comm.start(started, 0)
                for t in paired:
                    comm.advance(t, 0)
                for t in summed:
                    comm.advance(t, 1)
        return carry

    lax.fori_loop(0, width // PAIR, attn_step, 0)
    loads[9].wait()

    def grads(lo, hi):
        for h in range(lo, hi):
            prod = dot_nt(dp_s[h * seq : (h + 1) * seq, :], win_s[...])
            hg_ref[h] = (denc_s[h].astype(F32) + prod).astype(BF)

    grads(0, hists // 2)
    comm.advance(4, 0)
    comm.advance(2, 1)
    grads(hists // 2, hists)
    comm.advance(3, 1)
    comm.take_back(grads_hbm, ret_s, back, own)
    for block in range(width // PAIR):
        slots_s[:, block * PAIR : (block + 1) * PAIR] = from_chunks(ret_s, block)
    owner_col, place_col, _, _ = slot_of(owner_ref[...])
    slots = slots_s.shape[0]
    target_col = owner_col * SIDE + place_col
    chosen = jnp.where(iota((cand_ref.shape[0], slots), 1) == target_col, 1.0, 0.0).astype(BF)
    cand_ref[...] = dot_nn(chosen, slots_s[...]).astype(BF)
    for t in range(GROUPS):
        comm.land(t)
    comm.end(gin_ref, gout_ref)


def sort_slots(facts_ref, hists):
    hist_row, len_row = facts_ref[0:1], facts_ref[1:2]
    slots = hist_row.shape[1]
    picked = jnp.where((iota((8, slots), 0).astype(F32) == hist_row) & (len_row > 0.0), 1.0, 0.0)
    before = jnp.where(iota((slots, slots), 0) < iota((slots, slots), 1), 1.0, 0.0).astype(BF)
    rank = dot_nn(picked.astype(BF), before)
    place_row = jnp.full((1, slots), -1.0, F32)
    first, runs = jnp.int32(0), []
    for own in range(hists):
        tiles = (jnp.sum(picked[own : own + 1]).astype(jnp.int32) + (TILE - 1)) // TILE
        here = rank[own : own + 1] + (first * TILE).astype(F32)
        place_row = jnp.where(picked[own : own + 1] > 0.0, here, place_row)
        runs.append((first, first + tiles))
        first = first + tiles
    return place_row, runs


def target_kernel(
    facts_ref, recv_ref, enc_hbm, dq_ref, denc_hbm, rows_s, sorted_s, len_s, de_s, dq_s, enc_ref, denc_s, load, save
):
    hists, seq, width = enc_ref.shape
    fetch = pltpu.make_async_copy(enc_hbm, enc_ref, load)
    fetch.start()
    saves = [pltpu.make_async_copy(denc_s.at[h], denc_hbm.at[h], save.at[h]) for h in range(hists)]
    slots = rows_s.shape[0]
    room = sorted_s.shape[0]
    blocks = width // PAIR
    for block in range(2 * blocks):
        rows_s[:, block * PAIR : (block + 1) * PAIR] = from_chunks(recv_ref, block)
    place_row, runs = sort_slots(facts_ref, hists)
    chosen = jnp.where(iota((room, slots), 0).astype(F32) == place_row, 1.0, 0.0).astype(BF)
    for half in range(2):
        cols = slice(half * width, (half + 1) * width)
        sorted_s[:, cols] = dot_nn(chosen, rows_s[:, cols]).astype(BF)
    len_s[...] = dot_nt(facts_ref[...].astype(BF), chosen)
    de_s[...] = jnp.zeros(de_s.shape, F32)
    dq_s[...] = jnp.zeros(dq_s.shape, BF)
    scale = 0.5 * HEAD_DIM**-0.5
    half_scale = head_rows(scale)
    one = head_rows(1.0)
    positions = iota((seq, TILE), 0).astype(F32)
    low = iota((TILE, PAIR), 1) < HEAD_DIM
    fetch.wait()
    for own in range(hists):

        def body(tile, carry):
            at = pl.ds(pl.multiple_of(tile * TILE, TILE), TILE)
            length = len_s[1:2, at]
            weight = jnp.where(positions < length, 1.0 / jnp.maximum(length, 1.0), 0.0)
            weight = jnp.concatenate([weight, weight], axis=1)
            for pair in range(blocks):
                cols = slice(pair * PAIR, (pair + 1) * PAIR)
                enc = enc_ref[own, :, cols]
                q, g = sorted_s[at, cols], sorted_s[at, width + pair * PAIR : width + (pair + 1) * PAIR]
                qq = jnp.concatenate([q * half_scale[0], q * half_scale[1]], axis=0)
                gg = jnp.concatenate([g * one[0], g * one[1]], axis=0)
                act, grad2 = silu_parts(dot_nt(enc, qq))
                a = (act * weight).astype(BF)
                d_s = (dot_nt(enc, gg) * grad2 * weight).astype(BF)
                de_s[own, :, cols] += dot_nn(a, gg) + dot_nn(d_s, qq)
                both = dot_tn(d_s, enc)
                dq_s[at, cols] = (jnp.where(low, both[:TILE], both[TILE:]) * scale).astype(BF)
            return carry

        lax.fori_loop(runs[own][0], runs[own][1], body, 0)
        denc_s[own] = de_s[own].astype(BF)
        saves[own].start()
    place_col = jnp.transpose(jnp.broadcast_to(place_row, (8, slots)))[:, 0:1]
    back = jnp.where(iota((slots, room), 1).astype(F32) == place_col, 1.0, 0.0).astype(BF)
    to_chunks(dq_ref, dot_nn(back, dq_s[...]))
    for c in saves:
        c.wait()


def forward(histories, weight_in, weight_out, routing, candidates, cotangent, devices, capacity, alone=False):
    hists, seq, width = histories.shape
    chunk = (devices, 2 * width // PAIR * SIDE, PAIR)
    widths = [(width, BF), (4 * width, BF), (width, BF), (3 * width, BF), (width, BF), (PAIR, F32)]
    kept = [((hists, seq, w), t) for w, t in widths]
    kept += [((hists, HEADS, seq // 2, seq // 2 * 3), BF)] * 2 + [((width, hists * seq), BF)]
    scratch = [pltpu.VMEM(o.shape, o.dtype) for o in (histories, weight_in, weight_out)]
    scratch += [pltpu.SemaphoreType.DMA((3,)), pltpu.VMEM(chunk, BF)]
    scratch += [pltpu.VMEM(*k) for k in kept]
    scratch += [pltpu.SemaphoreType.DMA((len(kept) - 1, hists)), pltpu.VMEM((seq, width), F32)]
    scratch += [pltpu.SemaphoreType.DMA] * 3
    scratch += [pltpu.VMEM((devices, 1, PAIR), F32)] * 2 + [pltpu.SemaphoreType.DMA] * 2
    vmem = pl.BlockSpec(memory_space=pltpu.VMEM)
    hbm = pl.BlockSpec(memory_space=pl.ANY)
    return pl.pallas_call(
        functools.partial(forward_kernel, alone, capacity),
        in_specs=[vmem] * 5 + [hbm] * 3,
        out_specs=[vmem] + [hbm] * (1 + len(kept)),
        out_shape=[jax.ShapeDtypeStruct((8, devices * capacity), F32), jax.ShapeDtypeStruct(chunk, BF)] + [jax.ShapeDtypeStruct(*k) for k in kept],
        scratch_shapes=scratch,
        compiler_params=pltpu.CompilerParams(vmem_limit_bytes=VMEM_LIMIT, **({} if alone else {"collective_id": 1, "has_side_effects": True})),
        cost_estimate=pl.CostEstimate(flops=8_000_000_000, bytes_accessed=12_000_000, transcendentals=4_000_000),
        name="route_and_forward",
    )(*routing, candidates, cotangent, histories, weight_in, weight_out)


def backward(histories, weight_in, weight_out, saved, d_enc, d_query, owner_row, alone=False):
    hists, seq, width = histories.shape
    total = hists * seq
    operands = (weight_in, weight_out, *saved, d_enc)
    tile = (SIDE * SIDE, PAIR)
    scratch = [pltpu.VMEM(o.shape, o.dtype) for o in operands]
    operands += (d_query, owner_row)
    scratch += [
        pltpu.SemaphoreType.DMA((10,)),
        pltpu.SemaphoreType.DMA((2, width // PAIR)),
        pltpu.SemaphoreType.DMA((2,)),
        pltpu.SemaphoreType.DMA,
        pltpu.VMEM(d_query.shape, BF),
        pltpu.VMEM((d_query.shape[0] * SIDE, width), BF),
        pltpu.VMEM((total, width), BF),
        pltpu.VMEM((total, 4 * width), BF),
        pltpu.VMEM((total, width), BF),
        pltpu.VMEM((GROUPS, 2, SIDE, 2, SIDE, 2) + tile, BF),
        pltpu.VMEM((GROUPS,) + shape_of(DIMS) + tile, BF),
        pltpu.VMEM((GROUPS,) + shape_of(DIMS) + tile, BF),
        pltpu.VMEM((GROUPS,) + tile, F32),
        pltpu.SemaphoreType.DMA((GROUPS + 3 * len(ORDERS),)),
        pltpu.SemaphoreType.DMA((GROUPS + 3 * len(ORDERS),)),
        pltpu.SemaphoreType.DMA((GROUPS,)),
        pltpu.SemaphoreType.DMA((GROUPS,)),
    ]
    rest = [shape_of(without(DIMS, order[0])) for order in ORDERS]
    scratch += [pltpu.VMEM((SIDE - 1,) + dims + tile, BF) for dims in rest]
    scratch += [pltpu.VMEM(dims + tile, BF) for dims in rest]
    scratch += [pltpu.VMEM((SIDE**2 - 1,) + tile, BF)] * len(ORDERS) + [pltpu.VMEM((SIDE**3 - 1,) + tile, BF)]
    more = {} if alone else {"collective_id": 0, "has_side_effects": True}
    return pl.pallas_call(
        functools.partial(backward_kernel, alone),
        in_specs=[pl.BlockSpec(memory_space=pl.ANY)] * (len(operands) - 1) + [pl.BlockSpec(memory_space=pltpu.VMEM)],
        out_specs=[pl.BlockSpec(memory_space=pltpu.VMEM)] * 4,
        out_shape=[
            jax.ShapeDtypeStruct((hists, seq, width), BF),
            jax.ShapeDtypeStruct((SIDE, 4 * width), F32),
            jax.ShapeDtypeStruct((SIDE, width), F32),
            jax.ShapeDtypeStruct((owner_row.shape[1], width), BF),
        ],
        scratch_shapes=scratch,
        compiler_params=pltpu.CompilerParams(vmem_limit_bytes=VMEM_LIMIT, **more),
        cost_estimate=pl.CostEstimate(flops=16_000_000_000, bytes_accessed=18_000_000, transcendentals=2_000_000),
        name="layer_backward",
    )(*operands)


def target(facts, recv, encoded, slots):
    hists, seq, width = encoded.shape
    room = (slots // TILE + hists - 1) * TILE
    vmem = pl.BlockSpec(memory_space=pltpu.VMEM)
    return pl.pallas_call(
        target_kernel,
        in_specs=[vmem, vmem, pl.BlockSpec(memory_space=pl.ANY)],
        out_specs=[vmem, pl.BlockSpec(memory_space=pl.ANY)],
        out_shape=[
            jax.ShapeDtypeStruct((slots // SIDE, SIDE * SIDE, PAIR), BF),
            jax.ShapeDtypeStruct((hists, seq, width), BF),
        ],
        scratch_shapes=[
            pltpu.VMEM((slots, 2 * width), BF),
            pltpu.VMEM((room, 2 * width), BF),
            pltpu.VMEM((8, room), F32),
            pltpu.VMEM((hists, seq, width), F32),
            pltpu.VMEM((room, width), BF),
            pltpu.VMEM((hists, seq, width), BF),
            pltpu.VMEM((hists, seq, width), BF),
            pltpu.SemaphoreType.DMA,
            pltpu.SemaphoreType.DMA((hists,)),
        ],
        compiler_params=pltpu.CompilerParams(vmem_limit_bytes=VMEM_LIMIT),
        cost_estimate=pl.CostEstimate(flops=8_000_000_000, bytes_accessed=4_000_000, transcendentals=4_000_000),
        name="target_backward",
    )(facts, recv, encoded)


def finish(*results):
    hbm = pl.BlockSpec(memory_space=pl.ANY)
    return pl.pallas_call(
        finish_kernel,
        in_specs=[hbm] * len(results),
        out_specs=[hbm] * len(results),
        out_shape=[jax.ShapeDtypeStruct(r.shape, r.dtype) for r in results],
        scratch_shapes=[pltpu.VMEM(r.shape, r.dtype) for r in results]
        + [pltpu.SemaphoreType.DMA((2, len(results)))],
        compiler_params=pltpu.CompilerParams(vmem_limit_bytes=VMEM_LIMIT),
        name="finish",
    )(*results)


def local(histories, weight_in, weight_out, candidates, cotangent, owner_ids, hist_slot, lengths):
    devices = lax.axis_size(AXES)
    imp_rows, width = candidates.shape
    capacity = max(2, 2 * imp_rows // devices)
    slots = devices * capacity
    routing = [r.reshape(1, imp_rows) for r in (owner_ids, hist_slot, lengths)]
    facts, recv, encoded, *saved = forward(
        histories, weight_in, weight_out, routing, candidates, cotangent, devices, capacity
    )
    d_query, d_encoded = target(facts, recv, encoded, slots)
    history_grad, in_grad, out_grad, candidate_grad = backward(
        histories, weight_in, weight_out, saved, d_encoded, d_query, routing[0]
    )
    return finish(history_grad, candidate_grad, in_grad, out_grad)


def solution(mesh):
    return jax.shard_map(
        local,
        mesh=mesh,
        in_specs=(
            P(AXES, None, None),
            P(),
            P(),
            P(AXES, None),
            P(AXES, None),
            P(AXES, None),
            P(AXES),
            P(AXES),
        ),
        out_specs=(P(AXES, None, None), P(AXES, None), P(AXES, None), P(AXES, None)),
        check_vma=False,
    )
```

```python
import functools

import jax
import jax.numpy as jnp
from jax import lax
from jax.experimental import pallas as pl
from jax.experimental.pallas import tpu as pltpu
from jax.sharding import PartitionSpec as P

HEADS = 8
HEAD_DIM = 64
PAIR = 128
EPS = 1e-05
BF = jnp.bfloat16
F32 = jnp.float32
AXES = ("hash", "dp")
VMEM_LIMIT = 60 * 1024 * 1024
MESH = pl.DeviceIdType.MESH
SIDE = 4
ORDERS = ("xyz", "yzx", "zxy", "xyz")
GROUPS = 5
TILE = 128
PLAN = ((1, (0,), ()), (2, (1,), ()), (3, (2,), (0,)), (4, (3,), (1,)))
DIMS = "lyxh"


def dot_nn(a, b):
    return lax.dot_general(a, b, (((1,), (0,)), ((), ())), preferred_element_type=F32)


def dot_nt(a, b):
    return lax.dot_general(a, b, (((1,), (1,)), ((), ())), preferred_element_type=F32)


def dot_tn(a, b):
    return lax.dot_general(a, b, (((0,), (0,)), ((), ())), preferred_element_type=F32)


def iota(shape, dim):
    return lax.broadcasted_iota(jnp.int32, shape, dim)


def silu_parts(half):
    t = jnp.tanh(half)
    plus = 1.0 + t
    return half * plus, plus * (1.0 + half * (1.0 - t))


def head_rows(scale):
    lanes = iota((1, PAIR), 1)
    first = jnp.where(lanes < HEAD_DIM, scale, 0.0).astype(BF)
    second = jnp.where(lanes < HEAD_DIM, 0.0, scale).astype(BF)
    return first, second


def lower_half(shape):
    return iota(shape, 1) < SIDE


def turn(x):
    return pltpu.roll(x, SIDE, 1)


def chunk_at(device, devices):
    return device % 2 * (devices // 2) + device // 2


def four_blocks(value):
    rows = value.shape[0]
    v = value.reshape(rows // 8, 8, 4 * PAIR)
    low = lower_half((rows // 8, 8, PAIR))
    even, odd = [], []
    for g in (0, 2):
        first, second = v[:, :, g * PAIR : (g + 1) * PAIR], v[:, :, (g + 1) * PAIR : (g + 2) * PAIR]
        even.append(jnp.where(low, first, turn(second)))
        odd.append(jnp.where(low, turn(first), second))
    return [jnp.concatenate(half, axis=1).astype(BF) for half in (even, odd)]


def to_chunks(ref, value):
    half = value.shape[0] // 8
    for pos in range(0, value.shape[1] // PAIR, 4):
        even, odd = four_blocks(value[:, pos * PAIR : (pos + 4) * PAIR])
        ref[:half, pos * SIDE : (pos + 4) * SIDE, :] = even
        ref[half:, pos * SIDE : (pos + 4) * SIDE, :] = odd


def from_chunks(ref, block):
    half = ref.shape[0] // 2
    low = lower_half((half, 8, PAIR))
    at = block // 2 * 8
    tile = at // 16 * 16
    first, second = ref[:half, tile : tile + 16, :], ref[half:, tile : tile + 16, :]
    first = first.astype(F32)[:, at - tile : at - tile + 8]
    second = second.astype(F32)[:, at - tile : at - tile + 8]
    if block % 2 == 0:
        rows = jnp.where(low, first, turn(second))
    else:
        rows = jnp.where(low, turn(first), second)
    return rows.reshape(half * 8, PAIR).astype(BF)


def as_column(row):
    rows = row.shape[1]
    same = iota((rows, rows), 0) == iota((rows, rows), 1)
    return jnp.sum(jnp.where(same, row, 0), axis=1, keepdims=True)


def slot_of(owner_row):
    rows = owner_row.shape[1]
    i, j = iota((rows, rows), 0), iota((rows, rows), 1)
    owner_col = as_column(owner_row)
    same = owner_col == owner_row
    place_col = jnp.sum(jnp.where(same & (j < i), 1, 0), axis=1, keepdims=True)
    place_row = jnp.sum(jnp.where(same & (i < j), 1, 0), axis=0, keepdims=True)
    return owner_col, place_col, owner_row, place_row


def finish_kernel(*refs):
    n = len(refs) // 3
    sources, results, buffers, sems = refs[:n], refs[n : 2 * n], refs[2 * n : 3 * n], refs[3 * n]
    ins = [pltpu.make_async_copy(a, b, sems.at[0, i]) for i, (a, b) in enumerate(zip(sources, buffers))]
    outs = [pltpu.make_async_copy(a, b, sems.at[1, i]) for i, (a, b) in enumerate(zip(buffers, results))]
    for c in ins:
        c.start()
    for c, d in zip(ins, outs):
        c.wait()
        d.start()
    for d in outs:
        d.wait()


def place():
    hash_i, dp_i = lax.axis_index("hash"), lax.axis_index("dp")
    return {"y": hash_i // 2, "core": hash_i % 2, "x": dp_i // SIDE, "z": dp_i % SIDE}


def device_at(at):
    return (at["y"] * 2 + at["core"], at["x"] * SIDE + at["z"])


def partner(me, axis, jump):
    size = 2 if axis == "core" else SIDE
    at = dict(me)
    at[axis] = (me[axis] + jump) % size
    return at


def partners(me):
    return [partner(me, "core", 1)] + [partner(me, a, j) for a in "xyz" for j in (1, 2, 3)]


def facts_by_owner(owner_row, place_row, slot_row, length_row, devices, capacity):
    rows = owner_row.shape[1]
    slot, length = as_column(slot_row), as_column(length_row)
    lane = iota((rows, PAIR), 1)
    total = jnp.zeros((devices, PAIR), F32)
    for p in range(capacity):
        chosen = (iota((devices, rows), 0) == owner_row) & (place_row == p)
        value = jnp.where(lane == p, slot, jnp.where(lane == capacity + p, length, 0))
        total += dot_nn(jnp.where(chosen, 1.0, 0.0).astype(BF), value.astype(F32).astype(BF))
    return total


def received(facts, shape):
    devices, slots = facts.shape[0], shape[1]
    capacity = slots // devices
    lane, source = iota((devices, slots), 1), iota((devices, slots), 0)
    rows = []
    for first in (0, capacity):
        total = jnp.zeros((devices, slots), F32)
        for p in range(capacity):
            total = jnp.where(lane == source * capacity + p, facts[:, first + p : first + p + 1], total)
        rows.append(jnp.sum(total, axis=0, keepdims=True))
    return jnp.where(iota(shape, 0) == 0, rows[0], rows[1])


def forward_kernel(
    alone, capacity,
    owner_ref, slot_ref, length_ref, cand_ref, cot_ref, x_hbm, win_hbm, wout_hbm,
    facts_ref, recv_hbm, enc_hbm, sg_hbm, gate_hbm, vqk_hbm, nrm_hbm, inv_hbm, act_hbm, slope_hbm, xt_hbm,
    x_s, win_s, wout_s, load, send_s, enc_s, sg_s, gate_s, vqk_s, nrm_s, inv_s, act_s, slope_s, xt_s, save, mix_s, send, recv, own, tell_s, told_s, tell, told,
):
    hists, seq, width = x_s.shape
    rows = cand_ref.shape[0]
    loads = [
        pltpu.make_async_copy(a, b, load.at[i])
        for i, (a, b) in enumerate(((x_hbm, x_s), (win_hbm, win_s), (wout_hbm, wout_s)))
    ]
    for c in loads:
        c.start()
    devices = send_s.shape[0]
    if not alone:
        hash_i, dp_i = lax.axis_index("hash"), lax.axis_index("dp")
        ring = lax.axis_size("dp")
        me = hash_i * ring + dp_i
        barrier = pltpu.get_barrier_semaphore()

        def greet(jump, carry):
            to = lax.rem(me + jump, devices)
            pl.semaphore_signal(barrier, inc=1, device_id=(to // ring, to % ring), device_id_type=MESH)
            return carry

        lax.fori_loop(1, devices, greet, 0)
    _, _, owner_row, place_row = slot_of(owner_ref[...])
    slots = devices * capacity
    chosen = jnp.where(iota((slots, rows), 0) == owner_row * capacity + place_row, 1.0, 0.0).astype(BF)
    facts = facts_by_owner(owner_row, place_row, slot_ref[...], length_ref[...], devices, capacity)
    tell_s[...] = facts.reshape(devices, 1, PAIR)
    sent_rows = width // PAIR * SIDE
    for i, value in enumerate((cand_ref[...], cot_ref[...])):
        to_chunks(send_s.at[:, i * sent_rows : (i + 1) * sent_rows], dot_nn(chosen, value))
    if not alone:
        pl.semaphore_wait(barrier, devices - 1)

        def push(jump, carry):
            to = lax.rem(me + lax.rem(jump * 37, devices), devices)
            pltpu.make_async_remote_copy(
                src_ref=send_s.at[chunk_at(to, devices)], dst_ref=recv_hbm.at[chunk_at(me, devices)],
                send_sem=send, recv_sem=recv, device_id=(to // ring, to % ring), device_id_type=MESH,
            ).start()
            pltpu.make_async_remote_copy(
                src_ref=tell_s.at[to], dst_ref=told_s.at[me],
                send_sem=tell, recv_sem=told, device_id=(to // ring, to % ring), device_id_type=MESH,
            ).start()
            return carry

        lax.fori_loop(1, devices, push, 0)
        keep = pltpu.make_async_copy(send_s.at[chunk_at(me, devices)], recv_hbm.at[chunk_at(me, devices)], own)
        keep.start()
        told_s[me] = tell_s[me]
    for c in loads:
        c.wait()
    cut = seq // 2
    seen = iota((cut, seq), 0) <= iota((cut, seq), 1)
    half_scale = head_rows(0.5 * HEAD_DIM**-0.5)
    inv_seq = head_rows(1.0 / seq)
    outs = (
        (enc_s, enc_hbm), (sg_s, sg_hbm), (gate_s, gate_hbm), (vqk_s, vqk_hbm), (nrm_s, nrm_hbm), (inv_s, inv_hbm),
        (act_s, act_hbm), (slope_s, slope_hbm),
    )

    def saves(h):
        return [pltpu.make_async_copy(a.at[h], b.at[h], save.at[i, h]) for i, (a, b) in enumerate(outs)]

    def one(hist, carry):
        x = x_s[hist]
        xh = x * 0.5
        xt_s[:, pl.ds(pl.multiple_of(hist * seq, seq), seq)] = x.T
        for part in range(4):
            cols = slice(part * width, (part + 1) * width)
            act, grad2 = silu_parts(dot_nn(xh, win_s[:, cols]))
            sg_s[hist, :, cols] = (0.5 * grad2).astype(BF)
            if part == 0:
                gate_s[hist] = act.astype(BF)
            else:
                vqk_s[hist, :, (part - 1) * width : part * width] = act.astype(BF)
        for pair in range(width // PAIR):
            lanes = [slice(b * width + pair * PAIR, b * width + (pair + 1) * PAIR) for b in range(3)]
            v = vqk_s[hist, :, lanes[0]]
            q = vqk_s[hist, :, lanes[1]]
            k = vqk_s[hist, :, lanes[2]]
            total = None
            for h in range(2):
                qs, vs = q * half_scale[h], v * inv_seq[h]
                act, grad2 = silu_parts(dot_nt(k[:cut], qs))
                a0 = jnp.where(seen, act, 0.0).astype(BF)
                g0 = jnp.where(seen, grad2, 0.0).astype(BF)
                act, grad2 = silu_parts(dot_nt(k[cut:], qs[cut:]))
                a1 = jnp.where(seen[:, :cut], act, 0.0).astype(BF)
                g1 = jnp.where(seen[:, :cut], grad2, 0.0).astype(BF)
                act_s[hist, 2 * pair + h] = jnp.concatenate([a0, a1], axis=1)
                slope_s[hist, 2 * pair + h] = jnp.concatenate([g0, g1], axis=1)
                later = jnp.concatenate([a0[:, cut:], a1], axis=0)
                terms = (dot_tn(a0[:, :cut], vs[:cut]), dot_tn(later, vs))
                total = terms if total is None else [a + b for a, b in zip(total, terms)]
            mix_s[:cut, lanes[0]] = total[0]
            mix_s[cut:, lanes[0]] = total[1]
        mixed = mix_s[...]
        centred = mixed - jnp.mean(mixed, axis=1, keepdims=True)
        inv = lax.rsqrt(jnp.mean(centred * centred, axis=1, keepdims=True) + EPS)
        normed = centred * inv
        nrm_s[hist] = normed.astype(BF)
        inv_s[hist] = jnp.broadcast_to(inv, (seq, PAIR))
        merged = (normed * gate_s[hist].astype(F32)).astype(BF)
        enc_s[hist] = (x.astype(F32) + dot_nn(merged, wout_s[...])).astype(BF)
        for c in saves(hist):
            c.start()
        return carry

    lax.fori_loop(0, hists, one, 0)
    turned = pltpu.make_async_copy(xt_s, xt_hbm, load.at[0])
    turned.start()
    for h in range(hists):
        for c in saves(h):
            c.wait()
    turned.wait()
    if not alone:
        keep.wait()
        all_but_one = pl.ds(0, devices - 1)
        pltpu.make_async_remote_copy(
            src_ref=send_s.at[all_but_one], dst_ref=recv_hbm.at[all_but_one], send_sem=send, recv_sem=recv,
            device_id=(lax.rem(hash_i + 1, devices // ring), dp_i), device_id_type=MESH,
        ).wait()
        pltpu.make_async_remote_copy(
            src_ref=tell_s.at[all_but_one], dst_ref=told_s.at[all_but_one], send_sem=tell, recv_sem=told,
            device_id=(lax.rem(hash_i + 1, devices // ring), dp_i), device_id_type=MESH,
        ).wait()
        facts_ref[...] = received(told_s[...].reshape(devices, PAIR), facts_ref.shape)


def without(dims, axis):
    return "".join(d for d in dims if d not in ("lh" if axis == "z" else axis))


def shape_of(dims):
    return tuple(2 if d in "lh" else SIDE for d in dims)


def along(ref, dims, axis, at):
    index = {"x": at["x"], "y": at["y"], "l": at["z"] % 2, "h": at["z"] // 2}
    gone = "lh" if axis == "z" else axis
    return ref.at[tuple(index[d] if d in gone else slice(None) for d in dims)]


class Reduction:
    def __init__(self, parts, got0, pair, axis_got, axis_sum, landed, sums, sems, push_sems):
        self.me = place()
        self.parts, self.got0, self.pair = parts, got0, pair
        self.axis_got, self.axis_sum, self.landed, self.sums = axis_got, axis_sum, landed, sums
        self.send, self.recv = sems
        self.push_sem, self.land_sem = push_sems

    def device(self, jump):
        ring = lax.axis_size("dp")
        to = lax.rem(self.index() + jump, lax.axis_size(AXES))
        return (to // ring, to % ring), to

    def index(self):
        return lax.axis_index("hash") * lax.axis_size("dp") + lax.axis_index("dp")

    def greet(self):
        barrier = pltpu.get_barrier_semaphore()

        def one(jump, carry):
            pl.semaphore_signal(barrier, inc=1, device_id=self.device(jump)[0], device_id_type=MESH)
            return carry

        lax.fori_loop(1, lax.axis_size(AXES), one, 0)

    def enter(self):
        pl.semaphore_wait(pltpu.get_barrier_semaphore(), lax.axis_size(AXES) - 1)

    def give_back(self, grads, returned, sems, own):
        me = chunk_at(self.index(), lax.axis_size(AXES))

        def one(jump, carry):
            device_id, to = self.device(jump)
            pltpu.make_async_remote_copy(
                src_ref=grads.at[chunk_at(to, lax.axis_size(AXES))], dst_ref=returned.at[me], send_sem=sems.at[0], recv_sem=sems.at[1],
                device_id=device_id, device_id_type=MESH,
            ).start()
            return carry

        lax.fori_loop(1, lax.axis_size(AXES), one, 0)
        pltpu.make_async_copy(grads.at[me], returned.at[me], own).start()

    def take_back(self, grads, returned, sems, own):
        me = chunk_at(self.index(), lax.axis_size(AXES))
        others = pl.ds(0, lax.axis_size(AXES) - 1)
        pltpu.make_async_remote_copy(
            src_ref=grads.at[others], dst_ref=returned.at[others], send_sem=sems.at[0], recv_sem=sems.at[1],
            device_id=self.device(1)[0], device_id_type=MESH,
        ).wait()
        pltpu.make_async_copy(grads.at[me], returned.at[me], own).wait()

    def chip(self, jump):
        me = self.me
        q = lax.rem((me["y"] * SIDE + me["x"]) * SIDE + me["z"] + jump, SIDE**3)
        return {"y": q // SIDE**2, "x": q // SIDE % SIDE, "z": q % SIDE, "core": me["core"]}

    def copy(self, src, dst, number, other):
        return pltpu.make_async_remote_copy(
            src_ref=src, dst_ref=dst, send_sem=self.send.at[number], recv_sem=self.recv.at[number],
            device_id=device_at(other), device_id_type=MESH,
        )

    def copies(self, t, stage):
        if stage == 0:
            mate = partner(self.me, "core", 1)
            return [self.copy(self.parts.at[t, :, :, mate["core"]], self.got0.at[t], t, mate)]
        out = []
        for j in (1, 2, 3):
            other = partner(self.me, ORDERS[t][0], j)
            src = along(self.pair.at[t], DIMS, ORDERS[t][0], other)
            out.append(self.copy(src, self.axis_got[t].at[j - 1], GROUPS + 3 * t + j - 1, other))
        return out

    def start(self, t, stage):
        for c in self.copies(t, stage):
            c.start()

    def finish(self, t, stage):
        for c in self.copies(t, stage):
            c.wait_recv()
        if stage == 0:
            total = self.parts[t, :, :, self.me["core"]].astype(F32) + self.got0[t].astype(F32)
            self.pair[t] = total.astype(BF)
            return
        total = along(self.pair.at[t], DIMS, ORDERS[t][0], self.me)[...].astype(F32)
        for j in range(3):
            total = total + self.axis_got[t][j].astype(F32)
        self.axis_sum[t][...] = total.astype(BF)

    def advance(self, t, stage):
        self.finish(t, stage)
        if stage == 0 and t < len(ORDERS):
            self.start(t, 1)
        else:
            self.push(t)

    def others(self, t):
        return (SIDE**2 if t < len(ORDERS) else SIDE**3) - 1

    def member(self, t, jump):
        if t == len(ORDERS):
            return self.chip(jump)
        a, b = ORDERS[t][1:]
        q = lax.rem(self.me[a] * SIDE + self.me[b] + jump, SIDE**2)
        return {**self.me, a: q // SIDE, b: q % SIDE}

    def chunk(self, t, at):
        index = {"x": at["x"], "y": at["y"], "l": at["z"] % 2, "h": at["z"] // 2}
        if t == len(ORDERS):
            return self.pair.at[(t,) + tuple(index[d] for d in DIMS)]
        return self.axis_sum[t].at[tuple(index[d] for d in without(DIMS, ORDERS[t][0]))]

    def push(self, t):
        def one(jump, carry):
            to = self.member(t, jump)
            pltpu.make_async_remote_copy(
                src_ref=self.chunk(t, to), dst_ref=self.landed[t].at[jump - 1],
                send_sem=self.push_sem.at[t], recv_sem=self.land_sem.at[t],
                device_id=device_at(to), device_id_type=MESH,
            ).start()
            return carry

        lax.fori_loop(1, self.others(t) + 1, one, 0)

    def land(self, t):
        every = self.landed[t]
        pltpu.make_async_remote_copy(
            src_ref=every, dst_ref=every, send_sem=self.push_sem.at[t], recv_sem=self.land_sem.at[t],
            device_id=device_at(self.member(t, 1)), device_id_type=MESH,
        ).wait()
        own = self.chunk(t, self.me)[...].astype(F32)
        self.sums[t] = own + jnp.sum(every[...].astype(F32), axis=0)

    def end(self, win_ref, wout_ref):
        width = wout_ref.shape[1]
        for block in range(SIDE):
            rows = slice(block * SIDE, (block + 1) * SIDE)
            wout_ref[:, block * PAIR : (block + 1) * PAIR] = self.sums[0, rows]
            for pair in range(GROUPS - 1):
                at = (block + 1) % SIDE * width + pair * PAIR
                win_ref[:, at : at + PAIR] = self.sums[1 + pair, rows]
        for t in range(GROUPS):
            for stage in range(2 if t < len(ORDERS) else 1):
                for c in self.copies(t, stage):
                    c.wait_send()


class Nothing:
    def __getattr__(self, name):
        return lambda *args: None


def backward_kernel(
    alone,
    win_hbm, wout_hbm, sg_hbm, gate_hbm, vqk_hbm, nrm_hbm, inv_hbm, act_hbm, slope_hbm, xt_hbm, denc_hbm, grads_hbm, owner_ref,
    hg_ref, gin_ref, gout_ref, cand_ref,
    win_s, wout_s, sg_s, gate_s, vqk_s, nrm_s, inv_s, act_s, slope_s, xt_s, denc_s, load, load_pair, back, own, ret_s, slots_s,
    mg_s, dp_s, dm_s, parts_s, got0, pair_s, sums, send, recv, push, land, *bufs,
):
    hists, seq, width = hg_ref.shape
    gate_cols, other_cols = pl.ds(0, width), pl.ds(width, 3 * width)
    moves = (
        (denc_hbm, denc_s), (wout_hbm, wout_s), (nrm_hbm, nrm_s), (gate_hbm, gate_s), (inv_hbm, inv_s),
        (sg_hbm.at[:, :, gate_cols], sg_s.at[:, :, gate_cols]),
        (vqk_hbm, vqk_s), (sg_hbm.at[:, :, other_cols], sg_s.at[:, :, other_cols]), (xt_hbm, xt_s), (win_hbm, win_s),
    )
    loads = [pltpu.make_async_copy(a, b, load.at[i]) for i, (a, b) in enumerate(moves)]

    def pair_loads(pair):
        heads = pl.ds(2 * pair, 2)
        return [
            pltpu.make_async_copy(a.at[:, heads], b.at[:, heads], load_pair.at[i, pair])
            for i, (a, b) in enumerate(((act_hbm, act_s), (slope_hbm, slope_s)))
        ]

    for c in loads[:6]:
        c.start()
    n = len(ORDERS)
    comm = Nothing()
    if not alone:
        comm = Reduction(
            parts_s, got0, pair_s, bufs[:n], bufs[n : 2 * n], bufs[2 * n :], sums, (send, recv), (push, land)
        )
    comm.greet()

    def rows_of(h):
        return pl.ds(pl.multiple_of(h * seq, seq), seq)

    def store_part(t, value):
        for i, half in enumerate(four_blocks(value)):
            parts_s[t, i] = half.reshape(parts_s.shape[2:])

    for c in loads[:6]:
        c.wait()
    for c in loads[6:8] + pair_loads(0) + loads[8:9]:
        c.start()
    for pair in range(1, width // PAIR):
        for c in pair_loads(pair):
            c.start()
    loads[9].start()

    def gate_step(h, carry):
        rows = rows_of(h)
        normed = nrm_s[h].astype(F32)
        gate = gate_s[h].astype(F32)
        mg_s[rows, :] = (normed * gate).astype(BF)
        d_merged = dot_nt(denc_s[h], wout_s[...])
        dp_s[rows, :width] = (d_merged * normed * sg_s[h, :, :width].astype(F32)).astype(BF)
        d_norm = d_merged * gate
        m1 = jnp.mean(d_norm, axis=1, keepdims=True)
        m2 = jnp.mean(d_norm * normed, axis=1, keepdims=True)
        dm_s[rows, :] = (inv_s[h][:, :1] * (d_norm - m1 - normed * m2)).astype(BF)
        return carry

    lax.fori_loop(0, hists, gate_step, 0)
    comm.enter()
    store_part(0, dot_tn(mg_s[...], denc_s[...].reshape(hists * seq, width)))
    comm.start(0, 0)
    comm.give_back(grads_hbm, ret_s, back, own)
    for c in loads[6:9]:
        c.wait()

    cut = seq // 2
    half_scale = head_rows(0.5 * HEAD_DIM**-0.5)
    one = head_rows(1.0)
    scales = (1.0 / seq, 0.5 * HEAD_DIM**-0.5 / seq, 1.0 / seq)

    def attn_step(pair, carry):
        lanes = [pl.ds(pl.multiple_of(b * width + pair * PAIR, PAIR), PAIR) for b in range(4)]
        for c in pair_loads(pair):
            c.wait()
        for h in range(hists):
            v, q, k = (vqk_s[h, :, lanes[b]] for b in range(3))
            dm = dm_s[h * seq : (h + 1) * seq, lanes[0]]
            sums_ = [None] * 6
            for head in range(2):
                qs, dms, ks = q * half_scale[head], dm * one[head], k * one[head]
                a, g = act_s[h, 2 * pair + head], slope_s[h, 2 * pair + head].astype(F32)
                a0, a1 = a[:, :seq], a[:, seq:]
                s0 = (dot_nt(v[:cut], dms) * g[:, :seq]).astype(BF)
                s1 = (dot_nt(v[cut:], dms[cut:]) * g[:, seq:]).astype(BF)
                terms = (
                    dot_nn(a0, dms), dot_nn(a1, dms[cut:]),
                    dot_tn(s0[:, :cut], ks[:cut]), dot_tn(jnp.concatenate([s0[:, cut:], s1], axis=0), ks),
                    dot_nn(s0, qs), dot_nn(s1, qs[cut:]),
                )
                sums_ = [t if total is None else total + t for total, t in zip(sums_, terms)]
            for i, value in enumerate(sums_):
                b, part = 1 + i // 2, i % 2
                at = slice(h * seq + part * cut, h * seq + (part + 1) * cut)
                sg = sg_s[h, part * cut : (part + 1) * cut, lanes[b]].astype(F32) * scales[b - 1]
                dp_s[at, lanes[b]] = (value * sg).astype(BF)
        d_pair = jnp.concatenate([dp_s[:, lanes[b]] for b in (1, 2, 3, 0)], axis=1)
        store_part(1 + pair, dot_nn(xt_s[...], d_pair))
        for now, (started, paired, summed) in enumerate(PLAN):
            @pl.when(pair == now)
            def _():
                comm.start(started, 0)
                for t in paired:
                    comm.advance(t, 0)
                for t in summed:
                    comm.advance(t, 1)
        return carry

    lax.fori_loop(0, width // PAIR, attn_step, 0)
    loads[9].wait()

    def grads(lo, hi):
        for h in range(lo, hi):
            prod = dot_nt(dp_s[h * seq : (h + 1) * seq, :], win_s[...])
            hg_ref[h] = (denc_s[h].astype(F32) + prod).astype(BF)

    grads(0, hists // 2)
    comm.advance(4, 0)
    comm.advance(2, 1)
    grads(hists // 2, hists)
    comm.advance(3, 1)
    comm.take_back(grads_hbm, ret_s, back, own)
    for block in range(width // PAIR):
        slots_s[:, block * PAIR : (block + 1) * PAIR] = from_chunks(ret_s, block)
    owner_col, place_col, _, _ = slot_of(owner_ref[...])
    slots = slots_s.shape[0]
    target_col = owner_col * SIDE + place_col
    chosen = jnp.where(iota((cand_ref.shape[0], slots), 1) == target_col, 1.0, 0.0).astype(BF)
    cand_ref[...] = dot_nn(chosen, slots_s[...]).astype(BF)
    for t in range(GROUPS):
        comm.land(t)
    comm.end(gin_ref, gout_ref)


def sort_slots(facts_ref, hists):
    hist_row, len_row = facts_ref[0:1], facts_ref[1:2]
    slots = hist_row.shape[1]
    picked = jnp.where((iota((8, slots), 0).astype(F32) == hist_row) & (len_row > 0.0), 1.0, 0.0)
    before = jnp.where(iota((slots, slots), 0) < iota((slots, slots), 1), 1.0, 0.0).astype(BF)
    rank = dot_nn(picked.astype(BF), before)
    place_row = jnp.full((1, slots), -1.0, F32)
    first, runs = jnp.int32(0), []
    for own in range(hists):
        tiles = (jnp.sum(picked[own : own + 1]).astype(jnp.int32) + (TILE - 1)) // TILE
        here = rank[own : own + 1] + (first * TILE).astype(F32)
        place_row = jnp.where(picked[own : own + 1] > 0.0, here, place_row)
        runs.append((first, first + tiles))
        first = first + tiles
    return place_row, runs


def target_kernel(
    facts_ref, recv_ref, enc_hbm, dq_ref, denc_hbm, rows_s, sorted_s, len_s, de_s, dq_s, enc_ref, denc_s, load, save
):
    hists, seq, width = enc_ref.shape
    fetch = pltpu.make_async_copy(enc_hbm, enc_ref, load)
    fetch.start()
    saves = [pltpu.make_async_copy(denc_s.at[h], denc_hbm.at[h], save.at[h]) for h in range(hists)]
    slots = rows_s.shape[0]
    room = sorted_s.shape[0]
    blocks = width // PAIR
    for block in range(2 * blocks):
        rows_s[:, block * PAIR : (block + 1) * PAIR] = from_chunks(recv_ref, block)
    place_row, runs = sort_slots(facts_ref, hists)
    chosen = jnp.where(iota((room, slots), 0).astype(F32) == place_row, 1.0, 0.0).astype(BF)
    for half in range(2):
        cols = slice(half * width, (half + 1) * width)
        sorted_s[:, cols] = dot_nn(chosen, rows_s[:, cols]).astype(BF)
    len_s[...] = dot_nt(facts_ref[...].astype(BF), chosen)
    de_s[...] = jnp.zeros(de_s.shape, F32)
    dq_s[...] = jnp.zeros(dq_s.shape, BF)
    scale = 0.5 * HEAD_DIM**-0.5
    half_scale = head_rows(scale)
    one = head_rows(1.0)
    positions = iota((seq, TILE), 0).astype(F32)
    low = iota((TILE, PAIR), 1) < HEAD_DIM
    fetch.wait()
    for own in range(hists):

        def body(tile, carry):
            at = pl.ds(pl.multiple_of(tile * TILE, TILE), TILE)
            length = len_s[1:2, at]
            weight = jnp.where(positions < length, 1.0 / jnp.maximum(length, 1.0), 0.0)
            weight = jnp.concatenate([weight, weight], axis=1)
            for pair in range(blocks):
                cols = slice(pair * PAIR, (pair + 1) * PAIR)
                enc = enc_ref[own, :, cols]
                q, g = sorted_s[at, cols], sorted_s[at, width + pair * PAIR : width + (pair + 1) * PAIR]
                qq = jnp.concatenate([q * half_scale[0], q * half_scale[1]], axis=0)
                gg = jnp.concatenate([g * one[0], g * one[1]], axis=0)
                act, grad2 = silu_parts(dot_nt(enc, qq))
                a = (act * weight).astype(BF)
                d_s = (dot_nt(enc, gg) * grad2 * weight).astype(BF)
                de_s[own, :, cols] += dot_nn(a, gg) + dot_nn(d_s, qq)
                both = dot_tn(d_s, enc)
                dq_s[at, cols] = (jnp.where(low, both[:TILE], both[TILE:]) * scale).astype(BF)
            return carry

        lax.fori_loop(runs[own][0], runs[own][1], body, 0)
        denc_s[own] = de_s[own].astype(BF)
        saves[own].start()
    place_col = jnp.transpose(jnp.broadcast_to(place_row, (8, slots)))[:, 0:1]
    back = jnp.where(iota((slots, room), 1).astype(F32) == place_col, 1.0, 0.0).astype(BF)
    to_chunks(dq_ref, dot_nn(back, dq_s[...]))
    for c in saves:
        c.wait()


def forward(histories, weight_in, weight_out, routing, candidates, cotangent, devices, capacity, alone=False):
    hists, seq, width = histories.shape
    chunk = (devices, 2 * width // PAIR * SIDE, PAIR)
    widths = [(width, BF), (4 * width, BF), (width, BF), (3 * width, BF), (width, BF), (PAIR, F32)]
    kept = [((hists, seq, w), t) for w, t in widths]
    kept += [((hists, HEADS, seq // 2, seq // 2 * 3), BF)] * 2 + [((width, hists * seq), BF)]
    scratch = [pltpu.VMEM(o.shape, o.dtype) for o in (histories, weight_in, weight_out)]
    scratch += [pltpu.SemaphoreType.DMA((3,)), pltpu.VMEM(chunk, BF)]
    scratch += [pltpu.VMEM(*k) for k in kept]
    scratch += [pltpu.SemaphoreType.DMA((len(kept) - 1, hists)), pltpu.VMEM((seq, width), F32)]
    scratch += [pltpu.SemaphoreType.DMA] * 3
    scratch += [pltpu.VMEM((devices, 1, PAIR), F32)] * 2 + [pltpu.SemaphoreType.DMA] * 2
    vmem = pl.BlockSpec(memory_space=pltpu.VMEM)
    hbm = pl.BlockSpec(memory_space=pl.ANY)
    return pl.pallas_call(
        functools.partial(forward_kernel, alone, capacity),
        in_specs=[vmem] * 5 + [hbm] * 3,
        out_specs=[vmem] + [hbm] * (1 + len(kept)),
        out_shape=[jax.ShapeDtypeStruct((8, devices * capacity), F32), jax.ShapeDtypeStruct(chunk, BF)] + [jax.ShapeDtypeStruct(*k) for k in kept],
        scratch_shapes=scratch,
        compiler_params=pltpu.CompilerParams(vmem_limit_bytes=VMEM_LIMIT, **({} if alone else {"collective_id": 1, "has_side_effects": True})),
        cost_estimate=pl.CostEstimate(flops=8_000_000_000, bytes_accessed=12_000_000, transcendentals=4_000_000),
        name="route_and_forward",
    )(*routing, candidates, cotangent, histories, weight_in, weight_out)


def backward(histories, weight_in, weight_out, saved, d_enc, d_query, owner_row, alone=False):
    hists, seq, width = histories.shape
    total = hists * seq
    operands = (weight_in, weight_out, *saved, d_enc)
    tile = (SIDE * SIDE, PAIR)
    scratch = [pltpu.VMEM(o.shape, o.dtype) for o in operands]
    operands += (d_query, owner_row)
    scratch += [
        pltpu.SemaphoreType.DMA((10,)),
        pltpu.SemaphoreType.DMA((2, width // PAIR)),
        pltpu.SemaphoreType.DMA((2,)),
        pltpu.SemaphoreType.DMA,
        pltpu.VMEM(d_query.shape, BF),
        pltpu.VMEM((d_query.shape[0] * SIDE, width), BF),
        pltpu.VMEM((total, width), BF),
        pltpu.VMEM((total, 4 * width), BF),
        pltpu.VMEM((total, width), BF),
        pltpu.VMEM((GROUPS, 2, SIDE, 2, SIDE, 2) + tile, BF),
        pltpu.VMEM((GROUPS,) + shape_of(DIMS) + tile, BF),
        pltpu.VMEM((GROUPS,) + shape_of(DIMS) + tile, BF),
        pltpu.VMEM((GROUPS,) + tile, F32),
        pltpu.SemaphoreType.DMA((GROUPS + 3 * len(ORDERS),)),
        pltpu.SemaphoreType.DMA((GROUPS + 3 * len(ORDERS),)),
        pltpu.SemaphoreType.DMA((GROUPS,)),
        pltpu.SemaphoreType.DMA((GROUPS,)),
    ]
    rest = [shape_of(without(DIMS, order[0])) for order in ORDERS]
    scratch += [pltpu.VMEM((SIDE - 1,) + dims + tile, BF) for dims in rest]
    scratch += [pltpu.VMEM(dims + tile, BF) for dims in rest]
    scratch += [pltpu.VMEM((SIDE**2 - 1,) + tile, BF)] * len(ORDERS) + [pltpu.VMEM((SIDE**3 - 1,) + tile, BF)]
    more = {} if alone else {"collective_id": 0, "has_side_effects": True}
    return pl.pallas_call(
        functools.partial(backward_kernel, alone),
        in_specs=[pl.BlockSpec(memory_space=pl.ANY)] * (len(operands) - 1) + [pl.BlockSpec(memory_space=pltpu.VMEM)],
        out_specs=[pl.BlockSpec(memory_space=pltpu.VMEM)] * 4,
        out_shape=[
            jax.ShapeDtypeStruct((hists, seq, width), BF),
            jax.ShapeDtypeStruct((SIDE, 4 * width), F32),
            jax.ShapeDtypeStruct((SIDE, width), F32),
            jax.ShapeDtypeStruct((owner_row.shape[1], width), BF),
        ],
        scratch_shapes=scratch,
        compiler_params=pltpu.CompilerParams(vmem_limit_bytes=VMEM_LIMIT, **more),
        cost_estimate=pl.CostEstimate(flops=16_000_000_000, bytes_accessed=18_000_000, transcendentals=2_000_000),
        name="layer_backward",
    )(*operands)


def target(facts, recv, encoded, slots):
    hists, seq, width = encoded.shape
    room = (slots // TILE + hists - 1) * TILE
    vmem = pl.BlockSpec(memory_space=pltpu.VMEM)
    return pl.pallas_call(
        target_kernel,
        in_specs=[vmem, vmem, pl.BlockSpec(memory_space=pl.ANY)],
        out_specs=[vmem, pl.BlockSpec(memory_space=pl.ANY)],
        out_shape=[
            jax.ShapeDtypeStruct((slots // SIDE, SIDE * SIDE, PAIR), BF),
            jax.ShapeDtypeStruct((hists, seq, width), BF),
        ],
        scratch_shapes=[
            pltpu.VMEM((slots, 2 * width), BF),
            pltpu.VMEM((room, 2 * width), BF),
            pltpu.VMEM((8, room), F32),
            pltpu.VMEM((hists, seq, width), F32),
            pltpu.VMEM((room, width), BF),
            pltpu.VMEM((hists, seq, width), BF),
            pltpu.VMEM((hists, seq, width), BF),
            pltpu.SemaphoreType.DMA,
            pltpu.SemaphoreType.DMA((hists,)),
        ],
        compiler_params=pltpu.CompilerParams(vmem_limit_bytes=VMEM_LIMIT),
        cost_estimate=pl.CostEstimate(flops=8_000_000_000, bytes_accessed=4_000_000, transcendentals=4_000_000),
        name="target_backward",
    )(facts, recv, encoded)


def finish(*results):
    hbm = pl.BlockSpec(memory_space=pl.ANY)
    return pl.pallas_call(
        finish_kernel,
        in_specs=[hbm] * len(results),
        out_specs=[hbm] * len(results),
        out_shape=[jax.ShapeDtypeStruct(r.shape, r.dtype) for r in results],
        scratch_shapes=[pltpu.VMEM(r.shape, r.dtype) for r in results]
        + [pltpu.SemaphoreType.DMA((2, len(results)))],
        compiler_params=pltpu.CompilerParams(vmem_limit_bytes=VMEM_LIMIT),
        name="finish",
    )(*results)


def local(histories, weight_in, weight_out, candidates, cotangent, owner_ids, hist_slot, lengths):
    devices = lax.axis_size(AXES)
    imp_rows, width = candidates.shape
    capacity = max(2, 2 * imp_rows // devices)
    slots = devices * capacity
    routing = [r.reshape(1, imp_rows) for r in (owner_ids, hist_slot, lengths)]
    facts, recv, encoded, *saved = forward(
        histories, weight_in, weight_out, routing, candidates, cotangent, devices, capacity
    )
    d_query, d_encoded = target(facts, recv, encoded, slots)
    history_grad, in_grad, out_grad, candidate_grad = backward(
        histories, weight_in, weight_out, saved, d_encoded, d_query, routing[0]
    )
    return finish(history_grad, candidate_grad, in_grad, out_grad)


def solution(mesh):
    return jax.shard_map(
        local,
        mesh=mesh,
        in_specs=(
            P(AXES, None, None),
            P(),
            P(),
            P(AXES, None),
            P(AXES, None),
            P(AXES, None),
            P(AXES),
            P(AXES),
        ),
        out_specs=(P(AXES, None, None), P(AXES, None), P(AXES, None), P(AXES, None)),
        check_vma=False,
    )
```
